32 devices in a mesh: dp: 8 (over z, y), fsdp: 4 (over x, core).
Axes of the slice: x: 2, y: 2, z: 4, core: 2. Of those that a mesh axis runs over, the one named last changes fastest.
Arguments:
- tokens: bfloat16 [32768, 768], P(('dp', 'fsdp')), may hold values from -6 to 6
- doc_ids: int32 [32768], P(('dp', 'fsdp')), may hold values from 0 to 4, as said below
- d_out: bfloat16 [32768, 768], P(('dp', 'fsdp')), may hold values from -6 to 6
- ln1_gain: bfloat16 [768], P(('dp', 'fsdp')), may hold values from 0.5 to 1.5
- ln1_shift: bfloat16 [768], P(('dp', 'fsdp')), may hold values from -1.5 to 1.5
- qkv_weight: bfloat16 [768, 2304], P(('dp', 'fsdp')), may hold values from -0.21875 to 0.21875
- qv_bias: bfloat16 [1536], P(('dp', 'fsdp')), may hold values from -1.5 to 1.5
- out_weight: bfloat16 [768, 768], P(('dp', 'fsdp')), may hold values from -0.625 to 0.625
- out_bias: bfloat16 [768], P(('dp', 'fsdp')), may hold values from -1.5 to 1.5
- ln2_gain: bfloat16 [768], P(('dp', 'fsdp')), may hold values from 0.5 to 1.5
- ln2_shift: bfloat16 [768], P(('dp', 'fsdp')), may hold values from -1.5 to 1.5
- fc_weight: bfloat16 [768, 3072], P(('dp', 'fsdp')), may hold values from -0.21875 to 0.21875
- fc_bias: bfloat16 [3072], P(('dp', 'fsdp')), may hold values from -1.5 to 1.5
- proj_weight: bfloat16 [3072, 768], P(('dp', 'fsdp')), may hold values from -0.109375 to 0.109375
- proj_bias: bfloat16 [768], P(('dp', 'fsdp')), may hold values from -1.5 to 1.5
Outputs:
- block_out: bfloat16 [32768, 768], P(('dp', 'fsdp'))
- input_grad: float32 [32768, 768], P(('dp', 'fsdp'))
- ln1_gain_grad: float32 [768], P(('dp', 'fsdp'))
- ln1_shift_grad: float32 [768], P(('dp', 'fsdp'))
- qkv_weight_grad: float32 [768, 2304], P(('dp', 'fsdp'))
- qv_bias_grad: float32 [1536], P(('dp', 'fsdp'))
- out_weight_grad: float32 [768, 768], P(('dp', 'fsdp'))
- out_bias_grad: float32 [768], P(('dp', 'fsdp'))
- ln2_gain_grad: float32 [768], P(('dp', 'fsdp'))
- ln2_shift_grad: float32 [768], P(('dp', 'fsdp'))
- fc_weight_grad: float32 [768, 3072], P(('dp', 'fsdp'))
- fc_bias_grad: float32 [3072], P(('dp', 'fsdp'))
- proj_weight_grad: float32 [3072, 768], P(('dp', 'fsdp'))
- proj_bias_grad: float32 [768], P(('dp', 'fsdp'))
The draws below stay inside these ranges and needn't reach their ends.
Inputs may be any that keep to these rules, and one draw needn't show every extreme that they name: `doc_ids`: within each packed row of 1024 tokens (rows start at multiples of 1024) the ids start at 1, rise by one at each new document, never fall until the row's padding, and the row ends with one or more padding tokens of id 0; no document crosses a row's end; a row holds at most 4 documents, and some row holds exactly 4.
All inputs are finite; a program needn't handle non-finite values.
Results may differ from the reference program's by a relative error of at most 0.0088.
Values may be sent and summed in bfloat16 or wider, within the bound.
No kernel may reach another device: no remote copies, remote signals or barrier semaphores. Data moves between devices by JAX's collectives and lax.ppermute only.
A program may use at most 192 MiB of HBM per device.

```python
import math
import jax
import jax.numpy as jnp
from jax import lax

D = 768
H = 12
HD = 64
FF = 3072
LEN = 1024
TOKENS = 32768
QB = 512


def draw_doc_ids(key, part):
    key = jax.random.fold_in(key, 7)
    count_key, row_key, cut_key, pad_key = jax.random.split(key, 4)
    nrows = TOKENS // LEN
    most = max(LEN // 256, 2)
    segment = (LEN - max(LEN // 8, 2)) // most
    counts = jax.random.randint(count_key, (nrows, 1), 1, most + 1)
    chosen = jax.random.randint(row_key, (), 0, nrows)
    row_index = jnp.arange(nrows)[:, None]
    counts = jnp.where(row_index == chosen, most, counts)
    order = jnp.arange(1, most)[None, :]
    offsets = jax.random.randint(cut_key, (nrows, most - 1), 0, segment)
    cuts = jnp.where(order < counts, order * segment + offsets, 2 * LEN)
    position = jnp.arange(LEN)[None, :]
    numbers = 1 + jnp.sum((cuts[:, None, :] <= position[:, :, None]).astype(jnp.int32), -1)
    padding = jax.random.randint(pad_key, (nrows, 1), 1, max(LEN // 8, 2))
    numbers = jnp.where(position >= LEN - padding, 0, numbers)
    return numbers.reshape(TOKENS).astype(jnp.int32)


def level_of(own_key, dims, cuts, smallest, high):
    level = 1.0
    for dim, parts in cuts:
        steps = jax.random.uniform(jax.random.fold_in(jax.random.fold_in(own_key, 6), dim), (parts,), jnp.float32, smallest / len(cuts), high / len(cuts))
        level = level * jnp.repeat(jnp.exp(steps), dims[dim] // parts).reshape((-1,) + (1,) * (len(dims) - 1 - dim))
    return level


def bell_draw(rng, extent, scale, bound, cuts=(), dtype=jnp.bfloat16):
    loudness = level_of(rng, extent, cuts, -0.22, 0.18) if cuts else 1.0
    drawn = jax.random.normal(rng, extent, jnp.float32) * scale * loudness
    return jnp.minimum(jnp.maximum(drawn, -bound), bound).astype(dtype)


def setup_inputs(seed: int = 0) -> dict:
    seeds = jax.random.split(jax.random.key(seed), 16)
    return {
        "tokens": bell_draw(seeds[0], (TOKENS, D), 1.0, 6.0, ((0, 32),)),
        "doc_ids": draw_doc_ids(jax.random.fold_in(seeds[15], 71), 0),
        "d_out": bell_draw(seeds[2], (TOKENS, D), 1.0, 6.0, ((0, 32),)),
        "ln1_gain": jnp.clip(1.0 + 0.1 * jax.random.normal(seeds[3], (D,), jnp.float32), 0.5, 1.5).astype(jnp.bfloat16),
        "ln1_shift": bell_draw(seeds[4], (D,), 0.3, 1.5, ((0, 32),)),
        "qkv_weight": bell_draw(seeds[5], (D, 3 * D), D ** -0.5, 0.21875, ((0, 32),)),
        "qv_bias": bell_draw(seeds[6], (2 * D,), 0.3, 1.5, ((0, 32),)),
        "out_weight": bell_draw(seeds[7], (D, D), (D // 8) ** -0.5, 0.625, ((0, 32),)),
        "out_bias": bell_draw(seeds[8], (D,), 0.3, 1.5, ((0, 32),)),
        "ln2_gain": jnp.clip(1.0 + 0.1 * jax.random.normal(seeds[9], (D,), jnp.float32), 0.5, 1.5).astype(jnp.bfloat16),
        "ln2_shift": bell_draw(seeds[10], (D,), 0.3, 1.5, ((0, 32),)),
        "fc_weight": bell_draw(seeds[11], (D, FF), D ** -0.5, 0.21875, ((0, 32),)),
        "fc_bias": bell_draw(seeds[12], (FF,), 0.3, 1.5, ((0, 32),)),
        "proj_weight": bell_draw(seeds[13], (FF, D), FF ** -0.5, 0.109375, ((0, 32),)),
        "proj_bias": bell_draw(seeds[14], (D,), 0.3, 1.5, ((0, 32),)),
    }


EPS = 1e-05
NEG = -1e+30
HIGH = lax.Precision.HIGHEST

@jax.custom_vjp
def low(v):
    return lax.optimization_barrier(v.astype(jnp.bfloat16)).astype(jnp.float32)

@jax.custom_vjp
def low_back(v):
    return v

def low_keep(v):
    return (low(v), None)

def low_pass(kept, grad):
    return (grad,)

def back_keep(v):
    return (v, None)

def back_low(kept, grad):
    return (low(grad),)
low.defvjp(low_keep, low_pass)
low_back.defvjp(back_keep, back_low)

def normalize(v, gain, shift):
    center = v - lax.optimization_barrier(jnp.mean(v, -1, keepdims=True))
    spread = lax.optimization_barrier(jnp.mean(center * center, -1, keepdims=True))
    return center * lax.rsqrt(spread + EPS) * gain + shift

def matmul(left, right):
    return jnp.dot(left, right, precision=HIGH)

def forward(params, x, docs):
    g1, b1, w_qkv, b_qv, w_out, b_out, g2, b2, w_fc, b_fc, w_proj, b_proj = params
    scale = 1.0 / math.sqrt(HD)
    h1 = low(normalize(x, g1, b1))
    mixed = matmul(h1, w_qkv)
    query = low_back(low(mixed[:, :D] + b_qv[:D])).reshape(LEN, H, HD)
    keys = low_back(low(mixed[:, D:2 * D])).reshape(LEN, H, HD)
    values = low_back(low(mixed[:, 2 * D:] + b_qv[D:])).reshape(LEN, H, HD)
    nblocks = LEN // QB
    qblocks = query.reshape(nblocks, QB, H, HD)
    starts = (jnp.arange(nblocks) * QB).astype(jnp.int32)
    kpos = jnp.arange(LEN).astype(jnp.int32)

    def block_fn(item):
        qblk, first = item
        qpos = first + jnp.arange(QB).astype(jnp.int32)
        qdoc = lax.dynamic_slice_in_dim(docs, first, QB)
        allow = (kpos[None, :] <= qpos[:, None]) & (qdoc[:, None] == docs[None, :]) & (docs[None, :] > 0)
        allow = allow | (kpos[None, :] == qpos[:, None])
        score = jnp.einsum('qhd,khd->hqk', qblk, keys, precision=HIGH)
        score = low_back(score * scale)
        score = jnp.where(allow[None], score, NEG)
        top = lax.optimization_barrier(jnp.max(score, -1, keepdims=True))
        expo = jnp.exp(score - top)
        prob = low(expo / lax.optimization_barrier(jnp.sum(expo, -1, keepdims=True)))
        return jnp.einsum('hqk,khd->qhd', prob, values, precision=HIGH)
    attended = lax.map(jax.checkpoint(block_fn), (qblocks, starts)).reshape(LEN, D)
    attended = low_back(low(attended))
    r1 = x + low_back(matmul(attended, w_out) + b_out)
    h2 = low(normalize(r1, g2, b2))
    hidden = low_back(matmul(h2, w_fc) + b_fc)
    act = low(jax.nn.gelu(hidden, approximate=True))
    return r1 + low_back(matmul(act, w_proj) + b_proj)

def reference(tokens, doc_ids, d_out, ln1_gain, ln1_shift, qkv_weight, qv_bias, out_weight, out_bias, ln2_gain, ln2_shift, fc_weight, fc_bias, proj_weight, proj_bias):
    params = tuple((p.astype(jnp.float32) for p in (ln1_gain, ln1_shift, qkv_weight, qv_bias, out_weight, out_bias, ln2_gain, ln2_shift, fc_weight, fc_bias, proj_weight, proj_bias)))
    nseq = TOKENS // LEN
    xs = tokens.astype(jnp.float32).reshape(nseq, LEN, D)
    cots = d_out.astype(jnp.float32).reshape(nseq, LEN, D)
    docs_all = doc_ids.reshape(nseq, LEN)

    def step(total, item):
        xrow, docrow, cotrow = item
        result, pull = jax.vjp(lambda p, v: forward(p, v, docrow), params, xrow)
        pgrad, xgrad = pull(cotrow)
        total = jax.tree.map(lambda a, b: a + b, total, pgrad)
        return (total, (result.astype(jnp.bfloat16), xgrad))
    zeros = tuple((jnp.zeros_like(p) for p in params))
    total, (outs, xgrads) = lax.scan(step, zeros, (xs, docs_all, cots))
    return (outs.reshape(TOKENS, D), xgrads.reshape(TOKENS, D)) + tuple(total)
```

```python
import functools
import math

import jax
import jax.numpy as jnp
from jax import lax
from jax.experimental import pallas as pl
from jax.experimental.pallas import tpu as pltpu
from jax.sharding import PartitionSpec as P

HD = 64
LEN = 1024
PAIR = 2 * HD
EPS = 1e-05
NEG = -1e30
AXES = ("dp", "fsdp")

F32 = jnp.float32
BF16 = jnp.bfloat16
NN = (((1,), (0,)), ((), ()))
NT = (((1,), (1,)), ((), ()))
TN = (((0,), (0,)), ((), ()))
ANY = pl.BlockSpec(memory_space=pl.ANY)
SMEM = pl.BlockSpec(memory_space=pltpu.SMEM)
VMEM_LIMIT = 56 << 20

CORE, X, Y, Z0, Z1 = 1, 2, 4, 8, 16
CX, CY, CZ0, CZ1 = 1, 2, 4, 8
GROUPS = (
    (0, CZ0, CY, CY | CZ0),
    (CX, CX | CZ0, CX | CY, CX | CY | CZ0),
    (CZ1, CZ1 | CZ0, CZ1 | CX, CZ1 | CX | CZ0),
    (CZ1 | CY, CZ1 | CY | CZ0, CZ1 | CY | CX, CZ1 | CY | CX | CZ0),
)


def dot(a, b, dims):
    return lax.dot_general(a, b, dims, preferred_element_type=F32)


def params(**more):
    return pltpu.CompilerParams(vmem_limit_bytes=VMEM_LIMIT, **more)


def cost(flops, size):
    return pl.CostEstimate(flops=int(flops), bytes_accessed=int(size), transcendentals=0)


def whole(shape):
    return pl.BlockSpec(shape, lambda *g: (0,) * len(shape))


def rows(block, width):
    return pl.BlockSpec((block, width), lambda i: (i, 0))


def swap(array, bit):
    count = lax.axis_size("dp") * lax.axis_size("fsdp")
    return lax.ppermute(array, AXES, [(i, i ^ bit) for i in range(count)])


def halves(array, core):
    width = array.shape[1] // 2
    low, high = array[:, :width], array[:, width:]
    first = core == 0
    return jnp.where(first, low, high), jnp.where(first, high, low)


def pair_block(array, core):
    keep, send = halves(array, core)
    other = swap(send, CORE)
    first = core == 0
    return jnp.concatenate([jnp.where(first, keep, other), jnp.where(first, other, keep)], 0)


def gather_blocks(block):
    near = swap(block, Z0)
    first = jnp.stack([block, near])
    second = swap(first, Z1)
    by_y = swap(first, Y)
    by_x = swap(second, X)
    a_two = jnp.concatenate([first, by_y], 0)
    b_two = jnp.concatenate([second, by_x], 0)
    a_three = swap(a_two, X)
    b_three = swap(b_two, Y)
    own = (a_two, a_three, b_two, b_three)
    return own + tuple(swap(piece, CORE) for piece in own)


def scatter_sum(mine, other):
    got = swap(other, CORE)

    def total(a, b):
        return (a.astype(F32) + b.astype(F32)).astype(BF16)

    a_keep = total(mine[0], got[0])
    a_send = total(mine[1], got[1])
    b_keep = total(mine[2], got[2])
    b_send = total(mine[3], got[3])
    by_x = swap(a_send, X)
    by_y = swap(b_send, Y)
    a_keep = (a_keep, by_x)
    b_keep = (b_keep, by_y)
    a_low = total(a_keep[0][:2], a_keep[1][:2])
    a_high = total(a_keep[0][2:], a_keep[1][2:])
    b_low = total(b_keep[0][:2], b_keep[1][:2])
    b_high = total(b_keep[0][2:], b_keep[1][2:])
    a_got = swap(a_high, Y)
    b_got = swap(b_high, X)
    b_sum = total(b_low, b_got)
    far = swap(b_sum, Z1)
    near = a_low.astype(F32) + a_got.astype(F32) + far.astype(F32)
    last = swap(near[1].astype(BF16), Z0)
    return near[0] + last.astype(F32)


def own_rows(block, core):
    count = block.shape[0] // 2
    low, high = block[:count], block[count:]
    first = core == 0
    keep = jnp.where(first, low, high)
    got = swap(jnp.where(first, high, low), CORE)
    return jnp.where(first, keep, got), jnp.where(first, got, keep)


def gather_all(array):
    return lax.all_gather(array, AXES, axis=0, tiled=True)


def scatter_all(array):
    return lax.psum_scatter(array, AXES, scatter_dimension=0, tiled=True)


def gather_small(vector, index):
    table = vector.reshape(1, -1)
    for bit in (CORE, X, Y, Z0, Z1):
        other = swap(table, bit)
        low = (index & bit) == 0
        table = jnp.concatenate([jnp.where(low, table, other), jnp.where(low, other, table)], 0)
    return table


def scatter_small(table, index):
    for bit in (Z1, Z0, Y, X, CORE):
        count = table.shape[0] // 2
        low = (index & bit) == 0
        keep = jnp.where(low, table[:count], table[count:])
        send = jnp.where(low, table[count:], table[:count])
        table = keep + swap(send, bit)
    return table.reshape(-1)


def fetch(place, pieces, which, lane, width, into, sem, groups=1):
    if len(pieces) < 8:
        pltpu.make_async_copy(pieces[which], into, sem).start()
        return lambda: pltpu.make_async_copy(into, into, sem).wait()
    chip, core = place[0], place[1]
    step = 48
    for side in range(2):
        half = core if side == 0 else 1 - core
        column = pl.ds(pl.multiple_of(half * width, 128), width)
        for group in range(4):
            for spot, relative in enumerate(GROUPS[group]):
                owner = lax.bitwise_xor(chip, relative)
                for part in range(groups):
                    start = pl.multiple_of((owner * groups + part) * step, step)
                    pltpu.make_async_copy(
                        pieces[4 * side + group].at[spot, :, pl.ds(lane + part * width, width)],
                        into.at[pl.ds(start, step), column],
                        sem,
                    ).start()
    return lambda: pltpu.make_async_copy(into, into, sem).wait()


def normal(v):
    center = v - jnp.mean(v, -1, keepdims=True)
    spread = jnp.mean(center * center, -1, keepdims=True)
    factor = lax.rsqrt(spread + EPS)
    return center * factor, factor


def project_kernel(place, x, gain, shift, q_bias, v_bias, *rest):
    pieces, (mixed, hidden, weight, sem) = rest[:-4], rest[-4:]
    width = x.shape[1]

    @pl.when(pl.program_id(0) == 0)
    def _():
        fetch(place, pieces, 0, 0, 3 * width // 2, weight, sem)()

    unit, _ = normal(x[...].astype(F32))
    h = (unit * gain[...] + shift[...]).astype(BF16)
    hidden[...] = h
    scale = 1.0 / math.sqrt(HD)
    q = dot(h, weight[:, :width], NN) + q_bias[...]
    mixed[:, :width] = (q.astype(BF16).astype(F32) * scale).astype(BF16)
    mixed[:, width : 2 * width] = dot(h, weight[:, width : 2 * width], NN).astype(BF16)
    mixed[:, 2 * width :] = (dot(h, weight[:, 2 * width :], NN) + v_bias[...]).astype(BF16)


def project(place, x, gain, shift, q_bias, v_bias, pieces):
    count, width = x.shape
    block = 256
    return pl.pallas_call(
        project_kernel,
        grid=(count // block,),
        in_specs=[SMEM, rows(block, width)] + [whole((1, width))] * 4 + [ANY] * len(pieces),
        out_specs=[rows(block, 3 * width), rows(block, width)],
        out_shape=[
            jax.ShapeDtypeStruct((count, 3 * width), BF16),
            jax.ShapeDtypeStruct((count, width), BF16),
        ],
        scratch_shapes=[pltpu.VMEM((width, 3 * width), BF16), pltpu.SemaphoreType.DMA],
        compiler_params=params(),
        cost_estimate=cost(6 * count * width * width, 12e6),
        name="project",
    )(place, x, gain, shift, q_bias, v_bias, *pieces)


def allowed(q_doc, k_doc, first, shape, q_dim):
    q_pos = lax.broadcasted_iota(jnp.int32, shape, q_dim) + first
    k_pos = lax.broadcasted_iota(jnp.int32, shape, 1 - q_dim)
    allow = ((k_pos <= q_pos) & (q_doc == k_doc) & (k_doc > 0)) | (k_pos == q_pos)
    return jnp.where(allow, 0.0, NEG)


def attend_kernel(block, q_docs, k_docs, q_all, k_all, v_all, out, lse, bias):
    count = LEN // block

    @pl.when(pl.program_id(0) == 0)
    def _():
        for i in range(count):
            sl, reach = slice(i * block, (i + 1) * block), (i + 1) * block
            bias[sl, :reach] = allowed(q_docs[sl, :], k_docs[:, :reach], i * block, (block, reach), 0)

    low = lax.broadcasted_iota(jnp.int32, (block, PAIR), 1) < HD
    for i in range(count):
        sl, reach = slice(i * block, (i + 1) * block), (i + 1) * block
        q = q_all[sl, :]
        outs, logs = [], []
        for head in range(2):
            q_one = jnp.where(low if head == 0 else ~low, q, jnp.zeros_like(q))
            score = dot(q_one, k_all[:reach, :], NT) + bias[sl, :reach]
            top = jnp.max(score, -1, keepdims=True)
            expo = jnp.exp(score - top)
            total = jnp.sum(expo, -1, keepdims=True)
            outs.append(dot(expo.astype(BF16), v_all[:reach, :], NN) / total)
            logs.append(top + jnp.log(total))
        out[sl, :] = jnp.where(low, outs[0], outs[1]).astype(BF16)
        turned = jnp.where(low, logs[0], logs[1]).T
        lse[0, 0:1, sl] = turned[0:1, :]
        lse[0, 1:2, sl] = turned[HD : HD + 1, :]


def attend(mixed, docs):
    width = mixed.shape[1] // 3
    pairs = width // PAIR
    block = 512
    column = lambda base: pl.BlockSpec((LEN, PAIR), lambda g: (0, base + g))
    return pl.pallas_call(
        functools.partial(attend_kernel, block),
        grid=(pairs,),
        in_specs=[whole((LEN, 1)), whole((1, LEN)), column(0), column(pairs), column(2 * pairs)],
        out_specs=[column(0), pl.BlockSpec((1, 2, LEN), lambda g: (g, 0, 0))],
        out_shape=[
            jax.ShapeDtypeStruct((LEN, width), BF16),
            jax.ShapeDtypeStruct((pairs, 2, LEN), F32),
        ],
        scratch_shapes=[pltpu.VMEM((LEN, LEN), F32)],
        compiler_params=params(),
        cost_estimate=cost(24e9, 8e6),
        name="attend",
    )(docs.reshape(LEN, 1), docs.reshape(1, LEN), mixed, mixed, mixed)


def attend_back_kernel(block, q_docs, k_docs, q_all, k_all, v_all, o_all, g_all, lse, dq, dk, dv, bias, k_sum, v_sum):
    count = LEN // block

    @pl.when(pl.program_id(0) == 0)
    def _():
        for i in range(count):
            sl, reach = slice(i * block, (i + 1) * block), (i + 1) * block
            bias[:reach, sl] = allowed(q_docs[:, sl], k_docs[:reach, :], i * block, (reach, block), 1)

    low = lax.broadcasted_iota(jnp.int32, (block, PAIR), 1) < HD
    low_all = lax.broadcasted_iota(jnp.int32, (LEN, PAIR), 1) < HD
    keys = k_all[...]
    key_one = [jnp.where(low_all, keys, jnp.zeros_like(keys)), jnp.where(low_all, jnp.zeros_like(keys), keys)]
    for i in reversed(range(count)):
        sl, reach = slice(i * block, (i + 1) * block), (i + 1) * block
        q, grad = q_all[sl, :], g_all[sl, :]
        turned = (grad.astype(F32) * o_all[sl, :].astype(F32)).T
        parts = []
        for head in range(2):
            lane = low if head == 0 else ~low
            q_one = jnp.where(lane, q, jnp.zeros_like(q))
            g_one = jnp.where(lane, grad, jnp.zeros_like(grad))
            inner = jnp.sum(turned[head * HD : (head + 1) * HD, :], 0, keepdims=True)
            score = dot(k_all[:reach, :], q_one, NT) + bias[:reach, sl]
            prob = jnp.exp(score - lse[0, head : head + 1, sl])
            v_part = dot(prob.astype(BF16), g_one, NN)
            slope = dot(v_all[:reach, :], g_one, NT)
            dscore = (prob * (slope - inner)).astype(BF16)
            k_part = dot(dscore, q_one, NN)
            if i == count - 1 and head == 0:
                k_sum[...] = k_part
                v_sum[...] = v_part
            else:
                k_sum[:reach, :] += k_part
                v_sum[:reach, :] += v_part
            parts.append(dot(dscore, key_one[head][:reach], TN))
        dq[sl, :] = ((parts[0] + parts[1]) * (1.0 / math.sqrt(HD))).astype(BF16)
    dk[...] = k_sum[...].astype(BF16)
    dv[...] = v_sum[...].astype(BF16)


def attend_back(mixed, attended, grad_o, lse, docs, first, number):
    width = attended.shape[1]
    pairs = width // PAIR
    block = 256
    column = lambda base: pl.BlockSpec((LEN, PAIR), lambda g: (0, base + g))
    return pl.pallas_call(
        functools.partial(attend_back_kernel, block),
        grid=(number,),
        in_specs=[
            whole((1, LEN)),
            whole((LEN, 1)),
            column(first),
            column(pairs + first),
            column(2 * pairs + first),
            column(first),
            column(first),
            pl.BlockSpec((1, 2, LEN), lambda g: (first + g, 0, 0)),
        ],
        out_specs=[column(0)] * 3,
        out_shape=[jax.ShapeDtypeStruct((LEN, PAIR * number), BF16)] * 3,
        scratch_shapes=[
            pltpu.VMEM((LEN, LEN), F32),
            pltpu.VMEM((LEN, PAIR), F32),
            pltpu.VMEM((LEN, PAIR), F32),
        ],
        compiler_params=params(),
        cost_estimate=cost(36e9 * number / pairs, 10e6),
        name="attend_back",
    )(docs.reshape(1, LEN), docs.reshape(LEN, 1), mixed, mixed, mixed, attended, grad_o, lse)


def widen_kernel(place, x, attended, out_bias, gain, shift, fc_bias, *rest):
    pieces, (resid, hidden, active, slope, w_out, w_fc, sems) = rest[:-7], rest[-7:]
    width = x.shape[1]
    depth = w_fc.shape[1]

    @pl.when(pl.program_id(0) == 0)
    def _():
        wait_out = fetch(place, pieces, 0, 0, width // 2, w_out, sems.at[0])
        wait_fc = fetch(place, pieces, 1, width // 2, depth // 2, w_fc, sems.at[1])
        wait_out()
        wait_fc()

    r = x[...].astype(F32) + dot(attended[...], w_out[...], NN) + out_bias[...]
    resid[...] = r
    unit, _ = normal(r)
    h = (unit * gain[...] + shift[...]).astype(BF16)
    hidden[...] = h
    c = math.sqrt(2.0 / math.pi)
    for first in range(0, depth, width):
        sl = slice(first, first + width)
        u = dot(h, w_fc[:, sl], NN) + fc_bias[:, sl]
        square = u * u
        t = jnp.tanh(u * (c + (c * 0.044715) * square))
        half = 0.5 * (1.0 + t)
        active[:, sl] = (u * half).astype(BF16)
        slope[:, sl] = (half + 0.5 * u * (1.0 - t * t) * (c + (3 * c * 0.044715) * square)).astype(BF16)


def widen(place, x, attended, out_bias, gain, shift, fc_bias, pieces):
    count, width = x.shape
    depth = fc_bias.shape[1]
    block = 256
    return pl.pallas_call(
        widen_kernel,
        grid=(count // block,),
        in_specs=[SMEM, rows(block, width), rows(block, width)]
        + [whole((1, width))] * 3
        + [whole((1, depth))]
        + [ANY] * len(pieces),
        out_specs=[rows(block, width), rows(block, width), rows(block, depth), rows(block, depth)],
        out_shape=[
            jax.ShapeDtypeStruct((count, width), F32),
            jax.ShapeDtypeStruct((count, width), BF16),
            jax.ShapeDtypeStruct((count, depth), BF16),
            jax.ShapeDtypeStruct((count, depth), BF16),
        ],
        scratch_shapes=[
            pltpu.VMEM((width, width), BF16),
            pltpu.VMEM((width, depth), BF16),
            pltpu.SemaphoreType.DMA((2,)),
        ],
        compiler_params=params(),
        cost_estimate=cost(2 * count * width * (width + depth), 25e6),
        name="widen",
    )(place, x, attended, out_bias, gain, shift, fc_bias, *pieces)


def narrow_kernel(lane, place, resid, active, slope, cot, proj_bias, *rest):
    pieces, (result, grad_u, fc_sum, proj_sum, w_proj, sem) = rest[:-6], rest[-6:]
    width = resid.shape[1]
    depth = active.shape[1]

    @pl.when(pl.program_id(0) == 0)
    def _():
        fetch(place, pieces, 2, lane, width // 2, w_proj, sem, depth // width)()
        fc_sum[...] = jnp.zeros_like(fc_sum)
        proj_sum[...] = jnp.zeros_like(proj_sum)

    result[...] = (resid[...] + dot(active[...], w_proj[...], NN) + proj_bias[...]).astype(BF16)
    g = cot[...]
    proj_sum[...] += jnp.sum(g.astype(F32), 0, keepdims=True)
    for first in range(0, depth, width):
        sl = slice(first, first + width)
        du = (dot(g, w_proj[sl, :], NT) * slope[:, sl].astype(F32)).astype(BF16)
        grad_u[:, sl] = du
        fc_sum[:, sl] += jnp.sum(du.astype(F32), 0, keepdims=True)


def narrow(place, resid, active, slope, cot, proj_bias, pieces):
    count, width = resid.shape
    depth = active.shape[1]
    block = 256
    return pl.pallas_call(
        functools.partial(narrow_kernel, (width + depth) // 2),
        grid=(count // block,),
        in_specs=[SMEM, rows(block, width), rows(block, depth), rows(block, depth), rows(block, width)]
        + [whole((1, width))]
        + [ANY] * len(pieces),
        out_specs=[rows(block, width), rows(block, depth), whole((1, depth)), whole((1, width))],
        out_shape=[
            jax.ShapeDtypeStruct((count, width), BF16),
            jax.ShapeDtypeStruct((count, depth), BF16),
            jax.ShapeDtypeStruct((1, depth), F32),
            jax.ShapeDtypeStruct((1, width), F32),
        ],
        scratch_shapes=[pltpu.VMEM((depth, width), BF16), pltpu.SemaphoreType.DMA],
        compiler_params=params(),
        cost_estimate=cost(4 * count * width * depth, 30e6),
        name="narrow",
    )(place, resid, active, slope, cot, proj_bias, *pieces)


def norm_back(v, gain, grad):
    unit, factor = normal(v)
    g = grad * gain
    pulled = factor * (g - jnp.mean(g, -1, keepdims=True) - unit * jnp.mean(g * unit, -1, keepdims=True))
    return pulled, jnp.sum(grad * unit, 0, keepdims=True), jnp.sum(grad, 0, keepdims=True)


def middle_kernel(place, resid, grad_u, cot, gain, *rest):
    pieces, rest = rest[:-9], rest[-9:]
    grad_r, grad_t, grad_o, gain_sum, shift_sum, bias_sum, w_out, w_fc, sems = rest
    width = resid.shape[1]
    depth = grad_u.shape[1]

    @pl.when(pl.program_id(0) == 0)
    def _():
        wait_fc = fetch(place, pieces, 1, width // 2, depth // 2, w_fc, sems.at[0])
        wait_out = fetch(place, pieces, 0, 0, width // 2, w_out, sems.at[1])
        gain_sum[...] = jnp.zeros_like(gain_sum)
        shift_sum[...] = jnp.zeros_like(shift_sum)
        bias_sum[...] = jnp.zeros_like(bias_sum)
        wait_fc()
        wait_out()

    grad_h = dot(grad_u[...], w_fc[...], NT)
    pulled, gains, shifts = norm_back(resid[...], gain[...], grad_h)
    total = cot[...].astype(F32) + pulled
    grad_r[...] = total
    low = total.astype(BF16)
    grad_t[...] = low
    gain_sum[...] += gains
    shift_sum[...] += shifts
    bias_sum[...] += jnp.sum(low.astype(F32), 0, keepdims=True)
    grad_o[...] = dot(low, w_out[...], NT).astype(BF16)


def middle(place, resid, grad_u, cot, gain, pieces):
    count, width = resid.shape
    depth = grad_u.shape[1]
    block = 256
    return pl.pallas_call(
        middle_kernel,
        grid=(count // block,),
        in_specs=[SMEM, rows(block, width), rows(block, depth), rows(block, width), whole((1, width))]
        + [ANY] * len(pieces),
        out_specs=[rows(block, width)] * 3 + [whole((1, width))] * 3,
        out_shape=[
            jax.ShapeDtypeStruct((count, width), F32),
            jax.ShapeDtypeStruct((count, width), BF16),
            jax.ShapeDtypeStruct((count, width), BF16),
        ]
        + [jax.ShapeDtypeStruct((1, width), F32)] * 3,
        scratch_shapes=[
            pltpu.VMEM((width, width), BF16),
            pltpu.VMEM((width, depth), BF16),
            pltpu.SemaphoreType.DMA((2,)),
        ],
        compiler_params=params(),
        cost_estimate=cost(2 * count * width * (width + depth), 25e6),
        name="middle",
    )(place, resid, grad_u, cot, gain, *pieces)


def first_back_kernel(place, x, grad_r, gain, dq, dk, dv, *rest):
    pieces, (grad_x, gain_sum, shift_sum, weight, sem) = rest[:-5], rest[-5:]
    width = x.shape[1]

    @pl.when(pl.program_id(0) == 0)
    def _():
        fetch(place, pieces, 0, 0, 3 * width // 2, weight, sem)()
        gain_sum[...] = jnp.zeros_like(gain_sum)
        shift_sum[...] = jnp.zeros_like(shift_sum)

    grad_h = (
        dot(dq[...], weight[:, :width], NT)
        + dot(dk[...], weight[:, width : 2 * width], NT)
        + dot(dv[...], weight[:, 2 * width :], NT)
    )
    pulled, gains, shifts = norm_back(x[...].astype(F32), gain[...], grad_h)
    grad_x[...] = grad_r[...] + pulled
    gain_sum[...] += gains
    shift_sum[...] += shifts


def first_back(place, x, grad_r, gain, dq, dk, dv, pieces):
    count, width = x.shape
    block = 256
    return pl.pallas_call(
        first_back_kernel,
        grid=(count // block,),
        in_specs=[SMEM, rows(block, width), rows(block, width), whole((1, width))]
        + [rows(block, width)] * 3
        + [ANY] * len(pieces),
        out_specs=[rows(block, width)] + [whole((1, width))] * 2,
        out_shape=[jax.ShapeDtypeStruct((count, width), F32)] + [jax.ShapeDtypeStruct((1, width), F32)] * 2,
        scratch_shapes=[pltpu.VMEM((width, 3 * width), BF16), pltpu.SemaphoreType.DMA],
        compiler_params=params(),
        cost_estimate=cost(6 * count * width * width, 16e6),
        name="first_back",
    )(place, x, grad_r, gain, dq, dk, dv, *pieces)


def weight_grad_kernel(number, steps, step_rows, place, left, *rest):
    rights, mine, other, stage, sems = rest[:number], rest[number], rest[number + 1], rest[number + 2], rest[number + 3]
    tile = stage.shape[3]
    step = pl.program_id(0)
    slot = lax.rem(step, 2)
    chip, core = place[0], place[1]
    per_half = steps // 2

    def send(at, start):
        which = lax.rem(at, 2)
        own = (at // per_half) == core
        for index in range(number):
            lane = pl.multiple_of((index * per_half + lax.rem(at, per_half)) * tile, 128)
            for group in range(4):
                for spot, relative in enumerate(GROUPS[group]):
                    owner = lax.bitwise_xor(chip, relative)
                    source = stage.at[which, index, pl.ds(pl.multiple_of(owner * step_rows, 16), step_rows), :]
                    for flag, target in ((own, mine), (jnp.logical_not(own), other)):
                        copy = pltpu.make_async_copy(
                            source, target.at[group, spot, :, pl.ds(lane, tile)], sems.at[which]
                        )
                        if start:
                            pl.when(flag)(copy.start)

    def finish(which):
        pltpu.make_async_copy(stage.at[which], stage.at[which], sems.at[which]).wait()

    @pl.when(step >= 2)
    def _():
        finish(slot)

    for index in range(number):
        stage[slot, index] = dot(left[...], rights[index][...], TN).astype(BF16)
    send(step, True)

    @pl.when(step == steps - 1)
    def _():
        finish(slot)
        if steps > 1:
            finish(1 - slot)


def weight_grad(place, left, rights, tile, name):
    count, tall = left.shape
    wide = rights[0].shape[1]
    number = len(rights)
    steps = wide // tile
    step_rows = tall // 16
    shape = (4, 4, step_rows, number * wide // 2)
    return pl.pallas_call(
        functools.partial(weight_grad_kernel, number, steps, step_rows),
        grid=(steps,),
        in_specs=[SMEM, whole((count, tall))] + [pl.BlockSpec((count, tile), lambda i: (0, i))] * number,
        out_specs=[ANY, ANY],
        out_shape=[jax.ShapeDtypeStruct(shape, BF16)] * 2,
        scratch_shapes=[pltpu.VMEM((2, number, tall, tile), BF16), pltpu.SemaphoreType.DMA((2,))],
        compiler_params=params(),
        cost_estimate=cost(2 * count * tall * wide * number, 2 * (count * tall + wide * number * (count + tall))),
        name=name,
    )(place, left, *rights)


def whole_grad(place, left, rights, tile, name):
    return jnp.concatenate([dot(left, right, TN) for right in rights], 1)


def unpack(table):
    count = table.shape[1] // 12
    spans = (1, 1, 2, 1, 1, 1, 4, 1)
    found, at = [], 0
    for span in spans:
        found.append(table[:, at : at + span * count].reshape(1, -1).astype(F32))
        at += span * count
    return found


def pack(vectors, devices):
    return jnp.concatenate([v.reshape(devices, -1) for v in vectors], 1)


def staged(
    tokens,
    doc_ids,
    d_out,
    ln1_gain,
    ln1_shift,
    qkv_weight,
    qv_bias,
    out_weight,
    out_bias,
    ln2_gain,
    ln2_shift,
    fc_weight,
    fc_bias,
    proj_weight,
    proj_bias,
):
    width = tokens.shape[1]
    depth = fc_weight.shape[1]
    index = lax.axis_index("dp") * lax.axis_size("fsdp") + lax.axis_index("fsdp")
    core = index & 1
    place = jnp.stack([index >> 1, core]).astype(jnp.int32)
    devices = lax.axis_size("dp") * lax.axis_size("fsdp")

    smalls = jnp.concatenate([ln1_gain, ln1_shift, qv_bias, out_bias, ln2_gain, ln2_shift, fc_bias, proj_bias])
    by_stage = (lax.axis_size("dp"), lax.axis_size("fsdp")) == (8, 4)
    if by_stage:
        first_pieces = gather_blocks(pair_block(qkv_weight, core))
        table = gather_small(smalls, index)
        proj_block = pair_block(proj_weight, core)
        proj_parts = [proj_block[48 * j : 48 * (j + 1)] for j in range(depth // width)]
        rest_block = jnp.concatenate([pair_block(out_weight, core), pair_block(fc_weight, core)] + proj_parts, 1)
        rest_pieces = gather_blocks(rest_block)
    else:
        first_pieces, rest_pieces = [gather_all(qkv_weight)], [gather_all(w) for w in (out_weight, fc_weight, proj_weight)]
        table = gather_all(smalls.reshape(1, -1))
    g1, b1, qv_row, out_row, g2, b2, fc_row, proj_row = unpack(table)

    mixed, h_one = project(place, tokens, g1, b1, qv_row[:, :width], qv_row[:, width:], first_pieces)
    attended, lse = attend(mixed, doc_ids)
    resid, h_two, active, slope = widen(place, tokens, attended, out_row, g2, b2, fc_row, rest_pieces)
    grad_of = weight_grad if by_stage else whole_grad
    proj_terms = grad_of(place, active, [d_out], 384, "proj_grad")
    result, grad_u, fc_sum, proj_sum = narrow(place, resid, active, slope, d_out, proj_row, rest_pieces)
    fc_terms = grad_of(place, h_two, [grad_u], 384, "fc_grad")
    grad_r, grad_t, grad_o, gain_two, shift_two, out_sum = middle(place, resid, grad_u, d_out, g2, rest_pieces)
    out_terms = grad_of(place, attended, [grad_t], 384, "out_grad")
    pairs = width // PAIR
    parts = [
        attend_back(mixed, attended, grad_o, lse, doc_ids, first, pairs // 2) for first in (0, pairs // 2)
    ]
    dq, dk, dv = (jnp.concatenate(p, 1) for p in zip(*parts))
    qkv_terms = grad_of(place, h_one, [dq, dk, dv], 384, "qkv_grad")
    grad_x, gain_one, shift_one = first_back(place, tokens, grad_r, g1, dq, dk, dv, first_pieces)

    if by_stage:
        proj_grad = jnp.concatenate(own_rows(scatter_sum(*proj_terms), core), 1)
        fc_grad = jnp.concatenate(own_rows(scatter_sum(*fc_terms), core), 1)
        out_grad = jnp.concatenate(own_rows(scatter_sum(*out_terms), core), 1)
        sides = own_rows(scatter_sum(*qkv_terms), core)
        part = width // 2
        qkv_grad = jnp.concatenate([side[:, part * j : part * (j + 1)] for j in range(3) for side in sides], 1)
    else:
        proj_grad, fc_grad, out_grad, qkv_grad = (
            scatter_all(term) for term in (proj_terms, fc_terms, out_terms, qkv_terms)
        )
    q_sum = jnp.sum(dq.astype(F32), 0)
    v_sum = jnp.sum(dv.astype(F32), 0)
    sums = pack(
        [gain_one, shift_one, jnp.concatenate([q_sum, v_sum]), out_sum, gain_two, shift_two, fc_sum, proj_sum],
        devices,
    )
    own = scatter_small(sums, index) if by_stage else scatter_all(sums).reshape(-1)
    n = width // devices
    spots = (0, n, 2 * n, 4 * n, 5 * n, 6 * n, 7 * n, 11 * n, 12 * n)
    s = [own[a:b] for a, b in zip(spots[:-1], spots[1:])]
    return (
        result,
        grad_x,
        s[0],
        s[1],
        qkv_grad,
        s[2],
        out_grad,
        s[3],
        s[4],
        s[5],
        fc_grad,
        s[6],
        proj_grad,
        s[7],
    )


def solution(mesh):
    every, block = P(AXES), P(AXES, None)
    ins = (block, every, block, every, every, block, every, block, every, every, every, block, every, block, every)
    outs = (block, block, every, every, block, every, block, every, every, every, block, every, block, every)
    return jax.shard_map(staged, mesh=mesh, in_specs=ins, out_specs=outs, check_vma=False)
```

```python
import functools
import math

import jax
import jax.numpy as jnp
from jax import lax
from jax.experimental import pallas as pl
from jax.experimental.pallas import tpu as pltpu
from jax.sharding import PartitionSpec as P

HD = 64
LEN = 1024
PAIR = 2 * HD
EPS = 1e-05
NEG = -1e30
AXES = ("dp", "fsdp")

F32 = jnp.float32
BF16 = jnp.bfloat16
NN = (((1,), (0,)), ((), ()))
NT = (((1,), (1,)), ((), ()))
TN = (((0,), (0,)), ((), ()))
ANY = pl.BlockSpec(memory_space=pl.ANY)
SMEM = pl.BlockSpec(memory_space=pltpu.SMEM)
VMEM_LIMIT = 56 << 20
SHARE = 1.0

CORE, X, Y, Z0, Z1 = 1, 2, 4, 8, 16
CX, CY, CZ0, CZ1 = 1, 2, 4, 8
GROUPS = tuple(tuple(near | far for far in (0, CZ0, CZ1, CZ0 | CZ1)) for near in (0, CX, CY, CX | CY))


def dot(a, b, dims):
    return lax.dot_general(a, b, dims, preferred_element_type=F32)


def params(**more):
    return pltpu.CompilerParams(vmem_limit_bytes=VMEM_LIMIT, **more)


def cost(flops, size):
    return pl.CostEstimate(flops=int(flops * SHARE), bytes_accessed=int(size * SHARE), transcendentals=0)


def whole(shape):
    return pl.BlockSpec(shape, lambda *g: (0,) * len(shape))


def rows(block, width):
    return pl.BlockSpec((block, width), lambda i: (i, 0))


def swap(array, bit):
    count = lax.axis_size("dp") * lax.axis_size("fsdp")
    return lax.ppermute(array, AXES, [(i, i ^ bit) for i in range(count)])


def halves(array, core):
    width = array.shape[1] // 2
    low, high = array[:, :width], array[:, width:]
    first = core == 0
    return jnp.where(first, low, high), jnp.where(first, high, low)


def pair_block(array, core):
    keep, send = halves(array, core)
    other = swap(send, CORE)
    first = core == 0
    return jnp.concatenate([jnp.where(first, keep, other), jnp.where(first, other, keep)], 0)


def gather_z(block, *after):
    got = tie([swap(block, bits) for bits in (Z0, Z1, Z0 | Z1)], *after)
    return jnp.stack([block] + got)


def gather_xy(column):
    return [column] + [swap(column, bits) for bits in (X, Y, X | Y)]


def gather_core(own):
    return [*own, *(swap(piece, CORE) for piece in own)]


def add(*terms):
    return functools.reduce(lambda a, b: a + b, [t.astype(F32) for t in terms])


def scatter_core(terms):
    mine, other = terms
    got = swap(other, CORE)
    return [add(mine[g], got[g]).astype(BF16) for g in range(4)]


def scatter_xy(sums, *after):
    got = tie([swap(part, bits) for part, bits in zip(sums[1:], (X, Y, X | Y))], *after)
    return [add(*(part[spot] for part in [sums[0]] + got)).astype(BF16) for spot in range(4)]


def scatter_z(sums, *after):
    got = tie([swap(part, bits) for part, bits in zip(sums[1:], (Z0, Z1, Z0 | Z1))], *after)
    return add(sums[0], *got)


def tie(arrays, *others):
    if not others:
        return list(arrays)
    return list(lax.optimization_barrier((*arrays, *others))[: len(arrays)])


def kernel_call(kernel, inputs, after, **how):
    count, extra = len(inputs), len(after)

    def body(*refs):
        kernel(*refs[:count], *refs[count + extra :])

    how["in_specs"] = how["in_specs"] + [ANY] * extra
    return pl.pallas_call(body, **how)(*inputs, *after)


def own_rows(block, core):
    count = block.shape[0] // 2
    low, high = block[:count], block[count:]
    first = core == 0
    keep = jnp.where(first, low, high)
    got = swap(jnp.where(first, high, low), CORE)
    return jnp.where(first, keep, got), jnp.where(first, got, keep)


def gather_all(array):
    return lax.all_gather(array, AXES, axis=0, tiled=True)


def scatter_all(array):
    return lax.psum_scatter(array, AXES, scatter_dimension=0, tiled=True)


def gather_small(vector, index):
    table = vector.reshape(1, -1)
    for bit in (CORE, X, Y, Z0, Z1):
        other = swap(table, bit)
        low = (index & bit) == 0
        table = jnp.concatenate([jnp.where(low, table, other), jnp.where(low, other, table)], 0)
    return table


def scatter_small(table, index):
    for bit in (Z1, Z0, Y, X, CORE):
        count = table.shape[0] // 2
        low = (index & bit) == 0
        keep = jnp.where(low, table[:count], table[count:])
        send = jnp.where(low, table[count:], table[:count])
        table = keep + swap(send, bit)
    return table.reshape(-1)


def fetch(place, pieces, which, lane, width, into, sem):
    if len(pieces) < 8:
        pltpu.make_async_copy(pieces[which], into, sem).start()
        return lambda: pltpu.make_async_copy(into, into, sem).wait()
    chip, core = place[0], place[1]
    step = into.shape[0] // 16
    for side in range(2):
        half = core if side == 0 else 1 - core
        column = pl.ds(pl.multiple_of(half * width, 128), width)
        for group in range(4):
            for spot, relative in enumerate(GROUPS[group]):
                owner = lax.bitwise_xor(chip, relative)
                pltpu.make_async_copy(
                    pieces[4 * side + group].at[spot, :, pl.ds(lane, width)],
                    into.at[pl.ds(pl.multiple_of(owner * step, step), step), column],
                    sem,
                ).start()
    return lambda: pltpu.make_async_copy(into, into, sem).wait()


def normal(v):
    center = v - jnp.mean(v, -1, keepdims=True)
    spread = jnp.mean(center * center, -1, keepdims=True)
    factor = lax.rsqrt(spread + EPS)
    return center * factor, factor


def allowed(q_doc, k_doc, first, shape, q_dim):
    q_pos = lax.broadcasted_iota(jnp.int32, shape, q_dim) + first
    k_pos = lax.broadcasted_iota(jnp.int32, shape, 1 - q_dim)
    allow = ((k_pos <= q_pos) & (q_doc == k_doc) & (k_doc > 0)) | (k_pos == q_pos)
    return jnp.where(allow, 0.0, NEG)


def project_attend_kernel(steps, block, place, x, gain, shift, q_bias, v_bias, q_docs, k_docs, *rest):
    pieces, rest = rest[:-8], rest[-8:]
    mixed, hidden, out, lse, kept, bias, weight, sem = rest
    width = x.shape[1]
    size = x.shape[0]
    step = pl.program_id(0)

    @pl.when(step == 0)
    def _():
        wait = fetch(place, pieces, 0, 0, 3 * width // 2, weight, sem)
        for i in range(LEN // block):
            sl, reach = slice(i * block, (i + 1) * block), (i + 1) * block
            bias[sl, :reach] = allowed(q_docs[sl, :], k_docs[:, :reach], i * block, (block, reach), 0)
        wait()

    @pl.when(step < steps)
    def _():
        unit, _ = normal(x[...].astype(F32))
        h = (unit * gain[...] + shift[...]).astype(BF16)
        hidden[...] = h
        scale = 1.0 / math.sqrt(HD)
        here = pl.ds(pl.multiple_of(step * size, size), size)
        for part in range(3):
            sl = slice(part * width, (part + 1) * width)
            value = dot(h, weight[:, sl], NN)
            if part == 0:
                value = (value + q_bias[...]).astype(BF16).astype(F32) * scale
            if part == 2:
                value = value + v_bias[...]
            value = value.astype(BF16)
            mixed[:, sl] = value
            kept[here, sl] = value

    @pl.when(step >= steps)
    def _():
        lane = (step - steps) * PAIR
        q_at, k_at, v_at = (pl.ds(pl.multiple_of(lane + part * width, PAIR), PAIR) for part in range(3))
        low = lax.broadcasted_iota(jnp.int32, (block, PAIR), 1) < HD
        for i in range(LEN // block):
            sl, reach = slice(i * block, (i + 1) * block), (i + 1) * block
            q = kept[sl, q_at]
            outs, logs = [], []
            for head in range(2):
                q_one = jnp.where(low if head == 0 else ~low, q, jnp.zeros_like(q))
                score = dot(q_one, kept[:reach, k_at], NT) + bias[sl, :reach]
                top = jnp.max(score, -1, keepdims=True)
                expo = jnp.exp(score - top)
                total = jnp.sum(expo, -1, keepdims=True)
                outs.append(dot(expo.astype(BF16), kept[:reach, v_at], NN) / total)
                logs.append(top + jnp.log(total))
            out[sl, :] = jnp.where(low, outs[0], outs[1]).astype(BF16)
            turned = jnp.where(low, logs[0], logs[1]).T
            lse[0, 0:1, sl] = turned[0:1, :]
            lse[0, 1:2, sl] = turned[HD : HD + 1, :]


def project_attend(place, x, gain, shift, q_bias, v_bias, docs, pieces, after=()):
    count, width = x.shape
    size, block = 256, 512
    steps = count // size
    pairs = width // PAIR
    early = lambda i: (jnp.minimum(i, steps - 1), 0)
    late = lambda i: jnp.maximum(i - steps, 0)
    return kernel_call(
        functools.partial(project_attend_kernel, steps, block),
        [place, x, gain, shift, q_bias, v_bias, docs.reshape(LEN, 1), docs.reshape(1, LEN), *pieces],
        after,
        grid=(steps + pairs,),
        in_specs=[SMEM, pl.BlockSpec((size, width), early)]
        + [whole((1, width))] * 4
        + [whole((LEN, 1)), whole((1, LEN))]
        + [ANY] * len(pieces),
        out_specs=[
            pl.BlockSpec((size, 3 * width), early),
            pl.BlockSpec((size, width), early),
            pl.BlockSpec((LEN, PAIR), lambda i: (0, late(i))),
            pl.BlockSpec((1, 2, LEN), lambda i: (late(i), 0, 0)),
        ],
        out_shape=[
            jax.ShapeDtypeStruct((count, 3 * width), BF16),
            jax.ShapeDtypeStruct((count, width), BF16),
            jax.ShapeDtypeStruct((count, width), BF16),
            jax.ShapeDtypeStruct((pairs, 2, LEN), F32),
        ],
        scratch_shapes=[
            pltpu.VMEM((count, 3 * width), BF16),
            pltpu.VMEM((LEN, LEN), F32),
            pltpu.VMEM((width, 3 * width), BF16),
            pltpu.SemaphoreType.DMA,
        ],
        compiler_params=params(),
        cost_estimate=cost(28e9, 20e6),
        name="project_attend",
    )


def norm_back(v, gain, grad):
    unit, factor = normal(v)
    g = grad * gain
    pulled = factor * (g - jnp.mean(g, -1, keepdims=True) - unit * jnp.mean(g * unit, -1, keepdims=True))
    return pulled, jnp.sum(grad * unit, 0, keepdims=True), jnp.sum(grad, 0, keepdims=True)


def send(place, tile, column, width, outs, lane, half, first, sem):
    here = pl.ds(column, width)
    if len(outs) == 1:
        per_half = outs[0].shape[1] // 2
        at = pl.ds(pl.multiple_of(half * per_half + lane, 128), width)
        top = pl.ds(pl.multiple_of(first * (outs[0].shape[0] // 16), 16), tile.shape[0])
        pltpu.make_async_copy(tile.at[:, here], outs[0].at[top, at], sem).start()
        return
    chip, core = place[0], place[1]
    step = outs[0].shape[2]
    at = pl.ds(pl.multiple_of(lane, 128), width)
    for index in range(tile.shape[0] // step):
        relative = lax.bitwise_xor(chip, first + index)
        group, spot = lax.bitwise_and(relative, 3), lax.shift_right_logical(relative, 2)
        source = tile.at[pl.ds(index * step, step), here]
        for own, target in ((True, outs[0]), (False, outs[1])):
            copy = pltpu.make_async_copy(source, target.at[group, spot, :, at], sem)
            pl.when((half == core) == own)(copy.start)


def finish(ref, sem):
    pltpu.make_async_copy(ref, ref, sem).wait()


def term_shapes(tall, wide, by_stage):
    if by_stage:
        return [jax.ShapeDtypeStruct((4, 4, tall // 16, wide // 2), BF16)] * 2
    return [jax.ShapeDtypeStruct((tall, wide), BF16)]


def widen_kernel(steps, terms, place, x, attended, out_bias, gain, shift, fc_bias, cot, *rest):
    count = terms + 13
    pieces, rest = rest[:-count], rest[-count:]
    resid, hidden, slope, active = rest[:4]
    outs, rest = rest[4 : 4 + terms], rest[4 + terms :]
    w_out, w_fc, kept, grad, stage, weight_sems, kept_sem, grad_sem, sems = rest
    size, width = x.shape
    depth = w_fc.shape[1]
    step = pl.program_id(0)
    here = pl.ds(pl.multiple_of(lax.rem(step, steps) * size, size), size)

    @pl.when(step == 0)
    def _():
        wait_out = fetch(place, pieces, 0, 0, width // 2, w_out, weight_sems.at[0])
        wait_fc = fetch(place, pieces, 1, width // 2, depth // 2, w_fc, weight_sems.at[1])
        pltpu.make_async_copy(cot, grad, grad_sem).start()
        wait_out()
        wait_fc()

    @pl.when(step < steps)
    def _():
        r = x[...].astype(F32) + dot(attended[...], w_out[...], NN) + out_bias[...]
        resid[...] = r
        unit, _ = normal(r)
        h = (unit * gain[...] + shift[...]).astype(BF16)
        hidden[...] = h
        c = math.sqrt(2.0 / math.pi)
        for first in range(0, depth, width):
            sl = slice(first, first + width)
            u = dot(h, w_fc[:, sl], NN) + fc_bias[:, sl]
            square = u * u
            t = jnp.tanh(u * (c + (c * 0.044715) * square))
            half = 0.5 * (1.0 + t)
            kept[here, sl] = (u * half).astype(BF16)
            slope[:, sl] = (half + 0.5 * u * (1.0 - t * t) * (c + (3 * c * 0.044715) * square)).astype(BF16)
        pltpu.make_async_copy(kept.at[here, :], active.at[here, :], kept_sem).start()

    @pl.when(step >= steps)
    def _():
        tile = step - steps
        slot = lax.rem(tile, 2)

        @pl.when(tile == 0)
        def _():
            finish(grad, grad_sem)

        @pl.when(tile >= 2)
        def _():
            finish(stage.at[slot], sems.at[slot])

        tall = stage.shape[1]
        part = kept[:, pl.ds(pl.multiple_of(tile * tall, tall), tall)]
        stage[slot] = dot(part, grad[...], TN).astype(BF16)
        chips = tall * 16 // depth
        for half in range(2):
            send(place, stage.at[slot], half * (width // 2), width // 2, outs, 0, half, tile * chips, sems.at[slot])

        @pl.when(tile == depth // tall - 1)
        def _():
            finish(stage.at[slot], sems.at[slot])
            finish(stage.at[1 - slot], sems.at[1 - slot])
            finish(kept, kept_sem)


def widen(place, x, attended, out_bias, gain, shift, fc_bias, cot, pieces, after=()):
    count, width = x.shape
    depth = fc_bias.shape[1]
    size, tall = 256, width
    steps = count // size
    early = lambda i: (jnp.minimum(i, steps - 1), 0)
    block = lambda wide: pl.BlockSpec((size, wide), early)
    terms = term_shapes(depth, width, len(pieces) == 8)
    return kernel_call(
        functools.partial(widen_kernel, steps, len(terms)),
        [place, x, attended, out_bias, gain, shift, fc_bias, cot, *pieces],
        after,
        grid=(steps + depth // tall,),
        in_specs=[SMEM, block(width), block(width)]
        + [whole((1, width))] * 3
        + [whole((1, depth)), ANY]
        + [ANY] * len(pieces),
        out_specs=[block(width), block(width), block(depth), ANY] + [ANY] * len(terms),
        out_shape=[
            jax.ShapeDtypeStruct((count, width), F32),
            jax.ShapeDtypeStruct((count, width), BF16),
            jax.ShapeDtypeStruct((count, depth), BF16),
            jax.ShapeDtypeStruct((count, depth), BF16),
        ]
        + terms,
        scratch_shapes=[
            pltpu.VMEM((width, width), BF16),
            pltpu.VMEM((width, depth), BF16),
            pltpu.VMEM((count, depth), BF16),
            pltpu.VMEM((count, width), BF16),
            pltpu.VMEM((2, tall, width), BF16),
            pltpu.SemaphoreType.DMA((2,)),
            pltpu.SemaphoreType.DMA,
            pltpu.SemaphoreType.DMA,
            pltpu.SemaphoreType.DMA((2,)),
        ],
        compiler_params=params(),
        cost_estimate=cost(2 * count * width * (width + 2 * depth), 30e6),
        name="widen",
    )


def narrow_kernel(steps, terms, sides, place, resid, active, slope, cot, proj_bias, gain, hidden, attended, *rest):
    count = terms + 19
    pieces, rest = rest[:-count], rest[-count:]
    wide_pieces, proj_pieces = pieces[:sides], pieces[sides:]
    result, grad_r, grad_o, fc_sum, proj_sum, gain_sum, shift_sum, bias_sum = rest[:8]
    outs, rest = rest[8 : 8 + terms], rest[8 + terms :]
    w_proj, w_fc, w_out, du, dt, h_kept, o_kept, stage, weight_sems, kept_sems, sems = rest
    size, width = resid.shape
    depth = active.shape[1]
    step = pl.program_id(0)
    here = pl.ds(pl.multiple_of(lax.rem(step, steps) * size, size), size)

    @pl.when(step == 0)
    def _():
        wait_proj = fetch(place, proj_pieces, 0, 0, width // 2, w_proj, weight_sems.at[0])
        wait_fc = fetch(place, wide_pieces, 1, width // 2, depth // 2, w_fc, weight_sems.at[1])
        wait_out = fetch(place, wide_pieces, 0, 0, width // 2, w_out, weight_sems.at[2])
        pltpu.make_async_copy(hidden, h_kept, kept_sems.at[0]).start()
        pltpu.make_async_copy(attended, o_kept, kept_sems.at[1]).start()
        for total in (fc_sum, proj_sum, gain_sum, shift_sum, bias_sum):
            total[...] = jnp.zeros_like(total)
        wait_proj()
        wait_fc()
        wait_out()

    @pl.when(step < steps)
    def _():
        g = cot[...]
        for first in range(0, depth, width):
            sl = slice(first, first + width)
            part = (dot(g, w_proj[sl, :], NT) * slope[:, sl].astype(F32)).astype(BF16)
            du[here, sl] = part
            fc_sum[:, sl] += jnp.sum(part.astype(F32), 0, keepdims=True)
        r = resid[...]
        result[...] = (r + dot(active[...], w_proj[...], NN) + proj_bias[...]).astype(BF16)
        wide = g.astype(F32)
        proj_sum[...] += jnp.sum(wide, 0, keepdims=True)
        grad_h = dot(du[here, :], w_fc[...], NT)
        pulled, gains, shifts = norm_back(r, gain[...], grad_h)
        total = wide + pulled
        grad_r[...] = total
        low = total.astype(BF16)
        dt[here, :] = low
        gain_sum[...] += gains
        shift_sum[...] += shifts
        bias_sum[...] += jnp.sum(low.astype(F32), 0, keepdims=True)
        grad_o[...] = dot(low, w_out[...], NT).astype(BF16)

    tiles = depth // width

    @pl.when(step >= steps)
    def _():
        tile = step - steps
        slot = lax.rem(tile, 2)

        @pl.when(tile == 0)
        def _():
            finish(h_kept, kept_sems.at[0])
            finish(o_kept, kept_sems.at[1])

        @pl.when(tile >= 2)
        def _():
            finish(stage.at[slot], sems.at[slot])

        @pl.when(tile < tiles)
        def _():
            part = du[:, pl.ds(pl.multiple_of(lax.rem(tile, tiles) * width, width), width)]
            stage[slot] = dot(h_kept[...], part, TN).astype(BF16)
            lane = lax.rem(tile, tiles // 2) * width
            send(place, stage.at[slot], 0, width, outs, lane, tile // (tiles // 2), 0, sems.at[slot])

        @pl.when(tile == tiles)
        def _():
            stage[slot] = dot(o_kept[...], dt[...], TN).astype(BF16)
            for half in range(2):
                send(place, stage.at[slot], half * (width // 2), width // 2, outs, depth // 2, half, 0, sems.at[slot])
            finish(stage.at[slot], sems.at[slot])
            finish(stage.at[1 - slot], sems.at[1 - slot])


def narrow(place, resid, active, slope, cot, proj_bias, gain, hidden, attended, wide_pieces, proj_pieces, after=()):
    count, width = resid.shape
    depth = active.shape[1]
    size = 256
    steps = count // size
    early = lambda i: (jnp.minimum(i, steps - 1), 0)
    block = lambda wide: pl.BlockSpec((size, wide), early)
    pieces = [*wide_pieces, *proj_pieces]
    terms = term_shapes(width, width + depth, len(proj_pieces) == 8)
    return kernel_call(
        functools.partial(narrow_kernel, steps, len(terms), len(wide_pieces)),
        [place, resid, active, slope, cot, proj_bias, gain, hidden, attended, *pieces],
        after,
        grid=(steps + depth // width + 1,),
        in_specs=[SMEM, block(width), block(depth), block(depth), block(width)]
        + [whole((1, width))] * 2
        + [ANY] * (2 + len(pieces)),
        out_specs=[block(width)] * 3
        + [whole((1, depth))]
        + [whole((1, width))] * 4
        + [ANY] * len(terms),
        out_shape=[
            jax.ShapeDtypeStruct((count, width), BF16),
            jax.ShapeDtypeStruct((count, width), F32),
            jax.ShapeDtypeStruct((count, width), BF16),
            jax.ShapeDtypeStruct((1, depth), F32),
        ]
        + [jax.ShapeDtypeStruct((1, width), F32)] * 4
        + terms,
        scratch_shapes=[
            pltpu.VMEM((depth, width), BF16),
            pltpu.VMEM((width, depth), BF16),
            pltpu.VMEM((width, width), BF16),
            pltpu.VMEM((count, depth), BF16),
            pltpu.VMEM((count, width), BF16),
            pltpu.VMEM((count, width), BF16),
            pltpu.VMEM((count, width), BF16),
            pltpu.VMEM((2, width, width), BF16),
            pltpu.SemaphoreType.DMA((3,)),
            pltpu.SemaphoreType.DMA((2,)),
            pltpu.SemaphoreType.DMA((2,)),
        ],
        compiler_params=params(),
        cost_estimate=cost(2 * count * width * (2 * width + 4 * depth), 40e6),
        name="narrow",
    )


def attend_back_kernel(block, number, terms, place, q_docs, k_docs, q_all, k_all, v_all, o_all, g_all, lse, hidden, *rest):
    dq, dk, dv = rest[:3]
    outs, rest = rest[3 : 3 + terms], rest[3 + terms :]
    bias, k_sum, v_sum, kept, h_kept, stage, sem, sems = rest
    count = LEN // block
    step = pl.program_id(0)

    @pl.when(step == 0)
    def _():
        pltpu.make_async_copy(hidden, h_kept, sem).start()
        for i in range(count):
            sl, reach = slice(i * block, (i + 1) * block), (i + 1) * block
            bias[:reach, sl] = allowed(q_docs[:, sl], k_docs[:reach, :], i * block, (reach, block), 1)

    @pl.when(step < number)
    def _():
        low = lax.broadcasted_iota(jnp.int32, (block, PAIR), 1) < HD
        low_all = lax.broadcasted_iota(jnp.int32, (LEN, PAIR), 1) < HD
        keys = k_all[...]
        key_one = [jnp.where(low_all, keys, jnp.zeros_like(keys)), jnp.where(low_all, jnp.zeros_like(keys), keys)]
        at = pl.ds(pl.multiple_of(lax.rem(step, number) * PAIR, PAIR), PAIR)
        for i in reversed(range(count)):
            sl, reach = slice(i * block, (i + 1) * block), (i + 1) * block
            q, grad = q_all[sl, :], g_all[sl, :]
            turned = (grad.astype(F32) * o_all[sl, :].astype(F32)).T
            parts = []
            for head in range(2):
                lane = low if head == 0 else ~low
                q_one = jnp.where(lane, q, jnp.zeros_like(q))
                g_one = jnp.where(lane, grad, jnp.zeros_like(grad))
                inner = jnp.sum(turned[head * HD : (head + 1) * HD, :], 0, keepdims=True)
                score = dot(k_all[:reach, :], q_one, NT) + bias[:reach, sl]
                prob = jnp.exp(score - lse[0, head : head + 1, sl])
                v_part = dot(prob.astype(BF16), g_one, NN)
                slope = dot(v_all[:reach, :], g_one, NT)
                dscore = (prob * (slope - inner)).astype(BF16)
                k_part = dot(dscore, q_one, NN)
                if i == count - 1 and head == 0:
                    k_sum[...] = k_part
                    v_sum[...] = v_part
                else:
                    k_sum[:reach, :] += k_part
                    v_sum[:reach, :] += v_part
                parts.append(dot(dscore, key_one[head][:reach], TN))
            part = ((parts[0] + parts[1]) * (1.0 / math.sqrt(HD))).astype(BF16)
            dq[sl, :] = part
            kept[0, sl, at] = part
        for index, (ref, total) in enumerate(((dk, k_sum), (dv, v_sum))):
            part = total[...].astype(BF16)
            ref[...] = part
            kept[1 + index, :, at] = part

    wide = stage.shape[3]

    @pl.when(step >= number)
    def _():
        tile = step - number
        slot = lax.rem(tile, 2)

        @pl.when(tile == 0)
        def _():
            finish(h_kept, sem)

        for index in range(3):
            part = kept[index, :, pl.ds(pl.multiple_of(tile * wide, wide), wide)]
            stage[slot, index] = dot(h_kept[...], part, TN).astype(BF16)
        for index in range(3):
            for half in range(2):
                send(
                    place,
                    stage.at[slot, index],
                    half * (wide // 2),
                    wide // 2,
                    outs,
                    index * (number * PAIR // 2) + tile * (wide // 2),
                    half,
                    0,
                    sems.at[slot],
                )

        @pl.when(tile == number * PAIR // wide - 1)
        def _():
            finish(stage.at[slot], sems.at[slot])
            if number * PAIR // wide > 1:
                finish(stage.at[1 - slot], sems.at[1 - slot])


def attend_back(place, mixed, attended, grad_o, lse, docs, hidden, first, number, by_stage, after=()):
    width = attended.shape[1]
    pairs = width // PAIR
    block = 256
    wide = 2 * PAIR
    steps = number * PAIR // wide
    pair = lambda i: jnp.minimum(i, number - 1)
    column = lambda base: pl.BlockSpec((LEN, PAIR), lambda i: (0, base + pair(i)))
    terms = term_shapes(width, 3 * number * PAIR, by_stage)
    return kernel_call(
        functools.partial(attend_back_kernel, block, number, len(terms)),
        [place, docs.reshape(1, LEN), docs.reshape(LEN, 1), mixed, mixed, mixed, attended, grad_o, lse, hidden],
        after,
        grid=(number + steps,),
        in_specs=[
            SMEM,
            whole((1, LEN)),
            whole((LEN, 1)),
            column(first),
            column(pairs + first),
            column(2 * pairs + first),
            column(first),
            column(first),
            pl.BlockSpec((1, 2, LEN), lambda i: (first + pair(i), 0, 0)),
            ANY,
        ],
        out_specs=[column(0)] * 3 + [ANY] * len(terms),
        out_shape=[jax.ShapeDtypeStruct((LEN, PAIR * number), BF16)] * 3 + terms,
        scratch_shapes=[
            pltpu.VMEM((LEN, LEN), F32),
            pltpu.VMEM((LEN, PAIR), F32),
            pltpu.VMEM((LEN, PAIR), F32),
            pltpu.VMEM((3, LEN, PAIR * number), BF16),
            pltpu.VMEM((LEN, width), BF16),
            pltpu.VMEM((2, 3, width, wide), BF16),
            pltpu.SemaphoreType.DMA,
            pltpu.SemaphoreType.DMA((2,)),
        ],
        compiler_params=params(),
        cost_estimate=cost(42e9 * number / pairs, 10e6),
        name="attend_back",
    )


def first_back_kernel(place, x, grad_r, gain, *rest):
    parts, pieces, rest = rest[:6], rest[6:-7], rest[-7:]
    grad_x, gain_sum, shift_sum, q_sum, v_sum, weight, sem = rest
    width = x.shape[1]

    @pl.when(pl.program_id(0) == 0)
    def _():
        fetch(place, pieces, 0, 0, 3 * width // 2, weight, sem)()
        for total in (gain_sum, shift_sum, q_sum, v_sum):
            total[...] = jnp.zeros_like(total)

    grad_h = None
    at = 0
    for index, part in enumerate(parts):
        wide = part.shape[1]
        term = dot(part[...], weight[:, at : at + wide], NT)
        grad_h = term if grad_h is None else grad_h + term
        if index // 2 != 1:
            into = q_sum if index // 2 == 0 else v_sum
            lane = at % width
            into[:, lane : lane + wide] += jnp.sum(part[...].astype(F32), 0, keepdims=True)
        at += wide
    pulled, gains, shifts = norm_back(x[...].astype(F32), gain[...], grad_h)
    grad_x[...] = grad_r[...] + pulled
    gain_sum[...] += gains
    shift_sum[...] += shifts


def first_back(place, x, grad_r, gain, parts, pieces, after=()):
    count, width = x.shape
    block = 256
    return kernel_call(
        first_back_kernel,
        [place, x, grad_r, gain, *parts, *pieces],
        after,
        grid=(count // block,),
        in_specs=[SMEM, rows(block, width), rows(block, width), whole((1, width))]
        + [rows(block, part.shape[1]) for part in parts]
        + [ANY] * len(pieces),
        out_specs=[rows(block, width)] + [whole((1, width))] * 4,
        out_shape=[jax.ShapeDtypeStruct((count, width), F32)] + [jax.ShapeDtypeStruct((1, width), F32)] * 4,
        scratch_shapes=[pltpu.VMEM((width, 3 * width), BF16), pltpu.SemaphoreType.DMA],
        compiler_params=params(),
        cost_estimate=cost(6 * count * width * width, 16e6),
        name="first_back",
    )


def one_hot(shape, base, span, first):
    lane = lax.broadcasted_iota(jnp.int32, shape, 0)
    element = lax.broadcasted_iota(jnp.int32, shape, 1) + first
    return lane == base + lax.rem(element, span)


def owner(shape, span, first):
    element = lax.broadcasted_iota(jnp.int32, shape, 1) + first
    return lax.broadcasted_iota(jnp.int32, shape, 0) == element // span


def slots(unit, width):
    found, base = [], 0
    for span in (1, 1, 2, 1, 1, 1, 4, 1):
        found += [(base * unit, span * unit, index * width) for index in range(span)]
        base += span
    return found


def unpack_kernel(table, out):
    devices, lanes = table.shape
    width = out.shape[1]
    for index, (base, span, first) in enumerate(slots(lanes // 12, width)):
        pick = one_hot((lanes, width), base, span, first).astype(BF16)
        value = dot(table[...], pick, NN)
        out[index : index + 1, :] = jnp.sum(jnp.where(owner((devices, width), span, first), value, 0.0), 0, keepdims=True)


def unpack(table):
    devices, lanes = table.shape
    width = devices * lanes // 12
    return pl.pallas_call(
        unpack_kernel,
        out_shape=jax.ShapeDtypeStruct((12, width), F32),
        compiler_params=params(),
        name="unpack",
    )(table)


def pack_kernel(*refs):
    vectors, out = refs[:-1], refs[-1]
    devices, lanes = out.shape
    width = vectors[0].shape[1]
    rows_of = [vector[:, first : first + width] for vector in vectors for first in range(0, vector.shape[1], width)]
    total = jnp.zeros(out.shape, F32)
    for row, (base, span, first) in zip(rows_of, slots(lanes // 12, width)):
        pick = one_hot((lanes, width), base, span, first).astype(BF16)
        spread = jnp.where(owner((devices, width), span, first), row, 0.0)
        for _ in range(3):
            part = spread.astype(BF16)
            total = total + dot(part, pick, NT)
            spread = spread - part.astype(F32)
    out[...] = total


def pack(vectors, devices):
    lanes = sum(v.shape[1] for v in vectors) // devices
    return pl.pallas_call(
        pack_kernel,
        out_shape=jax.ShapeDtypeStruct((devices, lanes), F32),
        compiler_params=params(),
        name="pack",
    )(*vectors)


def staged(
    tokens,
    doc_ids,
    d_out,
    ln1_gain,
    ln1_shift,
    qkv_weight,
    qv_bias,
    out_weight,
    out_bias,
    ln2_gain,
    ln2_shift,
    fc_weight,
    fc_bias,
    proj_weight,
    proj_bias,
):
    width = tokens.shape[1]
    depth = fc_weight.shape[1]
    devices = lax.axis_size("dp") * lax.axis_size("fsdp")
    index = lax.axis_index("dp") * lax.axis_size("fsdp") + lax.axis_index("fsdp")
    core = index & 1
    place = jnp.stack([index >> 1, core]).astype(jnp.int32)
    pairs = width // PAIR
    cut = 4
    by_stage = (lax.axis_size("dp"), lax.axis_size("fsdp")) == (8, 4)

    smalls = [ln1_gain, ln1_shift, qv_bias, out_bias, ln2_gain, ln2_shift, fc_bias, proj_bias]
    smalls = jnp.concatenate([v.astype(F32) for v in smalls]).reshape(1, -1).astype(BF16)
    if by_stage:
        first_column = gather_z(pair_block(qkv_weight, core))
        wide_block = jnp.concatenate([pair_block(out_weight, core), pair_block(fc_weight, core)], 1)
        proj_block = pair_block(proj_weight, core)
        first_own = gather_xy(first_column)
        smalls, wide_block = tie([smalls, wide_block], first_column)
        table = gather_small(smalls, index)
        wide_column = gather_z(wide_block)
        wide_column, *first_own = tie([wide_column], *first_own) + first_own
        wide_own = gather_xy(wide_column)
        first_pieces = gather_core(first_own)
        (proj_block,) = tie([proj_block], wide_column)
    else:
        first_pieces, proj_pieces = [gather_all(qkv_weight)], [gather_all(proj_weight)]
        wide_pieces = [gather_all(w) for w in (out_weight, fc_weight)]
        wide_column = None
        table = gather_all(smalls)
    hold = lambda *some: list(some) if by_stage else []
    cores = scatter_core if by_stage else lambda terms: terms[0]
    planes = scatter_xy if by_stage else lambda terms, *after: terms
    columns = scatter_z if by_stage else lambda terms, *after: scatter_all(terms.astype(F32))
    vectors = unpack(table)
    row = lambda at, count=1: vectors[at : at + count].reshape(1, -1)

    mixed, h_one, attended, lse = project_attend(
        place, tokens, row(0), row(1), row(2), row(3), doc_ids, first_pieces, after=hold(wide_column)
    )
    if by_stage:
        proj_column = gather_z(proj_block, lse)
        wide_own = tie(wide_own, lse)
        proj_column, *wide_own = tie([proj_column, *wide_own], proj_column)
        proj_own = gather_xy(proj_column)
        wide_pieces = gather_core(wide_own)
    resid, h_two, slope, active, *proj_terms = widen(
        place, tokens, attended, row(4), row(5), row(6), row(7, 4), d_out, wide_pieces
    )
    if by_stage:
        proj_own = tie(proj_own, resid)
        proj_pieces = gather_core(proj_own)
        proj_terms = tie(proj_terms, *proj_own)
    proj_sums = cores(proj_terms)
    result, grad_r, grad_o, fc_sum, proj_sum, gain_two, shift_two, out_sum, *wide_terms = narrow(
        place,
        resid,
        active,
        slope,
        d_out,
        row(11),
        row(5),
        h_two,
        attended,
        wide_pieces,
        proj_pieces,
        after=hold(*proj_sums),
    )
    if by_stage:
        proj_sums = planes(proj_sums, grad_o)
        wide_terms = tie(wide_terms, *proj_sums)
    wide_sums = cores(wide_terms)
    *head, head_one, head_two = (lambda found: found if by_stage else [*found, None])(
        attend_back(
            place,
            mixed,
            attended,
            grad_o,
            lse,
            doc_ids,
            h_one,
            0,
            cut,
            by_stage,
            after=hold(*proj_sums, *wide_sums),
        )
    )
    proj_grad = columns(proj_sums, head_one)
    wide_sums = planes(wide_sums, head_one)
    if by_stage:
        head_one, head_two = tie([head_one, head_two], proj_grad, *wide_sums)
    head_sums = cores([head_one, head_two])
    *tail, tail_one, tail_two = (lambda found: found if by_stage else [*found, None])(
        attend_back(
            place,
            mixed,
            attended,
            grad_o,
            lse,
            doc_ids,
            h_one,
            cut,
            pairs - cut,
            by_stage,
            after=hold(*head_sums, *wide_sums),
        )
    )
    parts = [part for both in zip(head, tail) for part in both]
    head_sums = planes(head_sums, tail_one)
    wide_grad = columns(wide_sums, tail_one)
    if by_stage:
        tail_one, tail_two = tie([tail_one, tail_two], wide_grad, *head_sums)
    tail_sums = cores([tail_one, tail_two])
    grad_x, gain_one, shift_one, q_sum, v_sum = first_back(
        place, tokens, grad_r, row(0), parts, first_pieces, after=hold(*head_sums, *tail_sums)
    )
    sums = [gain_one, shift_one, q_sum, v_sum, out_sum, gain_two, shift_two, fc_sum, proj_sum]
    sums = pack(sums, devices)
    head_grad = columns(head_sums, grad_x)
    tail_grad = columns(planes(tail_sums, grad_x))

    def sides(grad):
        if by_stage:
            return own_rows(grad, core)
        return jnp.split(grad, 2, 1)

    proj_grad = jnp.concatenate(sides(proj_grad), 1)
    both = sides(wide_grad)
    half = depth // 2
    fc_grad = jnp.concatenate([side[:, :half] for side in both], 1)
    out_grad = jnp.concatenate([side[:, half:] for side in both], 1)
    parts = []
    heads, tails = sides(head_grad), sides(tail_grad)
    for section in range(3):
        for both, number in ((heads, cut), (tails, pairs - cut)):
            start = section * number * PAIR // 2
            for pair in range(0, number, 2):
                lane = start + pair * PAIR // 2
                parts += [side[:, lane : lane + PAIR] for side in both]
    qkv_grad = jnp.concatenate(parts, 1)
    own = scatter_small(sums, index) if by_stage else scatter_all(sums).reshape(-1)
    n = width // devices
    spots = (0, n, 2 * n, 4 * n, 5 * n, 6 * n, 7 * n, 11 * n, 12 * n)
    s = [own[a:b] for a, b in zip(spots[:-1], spots[1:])]
    return (
        result,
        grad_x,
        s[0],
        s[1],
        qkv_grad,
        s[2],
        out_grad,
        s[3],
        s[4],
        s[5],
        fc_grad,
        s[6],
        proj_grad,
        s[7],
    )


def solution(mesh):
    every, block = P(AXES), P(AXES, None)
    ins = (block, every, block, every, every, block, every, block, every, every, every, block, every, block, every)
    outs = (block, block, every, every, block, every, block, every, every, every, block, every, block, every)
    return jax.shard_map(staged, mesh=mesh, in_specs=ins, out_specs=outs, check_vma=False)
```

```python
import functools
import math

import jax
import jax.numpy as jnp
from jax import lax
from jax.experimental import pallas as pl
from jax.experimental.pallas import tpu as pltpu
from jax.sharding import PartitionSpec as P

HD = 64
LEN = 1024
PAIR = 2 * HD
EPS = 1e-05
NEG = -1e30
AXES = ("dp", "fsdp")

F32 = jnp.float32
BF16 = jnp.bfloat16
NN = (((1,), (0,)), ((), ()))
NT = (((1,), (1,)), ((), ()))
TN = (((0,), (0,)), ((), ()))
ANY = pl.BlockSpec(memory_space=pl.ANY)
HBM = pl.BlockSpec(memory_space=pltpu.HBM)
SMEM = pl.BlockSpec(memory_space=pltpu.SMEM)

CORE, X, Y, Z0, Z1 = 1, 2, 4, 8, 16
CX, CY, CZ0, CZ1 = 1, 2, 4, 8
GROUPS = tuple(tuple(near | far for far in (0, CZ0, CZ1, CZ0 | CZ1)) for near in (0, CX, CY, CX | CY))


def dot(a, b, dims):
    return lax.dot_general(a, b, dims, preferred_element_type=F32)


def params(size):
    return pltpu.CompilerParams(vmem_limit_bytes=size << 20)


def cost(flops, size):
    return pl.CostEstimate(flops=int(flops), bytes_accessed=int(size), transcendentals=0)


def whole(shape):
    return pl.BlockSpec(shape, lambda *g: (0,) * len(shape))


def rows(block, width):
    return pl.BlockSpec((block, width), lambda i: (i, 0))


def swap(array, bit):
    count = lax.axis_size("dp") * lax.axis_size("fsdp")
    return lax.ppermute(array, AXES, [(i, i ^ bit) for i in range(count)])


def halves(array, core):
    width = array.shape[1] // 2
    low, high = array[:, :width], array[:, width:]
    first = core == 0
    return jnp.where(first, low, high), jnp.where(first, high, low)


def pair_block(array, core, extra=None):
    keep, send = halves(array, core)
    if extra is not None:
        keep, send = jnp.concatenate([keep, extra], 1), jnp.concatenate([send, extra], 1)
    other = swap(send, CORE)
    first = core == 0
    return jnp.concatenate([jnp.where(first, keep, other), jnp.where(first, other, keep)], 0)


def gather_z(block, *after):
    got = tie([swap(block, bits) for bits in (Z0, Z1, Z0 | Z1)], *after)
    return jnp.stack([block] + got)


def gather_xy(column):
    return [column] + [swap(column, bits) for bits in (X, Y, X | Y)]


def gather_core(own):
    return [*own, *(swap(piece, CORE) for piece in own)]


def add(*terms):
    return functools.reduce(lambda a, b: a + b, [t.astype(F32) for t in terms])


def scatter_core(terms):
    mine, other = terms
    got = swap(other, CORE)
    return [add(mine[g], got[g]).astype(BF16) for g in range(4)]


def scatter_xy(sums, *after):
    return sum_xy(sums, tie([swap(part, bits) for part, bits in zip(sums[1:], (X, Y, X | Y))], *after))


def sum_xy(sums, got):
    return [add(*(part[spot] for part in [sums[0]] + got)).astype(BF16) for spot in range(4)]


def scatter_z(sums, *after):
    got = tie([swap(part, bits) for part, bits in zip(sums[1:], (Z0, Z1, Z0 | Z1))], *after)
    return add(sums[0], *got)


def tie(arrays, *others):
    if not others:
        return list(arrays)
    return list(lax.optimization_barrier((*arrays, *others))[: len(arrays)])


def kernel_call(kernel, inputs, after, **how):
    return pl.pallas_call(kernel, **how)(*tie(inputs[:1], *after), *inputs[1:])


def own_rows(block, core):
    count = block.shape[0] // 2
    low, high = block[:count], block[count:]
    first = core == 0
    keep = jnp.where(first, low, high)
    got = swap(jnp.where(first, high, low), CORE)
    return jnp.where(first, keep, got), jnp.where(first, got, keep)


def gather_all(array):
    return lax.all_gather(array, AXES, axis=0, tiled=True)


def scatter_all(array):
    return lax.psum_scatter(array, AXES, scatter_dimension=0, tiled=True)


def scatter_small(table, index):
    for bit in (Z1, Z0, Y, X, CORE):
        count = table.shape[0] // 2
        low = (index & bit) == 0
        keep = jnp.where(low, table[:count], table[count:])
        send = jnp.where(low, table[count:], table[:count])
        table = keep + swap(send, bit)
    return table.reshape(-1)


def fetch(place, pieces, which, lane, width, into, sem):
    if len(pieces) < 8:
        pltpu.make_async_copy(pieces[which], into, sem).start()
        return lambda: pltpu.make_async_copy(into, into, sem).wait()
    chip, core = place[0], place[1]
    step = into.shape[0] // 16
    for side in range(2):
        half = core if side == 0 else 1 - core
        column = pl.ds(pl.multiple_of(half * width, 128), width)
        for group in range(4):
            for spot, relative in enumerate(GROUPS[group]):
                owner = lax.bitwise_xor(chip, relative)
                pltpu.make_async_copy(
                    pieces[4 * side + group].at[spot, :, pl.ds(lane, width)],
                    into.at[pl.ds(pl.multiple_of(owner * step, step), step), column],
                    sem,
                ).start()
    return lambda: pltpu.make_async_copy(into, into, sem).wait()


def normal(v):
    center = v - jnp.mean(v, -1, keepdims=True)
    spread = jnp.mean(center * center, -1, keepdims=True)
    factor = lax.rsqrt(spread + EPS)
    return center * factor, factor


def allowed(q_doc, k_doc, first, shape, q_dim):
    q_pos = lax.broadcasted_iota(jnp.int32, shape, q_dim) + first
    k_pos = lax.broadcasted_iota(jnp.int32, shape, 1 - q_dim)
    allow = ((k_pos <= q_pos) & (q_doc == k_doc) & (k_doc > 0)) | (k_pos == q_pos)
    return jnp.where(allow, 0.0, NEG)


def project_attend_kernel(steps, block, place, x, gain, shift, q_bias, v_bias, q_docs, k_docs, *rest):
    pieces, rest = rest[:-9], rest[-9:]
    mixed, hidden, out, lse, kept, bias, weight, sem, kept_sem = rest
    width = x.shape[1]
    size = x.shape[0]
    step = pl.program_id(0)

    @pl.when(step == 0)
    def _():
        wait = fetch(place, pieces, 0, 0, 3 * width // 2, weight, sem)
        for i in range(LEN // block):
            sl, reach = slice(i * block, (i + 1) * block), (i + 1) * block
            bias[sl, :reach] = allowed(q_docs[sl, :], k_docs[:, :reach], i * block, (block, reach), 0)
        wait()

    @pl.when(step < steps)
    def _():
        unit, _ = normal(x[...].astype(F32))
        h = (unit * gain[...] + shift[...]).astype(BF16)
        hidden[...] = h
        scale = 1.0 / math.sqrt(HD)
        here = pl.ds(pl.multiple_of(step * size, size), size)
        for part in range(3):
            sl = slice(part * width, (part + 1) * width)
            value = dot(h, weight[:, sl], NN)
            if part == 0:
                value = (value + q_bias[...]).astype(BF16).astype(F32) * scale
            if part == 2:
                value = value + v_bias[...]
            kept[here, sl] = value.astype(BF16)
        pltpu.make_async_copy(kept.at[here, :], mixed.at[here, :], kept_sem).start()

    @pl.when(step >= steps)
    def _():
        lane = (step - steps) * PAIR
        q_at, k_at, v_at = (pl.ds(pl.multiple_of(lane + part * width, PAIR), PAIR) for part in range(3))
        low = lax.broadcasted_iota(jnp.int32, (block, PAIR), 1) < HD
        for i in range(LEN // block):
            sl, reach = slice(i * block, (i + 1) * block), (i + 1) * block
            q = kept[sl, q_at]
            outs, logs = [], []
            for head in range(2):
                q_one = jnp.where(low if head == 0 else ~low, q, jnp.zeros_like(q))
                score = dot(q_one, kept[:reach, k_at], NT) + bias[sl, :reach]
                top = jnp.max(score, -1, keepdims=True)
                expo = jnp.exp(score - top)
                total = jnp.sum(expo, -1, keepdims=True)
                outs.append(dot(expo.astype(BF16), kept[:reach, v_at], NN) / total)
                logs.append(top + jnp.log(total))
            out[sl, :] = jnp.where(low, outs[0], outs[1]).astype(BF16)
            turned = jnp.where(low, logs[0], logs[1]).T
            lse[0, 0:1, sl] = turned[0:1, :]
            lse[0, 1:2, sl] = turned[HD : HD + 1, :]

    @pl.when(step == pl.num_programs(0) - 1)
    def _():
        finish(kept, kept_sem)


def project_attend(place, x, gain, shift, q_bias, v_bias, docs, pieces, after=()):
    count, width = x.shape
    size, block = 256, 512
    steps = count // size
    pairs = width // PAIR
    early = lambda i: (jnp.minimum(i, steps - 1), 0)
    late = lambda i: jnp.maximum(i - steps, 0)
    return kernel_call(
        functools.partial(project_attend_kernel, steps, block),
        [place, x, gain, shift, q_bias, v_bias, docs.reshape(LEN, 1), docs.reshape(1, LEN), *pieces],
        after,
        grid=(steps + pairs,),
        in_specs=[SMEM, pl.BlockSpec((size, width), early)]
        + [whole((1, width))] * 4
        + [whole((LEN, 1)), whole((1, LEN))]
        + [HBM] * len(pieces),
        out_specs=[
            HBM,
            pl.BlockSpec((size, width), early),
            pl.BlockSpec((LEN, PAIR), lambda i: (0, late(i))),
            pl.BlockSpec((1, 2, LEN), lambda i: (late(i), 0, 0)),
        ],
        out_shape=[
            jax.ShapeDtypeStruct((count, 3 * width), BF16),
            jax.ShapeDtypeStruct((count, width), BF16),
            jax.ShapeDtypeStruct((count, width), BF16),
            jax.ShapeDtypeStruct((pairs, 2, LEN), F32),
        ],
        scratch_shapes=[
            pltpu.VMEM((count, 3 * width), BF16),
            pltpu.VMEM((LEN, LEN), F32),
            pltpu.VMEM((width, 3 * width), BF16),
            pltpu.SemaphoreType.DMA,
            pltpu.SemaphoreType.DMA,
        ],
        compiler_params=params(24),
        cost_estimate=cost(28e9, 20e6),
        name="project_attend",
    )


def norm_back(v, gain, grad):
    unit, factor = normal(v)
    g = grad * gain
    pulled = factor * (g - jnp.mean(g, -1, keepdims=True) - unit * jnp.mean(g * unit, -1, keepdims=True))
    return pulled, jnp.sum(grad * unit, 0, keepdims=True), jnp.sum(grad, 0, keepdims=True)


def send(place, tile, column, width, outs, lane, half, first, sem):
    here = pl.ds(column, width)
    if len(outs) == 1:
        per_half = outs[0].shape[1] // 2
        at = pl.ds(pl.multiple_of(half * per_half + lane, 128), width)
        top = pl.ds(pl.multiple_of(first * (outs[0].shape[0] // 16), 16), tile.shape[0])
        pltpu.make_async_copy(tile.at[:, here], outs[0].at[top, at], sem).start()
        return
    chip, core = place[0], place[1]
    step = outs[0].shape[2]
    at = pl.ds(pl.multiple_of(lane, 128), width)
    for index in range(tile.shape[0] // step):
        relative = lax.bitwise_xor(chip, first + index)
        group, spot = lax.bitwise_and(relative, 3), lax.shift_right_logical(relative, 2)
        source = tile.at[pl.ds(index * step, step), here]
        for own, target in ((True, outs[0]), (False, outs[1])):
            copy = pltpu.make_async_copy(source, target.at[group, spot, :, at], sem)
            pl.when((half == core) == own)(copy.start)


def finish(ref, sem):
    pltpu.make_async_copy(ref, ref, sem).wait()


def term_shapes(tall, wide, by_stage):
    if by_stage:
        return [jax.ShapeDtypeStruct((4, 4, tall // 16, wide // 2), BF16)] * 2
    return [jax.ShapeDtypeStruct((tall, wide), BF16)]


def widen_kernel(steps, terms, place, x, attended, out_bias, gain, shift, fc_bias, cot, *rest):
    count = terms + 15
    pieces, rest = rest[:-count], rest[-count:]
    resid, hidden, slope, active = rest[:4]
    outs, rest = rest[4 : 4 + terms], rest[4 + terms :]
    w_out, w_fc, kept, bent, grad, stage, weight_sems, kept_sem, bent_sem, grad_sem, sems = rest
    size, width = x.shape
    depth = w_fc.shape[1]
    step = pl.program_id(0)
    here = pl.ds(pl.multiple_of(lax.rem(step, steps) * size, size), size)

    @pl.when(step == 0)
    def _():
        wait_out = fetch(place, pieces, 0, 0, width // 2, w_out, weight_sems.at[0])
        wait_fc = fetch(place, pieces, 1, width // 2, depth // 2, w_fc, weight_sems.at[1])
        pltpu.make_async_copy(cot, grad, grad_sem).start()
        wait_out()
        wait_fc()

    @pl.when(step < steps)
    def _():
        r = x[...].astype(F32) + dot(attended[...], w_out[...], NN) + out_bias[...]
        resid[...] = r
        unit, _ = normal(r)
        h = (unit * gain[...] + shift[...]).astype(BF16)
        hidden[...] = h
        c = math.sqrt(2.0 / math.pi)
        for first in range(0, depth, width):
            sl = slice(first, first + width)
            u = dot(h, w_fc[:, sl], NN) + fc_bias[:, sl]
            square = u * u
            t = jnp.tanh(u * (c + (c * 0.044715) * square))
            half = 0.5 * (1.0 + t)
            kept[here, sl] = (u * half).astype(BF16)
            bent[here, sl] = (half + 0.5 * u * (1.0 - t * t) * (c + (3 * c * 0.044715) * square)).astype(BF16)
        pltpu.make_async_copy(kept.at[here, :], active.at[here, :], kept_sem).start()
        pltpu.make_async_copy(bent.at[here, :], slope.at[here, :], bent_sem).start()

    @pl.when(step >= steps)
    def _():
        tile = step - steps
        slot = lax.rem(tile, 2)

        @pl.when(tile == 0)
        def _():
            finish(grad, grad_sem)

        @pl.when(tile >= 2)
        def _():
            finish(stage.at[slot], sems.at[slot])

        tall = stage.shape[1]
        part = kept[:, pl.ds(pl.multiple_of(tile * tall, tall), tall)]
        stage[slot] = dot(part, grad[...], TN).astype(BF16)
        chips = tall * 16 // depth
        for half in range(2):
            send(place, stage.at[slot], half * (width // 2), width // 2, outs, 0, half, tile * chips, sems.at[slot])

        @pl.when(tile == depth // tall - 1)
        def _():
            finish(stage.at[slot], sems.at[slot])
            finish(stage.at[1 - slot], sems.at[1 - slot])
            finish(kept, kept_sem)
            finish(bent, bent_sem)


def widen(place, x, attended, out_bias, gain, shift, fc_bias, cot, pieces, after=()):
    count, width = x.shape
    depth = fc_bias.shape[1]
    size, tall = 256, width
    steps = count // size
    early = lambda i: (jnp.minimum(i, steps - 1), 0)
    block = lambda wide: pl.BlockSpec((size, wide), early)
    terms = term_shapes(depth, width, len(pieces) == 8)
    return kernel_call(
        functools.partial(widen_kernel, steps, len(terms)),
        [place, x, attended, out_bias, gain, shift, fc_bias, cot, *pieces],
        after,
        grid=(steps + depth // tall,),
        in_specs=[SMEM, block(width), block(width)]
        + [whole((1, width))] * 3
        + [whole((1, depth)), ANY]
        + [HBM] * len(pieces),
        out_specs=[block(width), block(width), HBM, HBM] + [ANY] * len(terms),
        out_shape=[
            jax.ShapeDtypeStruct((count, width), F32),
            jax.ShapeDtypeStruct((count, width), BF16),
            jax.ShapeDtypeStruct((count, depth), BF16),
            jax.ShapeDtypeStruct((count, depth), BF16),
        ]
        + terms,
        scratch_shapes=[
            pltpu.VMEM((width, width), BF16),
            pltpu.VMEM((width, depth), BF16),
            pltpu.VMEM((count, depth), BF16),
            pltpu.VMEM((count, depth), BF16),
            pltpu.VMEM((count, width), BF16),
            pltpu.VMEM((2, tall, width), BF16),
            pltpu.SemaphoreType.DMA((2,)),
            pltpu.SemaphoreType.DMA,
            pltpu.SemaphoreType.DMA,
            pltpu.SemaphoreType.DMA,
            pltpu.SemaphoreType.DMA((2,)),
        ],
        compiler_params=params(32),
        cost_estimate=cost(2 * count * width * (width + 2 * depth), 30e6),
        name="widen",
    )


def narrow_kernel(steps, terms, sides, place, resid, active, slope, cot, proj_bias, gain, hidden, attended, *rest):
    count = terms + 19
    pieces, rest = rest[:-count], rest[-count:]
    wide_pieces, proj_pieces = pieces[:sides], pieces[sides:]
    result, grad_r, grad_o, fc_sum, proj_sum, gain_sum, shift_sum, bias_sum = rest[:8]
    outs, rest = rest[8 : 8 + terms], rest[8 + terms :]
    w_proj, w_fc, w_out, du, dt, h_kept, o_kept, stage, weight_sems, kept_sems, sems = rest
    size, width = resid.shape
    depth = active.shape[1]
    step = pl.program_id(0)
    here = pl.ds(pl.multiple_of(lax.rem(step, steps) * size, size), size)

    @pl.when(step == 0)
    def _():
        wait_proj = fetch(place, proj_pieces, 0, 0, width // 2, w_proj, weight_sems.at[0])
        wait_fc = fetch(place, wide_pieces, 1, width // 2, depth // 2, w_fc, weight_sems.at[1])
        wait_out = fetch(place, wide_pieces, 0, 0, width // 2, w_out, weight_sems.at[2])
        pltpu.make_async_copy(hidden, h_kept, kept_sems.at[0]).start()
        pltpu.make_async_copy(attended, o_kept, kept_sems.at[1]).start()
        for total in (fc_sum, proj_sum, gain_sum, shift_sum, bias_sum):
            total[...] = jnp.zeros_like(total)
        wait_proj()
        wait_fc()
        wait_out()

    @pl.when(step < steps)
    def _():
        g = cot[...]
        for first in range(0, depth, width):
            sl = slice(first, first + width)
            part = (dot(g, w_proj[sl, :], NT) * slope[:, sl].astype(F32)).astype(BF16)
            du[here, sl] = part
            fc_sum[:, sl] += jnp.sum(part.astype(F32), 0, keepdims=True)
        r = resid[...]
        result[...] = (r + dot(active[...], w_proj[...], NN) + proj_bias[...]).astype(BF16)
        wide = g.astype(F32)
        proj_sum[...] += jnp.sum(wide, 0, keepdims=True)
        grad_h = dot(du[here, :], w_fc[...], NT)
        pulled, gains, shifts = norm_back(r, gain[...], grad_h)
        total = wide + pulled
        grad_r[...] = total
        low = total.astype(BF16)
        dt[here, :] = low
        gain_sum[...] += gains
        shift_sum[...] += shifts
        bias_sum[...] += jnp.sum(low.astype(F32), 0, keepdims=True)
        grad_o[...] = dot(low, w_out[...], NT).astype(BF16)

    tiles = depth // width

    @pl.when(step >= steps)
    def _():
        tile = step - steps
        slot = lax.rem(tile, 2)

        @pl.when(tile == 0)
        def _():
            finish(h_kept, kept_sems.at[0])
            finish(o_kept, kept_sems.at[1])

        @pl.when(tile >= 2)
        def _():
            finish(stage.at[slot], sems.at[slot])

        @pl.when(tile < tiles)
        def _():
            part = du[:, pl.ds(pl.multiple_of(lax.rem(tile, tiles) * width, width), width)]
            stage[slot] = dot(h_kept[...], part, TN).astype(BF16)
            lane = lax.rem(tile, tiles // 2) * width
            send(place, stage.at[slot], 0, width, outs, lane, tile // (tiles // 2), 0, sems.at[slot])

        @pl.when(tile == tiles)
        def _():
            stage[slot] = dot(o_kept[...], dt[...], TN).astype(BF16)
            for half in range(2):
                send(place, stage.at[slot], half * (width // 2), width // 2, outs, depth // 2, half, 0, sems.at[slot])
            finish(stage.at[slot], sems.at[slot])
            finish(stage.at[1 - slot], sems.at[1 - slot])


def narrow(place, resid, active, slope, cot, proj_bias, gain, hidden, attended, wide_pieces, proj_pieces, after=()):
    count, width = resid.shape
    depth = active.shape[1]
    size = 256
    steps = count // size
    early = lambda i: (jnp.minimum(i, steps - 1), 0)
    block = lambda wide: pl.BlockSpec((size, wide), early)
    pieces = [*wide_pieces, *proj_pieces]
    terms = term_shapes(width, width + depth, len(proj_pieces) == 8)
    return kernel_call(
        functools.partial(narrow_kernel, steps, len(terms), len(wide_pieces)),
        [place, resid, active, slope, cot, proj_bias, gain, hidden, attended, *pieces],
        after,
        grid=(steps + depth // width + 1,),
        in_specs=[SMEM, block(width), block(depth), block(depth), block(width)]
        + [whole((1, width))] * 2
        + [ANY] * 2 + [HBM] * len(pieces),
        out_specs=[block(width)] * 3
        + [whole((1, depth))]
        + [whole((1, width))] * 4
        + [ANY] * len(terms),
        out_shape=[
            jax.ShapeDtypeStruct((count, width), BF16),
            jax.ShapeDtypeStruct((count, width), F32),
            jax.ShapeDtypeStruct((count, width), BF16),
            jax.ShapeDtypeStruct((1, depth), F32),
        ]
        + [jax.ShapeDtypeStruct((1, width), F32)] * 4
        + terms,
        scratch_shapes=[
            pltpu.VMEM((depth, width), BF16),
            pltpu.VMEM((width, depth), BF16),
            pltpu.VMEM((width, width), BF16),
            pltpu.VMEM((count, depth), BF16),
            pltpu.VMEM((count, width), BF16),
            pltpu.VMEM((count, width), BF16),
            pltpu.VMEM((count, width), BF16),
            pltpu.VMEM((2, width, width), BF16),
            pltpu.SemaphoreType.DMA((3,)),
            pltpu.SemaphoreType.DMA((2,)),
            pltpu.SemaphoreType.DMA((2,)),
        ],
        compiler_params=params(40),
        cost_estimate=cost(2 * count * width * (2 * width + 4 * depth), 40e6),
        name="narrow",
    )


def attend_back_kernel(block, number, terms, place, q_docs, k_docs, q_all, k_all, v_all, o_all, g_all, lse, hidden, *rest):
    dq, dk, dv = rest[:3]
    outs, rest = rest[3 : 3 + terms], rest[3 + terms :]
    bias, k_sum, v_sum, kept, h_kept, stage, sem, sems = rest
    count = LEN // block
    step = pl.program_id(0)

    @pl.when(step == 0)
    def _():
        pltpu.make_async_copy(hidden, h_kept, sem).start()
        for i in range(count):
            sl, reach = slice(i * block, (i + 1) * block), (i + 1) * block
            bias[:reach, sl] = allowed(q_docs[:, sl], k_docs[:reach, :], i * block, (reach, block), 1)

    @pl.when(step < number)
    def _():
        low = lax.broadcasted_iota(jnp.int32, (block, PAIR), 1) < HD
        low_all = lax.broadcasted_iota(jnp.int32, (LEN, PAIR), 1) < HD
        keys = k_all[...]
        key_one = [jnp.where(low_all, keys, jnp.zeros_like(keys)), jnp.where(low_all, jnp.zeros_like(keys), keys)]
        at = pl.ds(pl.multiple_of(lax.rem(step, number) * PAIR, PAIR), PAIR)
        for i in reversed(range(count)):
            sl, reach = slice(i * block, (i + 1) * block), (i + 1) * block
            q, grad = q_all[sl, :], g_all[sl, :]
            turned = (grad.astype(F32) * o_all[sl, :].astype(F32)).T
            parts = []
            for head in range(2):
                lane = low if head == 0 else ~low
                q_one = jnp.where(lane, q, jnp.zeros_like(q))
                g_one = jnp.where(lane, grad, jnp.zeros_like(grad))
                inner = jnp.sum(turned[head * HD : (head + 1) * HD, :], 0, keepdims=True)
                score = dot(k_all[:reach, :], q_one, NT) + bias[:reach, sl]
                prob = jnp.exp(score - lse[0, head : head + 1, sl])
                v_part = dot(prob.astype(BF16), g_one, NN)
                slope = dot(v_all[:reach, :], g_one, NT)
                dscore = (prob * (slope - inner)).astype(BF16)
                k_part = dot(dscore, q_one, NN)
                if i == count - 1 and head == 0:
                    k_sum[...] = k_part
                    v_sum[...] = v_part
                else:
                    k_sum[:reach, :] += k_part
                    v_sum[:reach, :] += v_part
                parts.append(dot(dscore, key_one[head][:reach], TN))
            part = ((parts[0] + parts[1]) * (1.0 / math.sqrt(HD))).astype(BF16)
            dq[sl, :] = part
            kept[0, sl, at] = part
        for index, (ref, total) in enumerate(((dk, k_sum), (dv, v_sum))):
            part = total[...].astype(BF16)
            ref[...] = part
            kept[1 + index, :, at] = part

    wide = stage.shape[3]

    @pl.when(step >= number)
    def _():
        tile = step - number
        slot = lax.rem(tile, 2)

        @pl.when(tile == 0)
        def _():
            finish(h_kept, sem)

        @pl.when(tile >= 2)
        def _():
            finish(stage.at[slot], sems.at[slot])

        for index in range(3):
            part = kept[index, :, pl.ds(pl.multiple_of(tile * wide, wide), wide)]
            stage[slot, index] = dot(h_kept[...], part, TN).astype(BF16)
        for index in range(3):
            for half in range(2):
                send(
                    place,
                    stage.at[slot, index],
                    half * (wide // 2),
                    wide // 2,
                    outs,
                    index * (number * PAIR // 2) + tile * (wide // 2),
                    half,
                    0,
                    sems.at[slot],
                )

        @pl.when(tile == number * PAIR // wide - 1)
        def _():
            finish(stage.at[slot], sems.at[slot])
            if number * PAIR // wide > 1:
                finish(stage.at[1 - slot], sems.at[1 - slot])


def attend_back(place, mixed, attended, grad_o, lse, docs, hidden, by_stage, after=()):
    width = attended.shape[1]
    number = width // PAIR
    block = 256
    wide = 2 * PAIR
    steps = width // wide
    pair = lambda i: jnp.minimum(i, number - 1)
    column = lambda base: pl.BlockSpec((LEN, PAIR), lambda i: (0, base + pair(i)))
    terms = term_shapes(width, 3 * number * PAIR, by_stage)
    return kernel_call(
        functools.partial(attend_back_kernel, block, number, len(terms)),
        [place, docs.reshape(1, LEN), docs.reshape(LEN, 1), mixed, mixed, mixed, attended, grad_o, lse, hidden],
        after,
        grid=(number + steps,),
        in_specs=[
            SMEM,
            whole((1, LEN)),
            whole((LEN, 1)),
            column(0),
            column(number),
            column(2 * number),
            column(0),
            column(0),
            pl.BlockSpec((1, 2, LEN), lambda i: (pair(i), 0, 0)),
            ANY,
        ],
        out_specs=[column(0)] * 3 + [ANY] * len(terms),
        out_shape=[jax.ShapeDtypeStruct((LEN, PAIR * number), BF16)] * 3 + terms,
        scratch_shapes=[
            pltpu.VMEM((LEN, LEN), F32),
            pltpu.VMEM((LEN, PAIR), F32),
            pltpu.VMEM((LEN, PAIR), F32),
            pltpu.VMEM((3, LEN, PAIR * number), BF16),
            pltpu.VMEM((LEN, width), BF16),
            pltpu.VMEM((2, 3, width, wide), BF16),
            pltpu.SemaphoreType.DMA,
            pltpu.SemaphoreType.DMA((2,)),
        ],
        compiler_params=params(20),
        cost_estimate=cost(42e9, 20e6),
        name="attend_back",
    )


def first_back_kernel(place, x, grad_r, gain, *rest):
    parts, pieces, rest = rest[:3], rest[3:-7], rest[-7:]
    grad_x, gain_sum, shift_sum, q_sum, v_sum, weight, sem = rest
    width = x.shape[1]

    @pl.when(pl.program_id(0) == 0)
    def _():
        fetch(place, pieces, 0, 0, 3 * width // 2, weight, sem)()
        for total in (gain_sum, shift_sum, q_sum, v_sum):
            total[...] = jnp.zeros_like(total)

    grad_h = dot(parts[0][...], weight[:, :width], NT)
    for index in (1, 2):
        grad_h += dot(parts[index][...], weight[:, index * width : (index + 1) * width], NT)
    for into, part in ((q_sum, parts[0]), (v_sum, parts[2])):
        into[...] += jnp.sum(part[...].astype(F32), 0, keepdims=True)
    pulled, gains, shifts = norm_back(x[...].astype(F32), gain[...], grad_h)
    grad_x[...] = grad_r[...] + pulled
    gain_sum[...] += gains
    shift_sum[...] += shifts


def first_back(place, x, grad_r, gain, parts, pieces, after=()):
    count, width = x.shape
    block = 256
    return kernel_call(
        first_back_kernel,
        [place, x, grad_r, gain, *parts, *pieces],
        after,
        grid=(count // block,),
        in_specs=[SMEM, rows(block, width), rows(block, width), whole((1, width))]
        + [rows(block, part.shape[1]) for part in parts]
        + [HBM] * len(pieces),
        out_specs=[rows(block, width)] + [whole((1, width))] * 4,
        out_shape=[jax.ShapeDtypeStruct((count, width), F32)] + [jax.ShapeDtypeStruct((1, width), F32)] * 4,
        scratch_shapes=[pltpu.VMEM((width, 3 * width), BF16), pltpu.SemaphoreType.DMA],
        compiler_params=params(56),
        cost_estimate=cost(6 * count * width * width, 16e6),
        name="first_back",
    )


def one_hot(shape, base, span, first):
    lane = lax.broadcasted_iota(jnp.int32, shape, 0)
    element = lax.broadcasted_iota(jnp.int32, shape, 1) + first
    return lane == base + lax.rem(element, span)


def owner(shape, span, first):
    element = lax.broadcasted_iota(jnp.int32, shape, 1) + first
    return lax.broadcasted_iota(jnp.int32, shape, 0) == element // span


def slots(unit, width):
    found, base = [], 0
    for span in (1, 1, 2, 1, 1, 1, 4, 1):
        found += [(base * unit, span * unit, index * width) for index in range(span)]
        base += span
    return found


def unpack_rows(table, out, lanes):
    devices = table.shape[0]
    width = out.shape[1]
    for index, (base, span, first) in enumerate(slots(lanes // 12, width)):
        pick = one_hot((table.shape[1], width), base, span, first).astype(BF16)
        value = dot(table, pick, NN)
        mine = owner((devices, width), span, first)
        out[index : index + 1, :] = jnp.sum(jnp.where(mine, value, 0.0), 0, keepdims=True)


def unpack_kernel(place, *rest):
    pieces, (out, kept, sem) = rest[:4], rest[4:]
    lane = pieces[0].shape[2] - 128
    chip = place[0]
    step = pieces[0].shape[1]
    for group in range(4):
        for spot, relative in enumerate(GROUPS[group]):
            there = pl.ds(pl.multiple_of(lax.bitwise_xor(chip, relative) * step, step), step)
            pltpu.make_async_copy(pieces[group].at[spot, :, pl.ds(lane, 128)], kept.at[there, :], sem).start()
    finish(kept, sem)
    width = out.shape[1]
    devices = width // (step // 2)
    lanes = 12 * step // 2
    parts = []
    for part in range(-(-lanes // 128)):
        shape = (devices, width)
        device = lax.broadcasted_iota(jnp.int32, shape, 0)
        pick = lax.broadcasted_iota(jnp.int32, shape, 1) == device * (step // 2) + part
        parts.append(dot(pick.astype(BF16), kept[...], NN).astype(BF16))
    unpack_rows(jnp.concatenate(parts, 1), out, lanes)


def unpack(place, pieces):
    width = 16 * pieces[0].shape[1]
    return pl.pallas_call(
        unpack_kernel,
        in_specs=[SMEM] + [HBM] * 4,
        out_shape=jax.ShapeDtypeStruct((12, width), F32),
        scratch_shapes=[pltpu.VMEM((width, 128), BF16), pltpu.SemaphoreType.DMA],
        compiler_params=params(16),
        name="unpack",
    )(place, *pieces)


def unpack_whole_kernel(table, out):
    unpack_rows(table[...], out, table.shape[1])


def unpack_whole(table):
    devices, lanes = table.shape
    return pl.pallas_call(
        unpack_whole_kernel,
        out_shape=jax.ShapeDtypeStruct((12, devices * lanes // 12), F32),
        compiler_params=params(32),
        name="unpack_whole",
    )(table)


def pack_kernel(*refs):
    vectors, out = refs[:-1], refs[-1]
    devices, lanes = out.shape
    width = vectors[0].shape[1]
    unit = lanes // 12
    rows_of = [vector[:, first : first + width] for vector in vectors for first in range(0, vector.shape[1], width)]
    total = jnp.zeros((devices, 12 * unit + (-12 * unit) % 128), F32)
    full = total.shape[1]
    at, base = 0, 0
    for span in (1, 1, 2, 1, 1, 1, 4, 1):
        size = span * unit + (-span * unit) % 128
        shape = (size, width)
        spreads = []
        for index in range(span):
            mine = owner((devices, width), span * unit, index * width)
            spreads.append(jnp.where(mine, rows_of[at + index], 0.0))
        at += span
        found = jnp.zeros((devices, size), F32)
        for index, spread in enumerate(spreads):
            pick = one_hot(shape, 0, span * unit, index * width).astype(BF16)
            high = spread.astype(BF16)
            low = (spread - high.astype(F32)).astype(BF16)
            both = dot(jnp.concatenate([high, low], 0), pick, NT)
            found = found + both[:devices] + both[devices:]
        if size < full:
            found = jnp.concatenate([found, jnp.zeros((devices, full - size), F32)], 1)
        total = total + (found if base == 0 else pltpu.roll(found, base * unit, 1))
        base += span
    out[...] = total[:, :lanes]


def pack(vectors, devices):
    lanes = sum(v.shape[1] for v in vectors) // devices
    return pl.pallas_call(
        pack_kernel,
        out_shape=jax.ShapeDtypeStruct((devices, lanes), F32),
        compiler_params=params(16),
        name="pack",
    )(*vectors)


def staged(
    tokens,
    doc_ids,
    d_out,
    ln1_gain,
    ln1_shift,
    qkv_weight,
    qv_bias,
    out_weight,
    out_bias,
    ln2_gain,
    ln2_shift,
    fc_weight,
    fc_bias,
    proj_weight,
    proj_bias,
):
    width = tokens.shape[1]
    depth = fc_weight.shape[1]
    devices = lax.axis_size("dp") * lax.axis_size("fsdp")
    index = lax.axis_index("dp") * lax.axis_size("fsdp") + lax.axis_index("fsdp")
    core = index & 1
    place = jnp.stack([index >> 1, core]).astype(jnp.int32)
    by_stage = (lax.axis_size("dp"), lax.axis_size("fsdp")) == (8, 4)

    smalls = [ln1_gain, ln1_shift, qv_bias, out_bias, ln2_gain, ln2_shift, fc_bias, proj_bias]
    smalls = jnp.concatenate([v.astype(F32).reshape(1, -1) for v in smalls], 1).reshape(-1)
    if by_stage:
        extra = jnp.pad(smalls, (0, -smalls.size % 128)).reshape(-1, 128).astype(BF16)
        extra = jnp.pad(extra, ((0, qkv_weight.shape[0] - extra.shape[0]), (0, 0)))
        first_block = pair_block(qkv_weight, core, extra)
        out_weight, fc_weight, proj_weight = tie([out_weight, fc_weight, proj_weight], first_block)
        first_column = gather_z(first_block)
        wide_block = jnp.concatenate([pair_block(out_weight, core), pair_block(fc_weight, core)], 1)
        proj_block = pair_block(proj_weight, core)
        first_own = gather_xy(first_column)
        (wide_block,) = tie([wide_block], first_column)
        wide_column = gather_z(wide_block, *first_own)
        first_pieces = gather_core(first_own)
        wide_own = gather_xy(wide_column)
        vectors = unpack(place, first_own)
        (proj_block,) = tie([proj_block], wide_column)
    else:
        first_pieces, proj_pieces = [gather_all(qkv_weight)], [gather_all(proj_weight)]
        wide_pieces = [gather_all(w) for w in (out_weight, fc_weight)]
        wide_column = None
        vectors = unpack_whole(gather_all(smalls.reshape(1, -1).astype(BF16)))
    hold = lambda *some: list(some) if by_stage else []
    cores = scatter_core if by_stage else lambda terms: terms[0]
    planes = scatter_xy if by_stage else lambda terms, *after: terms
    columns = scatter_z if by_stage else lambda terms, *after: scatter_all(terms.astype(F32))
    row = lambda at, count=1: vectors[at : at + count].reshape(1, -1)

    mixed, h_one, attended, lse = project_attend(
        place, tokens, row(0), row(1), row(2), row(3), doc_ids, first_pieces, after=hold(wide_column)
    )
    if by_stage:
        proj_column = gather_z(proj_block, lse)
        wide_own = tie(wide_own, lse)
        proj_column, *wide_own = tie([proj_column, *wide_own], proj_column)
        proj_own = gather_xy(proj_column)
        wide_pieces = gather_core(wide_own)
    resid, h_two, slope, active, *proj_terms = widen(
        place, tokens, attended, row(4), row(5), row(6), row(7, 4), d_out, wide_pieces
    )
    if by_stage:
        proj_own = tie(proj_own, resid)
        proj_pieces = gather_core(proj_own)
        proj_terms = tie(proj_terms, *proj_own)
    proj_sums = cores(proj_terms)
    result, grad_r, grad_o, fc_sum, proj_sum, gain_two, shift_two, out_sum, *wide_terms = narrow(
        place,
        resid,
        active,
        slope,
        d_out,
        row(11),
        row(5),
        h_two,
        attended,
        wide_pieces,
        proj_pieces,
        after=hold(*proj_sums),
    )
    if by_stage:
        proj_sums = planes(proj_sums, grad_o)
        wide_terms = tie(wide_terms, *proj_sums)
    wide_sums = cores(wide_terms)
    *grads, qkv_one, qkv_two = (lambda found: found if by_stage else [*found, None])(
        attend_back(
            place, mixed, attended, grad_o, lse, doc_ids, h_one, by_stage, after=hold(*proj_sums, *wide_sums)
        )
    )
    proj_grad = columns(proj_sums, qkv_one)
    wide_sums = planes(wide_sums, qkv_one)
    if by_stage:
        qkv_one, qkv_two = tie([qkv_one, qkv_two], proj_grad, *wide_sums)
    qkv_sums = cores([qkv_one, qkv_two])
    grad_x, gain_one, shift_one, q_sum, v_sum = first_back(
        place, tokens, grad_r, row(0), grads, first_pieces, after=hold(*qkv_sums)
    )
    sums = [gain_one, shift_one, q_sum, v_sum, out_sum, gain_two, shift_two, fc_sum, proj_sum]
    wide_grad = columns(wide_sums, grad_x)
    if by_stage:
        by_x, by_y, by_both = (swap(part, bits) for part, bits in zip(qkv_sums[1:], (X, Y, X | Y)))
        by_x, by_y = tie([by_x, by_y], grad_x)
        sums[0] = tie(sums[:1], wide_grad, by_x, by_y)[0]
        sums = pack(sums, devices)
        qkv_sums = sum_xy(qkv_sums, tie([by_x, by_y, by_both], sums))
    else:
        sums = pack(sums, devices)
    qkv_grad = columns(qkv_sums)

    def sides(grad):
        if by_stage:
            return own_rows(grad, core)
        return jnp.split(grad, 2, 1)

    proj_grad = jnp.concatenate(sides(proj_grad), 1)
    both = sides(wide_grad)
    half = depth // 2
    fc_grad = jnp.concatenate([side[:, :half] for side in both], 1)
    out_grad = jnp.concatenate([side[:, half:] for side in both], 1)
    both = sides(qkv_grad)
    qkv_grad = jnp.concatenate(
        [side[:, lane : lane + PAIR] for lane in range(0, both[0].shape[1], PAIR) for side in both], 1
    )
    own = scatter_small(sums, index) if by_stage else scatter_all(sums).reshape(-1)
    n = width // devices
    spots = (0, n, 2 * n, 4 * n, 5 * n, 6 * n, 7 * n, 11 * n, 12 * n)
    s = [own[a:b] for a, b in zip(spots[:-1], spots[1:])]
    return (
        result,
        grad_x,
        s[0],
        s[1],
        qkv_grad,
        s[2],
        out_grad,
        s[3],
        s[4],
        s[5],
        fc_grad,
        s[6],
        proj_grad,
        s[7],
    )


def solution(mesh):
    every, block = P(AXES), P(AXES, None)
    ins = (block, every, block, every, every, block, every, block, every, every, every, block, every, block, every)
    outs = (block, block, every, every, block, every, block, every, every, every, block, every, block, every)
    return jax.shard_map(staged, mesh=mesh, in_specs=ins, out_specs=outs, check_vma=False)
```

```python
import functools
import math

import jax
import jax.numpy as jnp
from jax import lax
from jax.experimental import pallas as pl
from jax.experimental.pallas import tpu as pltpu
from jax.sharding import PartitionSpec as P

HD = 64
AL = 26
LEN = 1024
PAIR = 2 * HD
EPS = 1e-05
NEG = -1e30
AXES = ("dp", "fsdp")

F32 = jnp.float32
BF16 = jnp.bfloat16
NN = (((1,), (0,)), ((), ()))
NT = (((1,), (1,)), ((), ()))
TN = (((0,), (0,)), ((), ()))
ANY = pl.BlockSpec(memory_space=pl.ANY)
HBM = pl.BlockSpec(memory_space=pltpu.HBM)
SMEM = pl.BlockSpec(memory_space=pltpu.SMEM)

CORE, X, Y, Z0, Z1 = 1, 2, 4, 8, 16
CX, CY, CZ0, CZ1 = 1, 2, 4, 8
GROUPS = tuple(tuple(near | far for far in (0, CZ0, CZ1, CZ0 | CZ1)) for near in (0, CX, CY, CX | CY))


def dot(a, b, dims):
    return lax.dot_general(a, b, dims, preferred_element_type=F32)


def params(size):
    return pltpu.CompilerParams(vmem_limit_bytes=size << 20)


def cost(flops, size):
    return pl.CostEstimate(flops=int(flops), bytes_accessed=int(size), transcendentals=0)


def whole(shape):
    return pl.BlockSpec(shape, lambda *g: (0,) * len(shape))


def rows(block, width):
    return pl.BlockSpec((block, width), lambda i: (i, 0))


def swap(array, bit):
    count = lax.axis_size("dp") * lax.axis_size("fsdp")
    return lax.ppermute(array, AXES, [(i, i ^ bit) for i in range(count)])


def halves(array, core):
    width = array.shape[1] // 2
    low, high = array[:, :width], array[:, width:]
    first = core == 0
    return jnp.where(first, low, high), jnp.where(first, high, low)


def pair_block(array, core, extra=None):
    keep, send = halves(array, core)
    if extra is not None:
        keep, send = jnp.concatenate([keep, extra], 1), jnp.concatenate([send, extra], 1)
    other = swap(send, CORE)
    first = core == 0
    return jnp.concatenate([jnp.where(first, keep, other), jnp.where(first, other, keep)], 0)


def by_z(parts):
    return [swap(part, bits) for part, bits in zip(parts, (Z0, Z1, Z0 | Z1))]


def by_xy(parts):
    return [swap(part, bits) for part, bits in zip(parts, (X, Y, X | Y))]


def gather_core(own):
    return [*own, *(swap(piece, CORE) for piece in own)]


def add(*terms):
    return functools.reduce(lambda a, b: a + b, [t.astype(F32) for t in terms])


def scatter_core(terms):
    mine, other = terms
    got = swap(other, CORE)
    return [add(mine[g], got[g]).astype(BF16) for g in range(4)]


def sum_xy(sums, got):
    return [add(*(part[spot] for part in [sums[0], *got])).astype(BF16) for spot in range(4)]


def tie(arrays, *others):
    if not others:
        return list(arrays)
    return list(lax.optimization_barrier((*arrays, *others))[: len(arrays)])


def meet(*lists):
    found = iter(lax.optimization_barrier(tuple(array for arrays in lists for array in arrays)))
    return [[next(found) for _ in arrays] for arrays in lists]


def kernel_call(kernel, inputs, after, **how):
    return pl.pallas_call(kernel, **how)(*tie(inputs[:1], *after), *inputs[1:])


def own_rows(block, core):
    count = block.shape[0] // 2
    low, high = block[:count], block[count:]
    first = core == 0
    keep = jnp.where(first, low, high)
    got = swap(jnp.where(first, high, low), CORE)
    return jnp.where(first, keep, got), jnp.where(first, got, keep)


def gather_all(array):
    return lax.all_gather(array, AXES, axis=0, tiled=True)


def scatter_all(array):
    return lax.psum_scatter(array, AXES, scatter_dimension=0, tiled=True)


def scatter_small(table, index, bits):
    for bit in bits:
        count = table.shape[0] // 2
        low = (index & bit) == 0
        keep = jnp.where(low, table[:count], table[count:])
        send = jnp.where(low, table[count:], table[:count])
        table = keep + swap(send, bit)
    return table


def fetch(place, pieces, which, lane, width, into, sem):
    if len(pieces) < 8:
        pltpu.make_async_copy(pieces[which], into, sem).start()
        return lambda: pltpu.make_async_copy(into, into, sem).wait()
    chip, core = place[0], place[1]
    step = into.shape[0] // 16
    for side in range(2):
        half = core if side == 0 else 1 - core
        column = pl.ds(pl.multiple_of(half * width, 128), width)
        for group in range(4):
            for spot, relative in enumerate(GROUPS[group]):
                owner = lax.bitwise_xor(chip, relative)
                pltpu.make_async_copy(
                    pieces[4 * side + group].at[spot, :, pl.ds(lane, width)],
                    into.at[pl.ds(pl.multiple_of(owner * step, step), step), column],
                    sem,
                ).start()
    return lambda: pltpu.make_async_copy(into, into, sem).wait()


def normal(v):
    center = v - jnp.mean(v, -1, keepdims=True)
    spread = jnp.mean(center * center, -1, keepdims=True)
    factor = lax.rsqrt(spread + EPS)
    return center * factor, factor


def one_hot(shape, base, span, first):
    lane = lax.broadcasted_iota(jnp.int32, shape, 0)
    element = lax.broadcasted_iota(jnp.int32, (1, shape[1]), 1) + first
    return lane == base + lax.rem(element, span)


def owner(shape, span, first):
    element = lax.broadcasted_iota(jnp.int32, (1, shape[1]), 1) + first
    return lax.broadcasted_iota(jnp.int32, shape, 0) == element // span


def slots(unit, width):
    found, base = [], 0
    for span in (1, 1, 2, 1, 1, 1, 4, 1):
        found += [(base * unit, span * unit, index * width) for index in range(span)]
        base += span
    return found


def unpack_rows(table, out, lanes):
    devices = table.shape[0]
    width = out.shape[1]
    for index, (base, span, first) in enumerate(slots(lanes // 12, width)):
        pick = one_hot((table.shape[1], width), base, span, first).astype(BF16)
        value = dot(table, pick, NN)
        mine = owner((devices, width), span, first)
        out[index : index + 1, :] = jnp.sum(jnp.where(mine, value, 0.0), 0, keepdims=True)


def unpack_blocks(place, pieces, out, kept, sem):
    lane = pieces[0].shape[2] - 128
    chip = place[0]
    step = pieces[0].shape[1]
    for group in range(4):
        for spot, relative in enumerate(GROUPS[group]):
            there = pl.ds(pl.multiple_of(lax.bitwise_xor(chip, relative) * step, step), step)
            pltpu.make_async_copy(pieces[group].at[spot, :, pl.ds(lane, 128)], kept.at[there, :], sem).start()
    finish(kept, sem)
    width = out.shape[1]
    devices = width // (step // 2)
    lanes = 12 * step // 2
    parts = []
    for part in range(-(-lanes // 128)):
        shape = (devices, width)
        device = lax.broadcasted_iota(jnp.int32, shape, 0)
        pick = lax.broadcasted_iota(jnp.int32, shape, 1) == device * (step // 2) + part
        parts.append(dot(pick.astype(BF16), kept[...], NN).astype(BF16))
    unpack_rows(jnp.concatenate(parts, 1), out, lanes)


def allowed(q_doc, k_doc, first, shape, q_dim):
    q_pos = lax.broadcasted_iota(jnp.int32, shape, q_dim) + first
    k_pos = lax.broadcasted_iota(jnp.int32, shape, 1 - q_dim)
    allow = ((k_pos <= q_pos) & (q_doc == k_doc) & (k_doc > 0)) | (k_pos == q_pos)
    return jnp.where(allow, 0.0, NEG)


def project_attend_kernel(steps, block, place, x, q_docs, k_docs, *rest):
    pieces, rest = rest[:-12], rest[-12:]
    mixed, hidden, out, lse, vectors, kept, bias, weight, small, sem, kept_sem, small_sem = rest
    width = x.shape[1]
    size = x.shape[0]
    step = pl.program_id(0)

    @pl.when(step == 0)
    def _():
        wait = fetch(place, pieces, 0, 0, 3 * width // 2, weight, sem)
        if len(pieces) == 8:
            unpack_blocks(place, pieces[:4], vectors, small, small_sem)
        else:
            unpack_rows(pieces[1][...], vectors, pieces[1].shape[1])
        for i in range(LEN // block):
            sl, reach = slice(i * block, (i + 1) * block), (i + 1) * block
            bias[sl, :reach] = allowed(q_docs[sl, :], k_docs[:, :reach], i * block, (block, reach), 0)
        wait()

    @pl.when(step < steps)
    def _():
        unit, _ = normal(x[...].astype(F32))
        h = (unit * vectors[0:1, :] + vectors[1:2, :]).astype(BF16)
        hidden[...] = h
        scale = 1.0 / math.sqrt(HD)
        here = pl.ds(pl.multiple_of(step * size, size), size)
        for part in range(3):
            sl = slice(part * width, (part + 1) * width)
            value = dot(h, weight[:, sl], NN)
            if part == 0:
                value = (value + vectors[2:3, :]).astype(BF16).astype(F32) * scale
            if part == 2:
                value = value + vectors[3:4, :]
            kept[here, sl] = value.astype(BF16)
        pltpu.make_async_copy(kept.at[here, :], mixed.at[here, :], kept_sem).start()

    @pl.when(step >= steps)
    def _():
        lane = (step - steps) * PAIR
        q_at, k_at, v_at = (pl.ds(pl.multiple_of(lane + part * width, PAIR), PAIR) for part in range(3))
        low = lax.broadcasted_iota(jnp.int32, (block, PAIR), 1) < HD
        for i in range(LEN // block):
            sl, reach = slice(i * block, (i + 1) * block), (i + 1) * block
            q = kept[sl, q_at]
            outs, logs = [], []
            for head in range(2):
                q_one = jnp.where(low if head == 0 else ~low, q, jnp.zeros_like(q))
                score = dot(q_one, kept[:reach, k_at], NT) + bias[sl, :reach]
                top = jnp.max(score, -1, keepdims=True)
                expo = jnp.exp(score - top)
                total = jnp.sum(expo, -1, keepdims=True)
                outs.append(dot(expo.astype(BF16), kept[:reach, v_at], NN) / total)
                logs.append(top + jnp.log(total))
            out[sl, :] = jnp.where(low, outs[0], outs[1]).astype(BF16)
            turned = jnp.where(low, logs[0], logs[1]).T
            lse[0, 0:1, sl] = turned[0:1, :]
            lse[0, 1:2, sl] = turned[HD : HD + 1, :]

    @pl.when(step == pl.num_programs(0) - 1)
    def _():
        finish(kept, kept_sem)


def project_attend(place, x, docs, pieces, after=()):
    count, width = x.shape
    size, block = 256, 512
    steps = count // size
    pairs = width // PAIR
    early = lambda i: (jnp.minimum(i, steps - 1), 0)
    late = lambda i: jnp.maximum(i - steps, 0)
    return kernel_call(
        functools.partial(project_attend_kernel, steps, block),
        [place, x, docs.reshape(LEN, 1), docs.reshape(1, LEN), *pieces],
        after,
        grid=(steps + pairs,),
        in_specs=[SMEM, pl.BlockSpec((size, width), early), whole((LEN, 1)), whole((1, LEN))]
        + ([HBM] * 8 if len(pieces) == 8 else [HBM, whole(pieces[1].shape)]),
        out_specs=[
            HBM,
            pl.BlockSpec((size, width), early),
            pl.BlockSpec((LEN, PAIR), lambda i: (0, late(i))),
            pl.BlockSpec((1, 2, LEN), lambda i: (late(i), 0, 0)),
            whole((12, width)),
        ],
        out_shape=[
            jax.ShapeDtypeStruct((count, 3 * width), BF16),
            jax.ShapeDtypeStruct((count, width), BF16),
            jax.ShapeDtypeStruct((count, width), BF16),
            jax.ShapeDtypeStruct((pairs, 2, LEN), F32),
            jax.ShapeDtypeStruct((12, width), F32),
        ],
        scratch_shapes=[
            pltpu.VMEM((count, 3 * width), BF16),
            pltpu.VMEM((LEN, LEN), F32),
            pltpu.VMEM((width, 3 * width), BF16),
            pltpu.VMEM((width, 128), BF16),
            pltpu.SemaphoreType.DMA,
            pltpu.SemaphoreType.DMA,
            pltpu.SemaphoreType.DMA,
        ],
        compiler_params=params(AL),
        cost_estimate=cost(28e9, 20e6),
        name="project_attend",
    )


def norm_back(v, gain, grad):
    unit, factor = normal(v)
    g = grad * gain
    pulled = factor * (g - jnp.mean(g, -1, keepdims=True) - unit * jnp.mean(g * unit, -1, keepdims=True))
    return pulled, jnp.sum(grad * unit, 0, keepdims=True), jnp.sum(grad, 0, keepdims=True)


def send(place, tile, column, width, outs, lane, half, first, sem):
    here = pl.ds(column, width)
    if len(outs) == 1:
        per_half = outs[0].shape[1] // 2
        at = pl.ds(pl.multiple_of(half * per_half + lane, 128), width)
        top = pl.ds(pl.multiple_of(first * (outs[0].shape[0] // 16), 16), tile.shape[0])
        pltpu.make_async_copy(tile.at[:, here], outs[0].at[top, at], sem).start()
        return
    chip, core = place[0], place[1]
    step = outs[0].shape[2]
    at = pl.ds(pl.multiple_of(lane, 128), width)
    for index in range(tile.shape[0] // step):
        relative = lax.bitwise_xor(chip, first + index)
        group, spot = lax.bitwise_and(relative, 3), lax.shift_right_logical(relative, 2)
        source = tile.at[pl.ds(index * step, step), here]
        for own, target in ((True, outs[0]), (False, outs[1])):
            copy = pltpu.make_async_copy(source, target.at[group, spot, :, at], sem)
            pl.when((half == core) == own)(copy.start)


def finish(ref, sem):
    pltpu.make_async_copy(ref, ref, sem).wait()


def term_shapes(tall, wide, by_stage):
    if by_stage:
        return [jax.ShapeDtypeStruct((4, 4, tall // 16, wide // 2), BF16)] * 2
    return [jax.ShapeDtypeStruct((tall, wide), BF16)]


def widen_kernel(steps, terms, place, x, attended, out_bias, gain, shift, fc_bias, cot, *rest):
    count = terms + 15
    pieces, rest = rest[:-count], rest[-count:]
    resid, hidden, slope, active = rest[:4]
    outs, rest = rest[4 : 4 + terms], rest[4 + terms :]
    w_out, w_fc, kept, bent, grad, stage, weight_sems, kept_sem, bent_sem, grad_sem, sems = rest
    size, width = x.shape
    depth = w_fc.shape[1]
    step = pl.program_id(0)
    here = pl.ds(pl.multiple_of(lax.rem(step, steps) * size, size), size)

    @pl.when(step == 0)
    def _():
        wait_out = fetch(place, pieces, 0, 0, width // 2, w_out, weight_sems.at[0])
        wait_fc = fetch(place, pieces, 1, width // 2, depth // 2, w_fc, weight_sems.at[1])
        pltpu.make_async_copy(cot, grad, grad_sem).start()
        wait_out()
        wait_fc()

    @pl.when(step < steps)
    def _():
        r = x[...].astype(F32) + dot(attended[...], w_out[...], NN) + out_bias[...]
        resid[...] = r
        unit, _ = normal(r)
        h = (unit * gain[...] + shift[...]).astype(BF16)
        hidden[...] = h
        c = math.sqrt(2.0 / math.pi)
        for first in range(0, depth, width):
            sl = slice(first, first + width)
            u = dot(h, w_fc[:, sl], NN) + fc_bias[:, sl]
            square = u * u
            t = jnp.tanh(u * (c + (c * 0.044715) * square))
            half = 0.5 * (1.0 + t)
            kept[here, sl] = (u * half).astype(BF16)
            bent[here, sl] = (half + 0.5 * u * (1.0 - t * t) * (c + (3 * c * 0.044715) * square)).astype(BF16)
        pltpu.make_async_copy(kept.at[here, :], active.at[here, :], kept_sem).start()
        pltpu.make_async_copy(bent.at[here, :], slope.at[here, :], bent_sem).start()

    @pl.when(step >= steps)
    def _():
        tile = step - steps
        slot = lax.rem(tile, 2)

        @pl.when(tile == 0)
        def _():
            finish(grad, grad_sem)

        @pl.when(tile >= 2)
        def _():
            finish(stage.at[slot], sems.at[slot])

        tall = stage.shape[1]
        part = kept[:, pl.ds(pl.multiple_of(tile * tall, tall), tall)]
        stage[slot] = dot(part, grad[...], TN).astype(BF16)
        chips = tall * 16 // depth
        for half in range(2):
            send(place, stage.at[slot], half * (width // 2), width // 2, outs, 0, half, tile * chips, sems.at[slot])

        @pl.when(tile == depth // tall - 1)
        def _():
            finish(stage.at[slot], sems.at[slot])
            finish(stage.at[1 - slot], sems.at[1 - slot])
            finish(kept, kept_sem)
            finish(bent, bent_sem)


def widen(place, x, attended, out_bias, gain, shift, fc_bias, cot, pieces, after=()):
    count, width = x.shape
    depth = fc_bias.shape[1]
    size, tall = 256, width
    steps = count // size
    early = lambda i: (jnp.minimum(i, steps - 1), 0)
    block = lambda wide: pl.BlockSpec((size, wide), early)
    terms = term_shapes(depth, width, len(pieces) == 8)
    return kernel_call(
        functools.partial(widen_kernel, steps, len(terms)),
        [place, x, attended, out_bias, gain, shift, fc_bias, cot, *pieces],
        after,
        grid=(steps + depth // tall,),
        in_specs=[SMEM, block(width), block(width)]
        + [whole((1, width))] * 3
        + [whole((1, depth)), ANY]
        + [HBM] * len(pieces),
        out_specs=[block(width), block(width), HBM, HBM] + [ANY] * len(terms),
        out_shape=[
            jax.ShapeDtypeStruct((count, width), F32),
            jax.ShapeDtypeStruct((count, width), BF16),
            jax.ShapeDtypeStruct((count, depth), BF16),
            jax.ShapeDtypeStruct((count, depth), BF16),
        ]
        + terms,
        scratch_shapes=[
            pltpu.VMEM((width, width), BF16),
            pltpu.VMEM((width, depth), BF16),
            pltpu.VMEM((count, depth), BF16),
            pltpu.VMEM((count, depth), BF16),
            pltpu.VMEM((count, width), BF16),
            pltpu.VMEM((2, tall, width), BF16),
            pltpu.SemaphoreType.DMA((2,)),
            pltpu.SemaphoreType.DMA,
            pltpu.SemaphoreType.DMA,
            pltpu.SemaphoreType.DMA,
            pltpu.SemaphoreType.DMA((2,)),
        ],
        compiler_params=params(32),
        cost_estimate=cost(2 * count * width * (width + 2 * depth), 30e6),
        name="widen",
    )


def narrow_kernel(steps, terms, sides, place, resid, active, slope, cot, proj_bias, gain, hidden, attended, *rest):
    count = terms + 19
    pieces, rest = rest[:-count], rest[-count:]
    wide_pieces, proj_pieces = pieces[:sides], pieces[sides:]
    result, grad_r, grad_o, fc_sum, proj_sum, gain_sum, shift_sum, bias_sum = rest[:8]
    outs, rest = rest[8 : 8 + terms], rest[8 + terms :]
    w_proj, w_fc, w_out, du, dt, h_kept, o_kept, stage, weight_sems, kept_sems, sems = rest
    size, width = resid.shape
    depth = active.shape[1]
    step = pl.program_id(0)
    here = pl.ds(pl.multiple_of(lax.rem(step, steps) * size, size), size)

    @pl.when(step == 0)
    def _():
        wait_proj = fetch(place, proj_pieces, 0, 0, width // 2, w_proj, weight_sems.at[0])
        wait_fc = fetch(place, wide_pieces, 1, width // 2, depth // 2, w_fc, weight_sems.at[1])
        wait_out = fetch(place, wide_pieces, 0, 0, width // 2, w_out, weight_sems.at[2])
        pltpu.make_async_copy(hidden, h_kept, kept_sems.at[0]).start()
        pltpu.make_async_copy(attended, o_kept, kept_sems.at[1]).start()
        for total in (fc_sum, proj_sum, gain_sum, shift_sum, bias_sum):
            total[...] = jnp.zeros_like(total)
        wait_proj()
        wait_fc()
        wait_out()

    @pl.when(step < steps)
    def _():
        g = cot[...]
        for first in range(0, depth, width):
            sl = slice(first, first + width)
            part = (dot(g, w_proj[sl, :], NT) * slope[:, sl].astype(F32)).astype(BF16)
            du[here, sl] = part
            fc_sum[:, sl] += jnp.sum(part.astype(F32), 0, keepdims=True)
        r = resid[...]
        result[...] = (r + dot(active[...], w_proj[...], NN) + proj_bias[...]).astype(BF16)
        wide = g.astype(F32)
        proj_sum[...] += jnp.sum(wide, 0, keepdims=True)
        grad_h = dot(du[here, :], w_fc[...], NT)
        pulled, gains, shifts = norm_back(r, gain[...], grad_h)
        total = wide + pulled
        grad_r[...] = total
        low = total.astype(BF16)
        dt[here, :] = low
        gain_sum[...] += gains
        shift_sum[...] += shifts
        bias_sum[...] += jnp.sum(low.astype(F32), 0, keepdims=True)
        grad_o[...] = dot(low, w_out[...], NT).astype(BF16)

    tiles = depth // width

    @pl.when(step >= steps)
    def _():
        tile = step - steps
        slot = lax.rem(tile, 2)

        @pl.when(tile == 0)
        def _():
            finish(h_kept, kept_sems.at[0])
            finish(o_kept, kept_sems.at[1])

        @pl.when(tile >= 2)
        def _():
            finish(stage.at[slot], sems.at[slot])

        @pl.when(tile < tiles)
        def _():
            part = du[:, pl.ds(pl.multiple_of(lax.rem(tile, tiles) * width, width), width)]
            stage[slot] = dot(h_kept[...], part, TN).astype(BF16)
            lane = lax.rem(tile, tiles // 2) * width
            send(place, stage.at[slot], 0, width, outs, lane, tile // (tiles // 2), 0, sems.at[slot])

        @pl.when(tile == tiles)
        def _():
            stage[slot] = dot(o_kept[...], dt[...], TN).astype(BF16)
            for half in range(2):
                send(place, stage.at[slot], half * (width // 2), width // 2, outs, depth // 2, half, 0, sems.at[slot])
            finish(stage.at[slot], sems.at[slot])
            finish(stage.at[1 - slot], sems.at[1 - slot])


def narrow(place, resid, active, slope, cot, proj_bias, gain, hidden, attended, wide_pieces, proj_pieces, after=()):
    count, width = resid.shape
    depth = active.shape[1]
    size = 256
    steps = count // size
    early = lambda i: (jnp.minimum(i, steps - 1), 0)
    block = lambda wide: pl.BlockSpec((size, wide), early)
    pieces = [*wide_pieces, *proj_pieces]
    terms = term_shapes(width, width + depth, len(proj_pieces) == 8)
    return kernel_call(
        functools.partial(narrow_kernel, steps, len(terms), len(wide_pieces)),
        [place, resid, active, slope, cot, proj_bias, gain, hidden, attended, *pieces],
        after,
        grid=(steps + depth // width + 1,),
        in_specs=[SMEM, block(width), block(depth), block(depth), block(width)]
        + [whole((1, width))] * 2
        + [ANY] * 2 + [HBM] * len(pieces),
        out_specs=[block(width)] * 3
        + [whole((1, depth))]
        + [whole((1, width))] * 4
        + [ANY] * len(terms),
        out_shape=[
            jax.ShapeDtypeStruct((count, width), BF16),
            jax.ShapeDtypeStruct((count, width), F32),
            jax.ShapeDtypeStruct((count, width), BF16),
            jax.ShapeDtypeStruct((1, depth), F32),
        ]
        + [jax.ShapeDtypeStruct((1, width), F32)] * 4
        + terms,
        scratch_shapes=[
            pltpu.VMEM((depth, width), BF16),
            pltpu.VMEM((width, depth), BF16),
            pltpu.VMEM((width, width), BF16),
            pltpu.VMEM((count, depth), BF16),
            pltpu.VMEM((count, width), BF16),
            pltpu.VMEM((count, width), BF16),
            pltpu.VMEM((count, width), BF16),
            pltpu.VMEM((2, width, width), BF16),
            pltpu.SemaphoreType.DMA((3,)),
            pltpu.SemaphoreType.DMA((2,)),
            pltpu.SemaphoreType.DMA((2,)),
        ],
        compiler_params=params(40),
        cost_estimate=cost(2 * count * width * (2 * width + 4 * depth), 40e6),
        name="narrow",
    )


def attend_back_kernel(block, number, terms, place, q_docs, k_docs, q_all, k_all, v_all, o_all, g_all, lse, hidden, *rest):
    dq, dk, dv = rest[:3]
    outs, rest = rest[3 : 3 + terms], rest[3 + terms :]
    bias, k_sum, v_sum, kept, h_kept, stage, sem, sems = rest
    count = LEN // block
    step = pl.program_id(0)

    @pl.when(step == 0)
    def _():
        pltpu.make_async_copy(hidden, h_kept, sem).start()
        for i in range(count):
            sl, reach = slice(i * block, (i + 1) * block), (i + 1) * block
            bias[:reach, sl] = allowed(q_docs[:, sl], k_docs[:reach, :], i * block, (reach, block), 1)

    @pl.when(step < number)
    def _():
        low = lax.broadcasted_iota(jnp.int32, (block, PAIR), 1) < HD
        low_all = lax.broadcasted_iota(jnp.int32, (LEN, PAIR), 1) < HD
        keys = k_all[...]
        key_one = [jnp.where(low_all, keys, jnp.zeros_like(keys)), jnp.where(low_all, jnp.zeros_like(keys), keys)]
        at = pl.ds(pl.multiple_of(lax.rem(step, number) * PAIR, PAIR), PAIR)
        for i in reversed(range(count)):
            sl, reach = slice(i * block, (i + 1) * block), (i + 1) * block
            q, grad = q_all[sl, :], g_all[sl, :]
            turned = (grad.astype(F32) * o_all[sl, :].astype(F32)).T
            parts = []
            for head in range(2):
                lane = low if head == 0 else ~low
                q_one = jnp.where(lane, q, jnp.zeros_like(q))
                g_one = jnp.where(lane, grad, jnp.zeros_like(grad))
                inner = jnp.sum(turned[head * HD : (head + 1) * HD, :], 0, keepdims=True)
                score = dot(k_all[:reach, :], q_one, NT) + bias[:reach, sl]
                prob = jnp.exp(score - lse[0, head : head + 1, sl])
                v_part = dot(prob.astype(BF16), g_one, NN)
                slope = dot(v_all[:reach, :], g_one, NT)
                dscore = (prob * (slope - inner)).astype(BF16)
                k_part = dot(dscore, q_one, NN)
                if i == count - 1 and head == 0:
                    k_sum[...] = k_part
                    v_sum[...] = v_part
                else:
                    k_sum[:reach, :] += k_part
                    v_sum[:reach, :] += v_part
                parts.append(dot(dscore, key_one[head][:reach], TN))
            part = ((parts[0] + parts[1]) * (1.0 / math.sqrt(HD))).astype(BF16)
            dq[sl, :] = part
            kept[0, sl, at] = part
        for index, (ref, total) in enumerate(((dk, k_sum), (dv, v_sum))):
            part = total[...].astype(BF16)
            ref[...] = part
            kept[1 + index, :, at] = part

    wide = stage.shape[3]

    @pl.when(step >= number)
    def _():
        tile = step - number
        slot = lax.rem(tile, 2)

        @pl.when(tile == 0)
        def _():
            finish(h_kept, sem)

        @pl.when(tile >= 2)
        def _():
            finish(stage.at[slot], sems.at[slot])

        for index in range(3):
            part = kept[index, :, pl.ds(pl.multiple_of(tile * wide, wide), wide)]
            stage[slot, index] = dot(h_kept[...], part, TN).astype(BF16)
        for index in range(3):
            for half in range(2):
                send(
                    place,
                    stage.at[slot, index],
                    half * (wide // 2),
                    wide // 2,
                    outs,
                    index * (number * PAIR // 2) + tile * (wide // 2),
                    half,
                    0,
                    sems.at[slot],
                )

        @pl.when(tile == number * PAIR // wide - 1)
        def _():
            finish(stage.at[slot], sems.at[slot])
            if number * PAIR // wide > 1:
                finish(stage.at[1 - slot], sems.at[1 - slot])


def attend_back(place, mixed, attended, grad_o, lse, docs, hidden, by_stage, after=()):
    width = attended.shape[1]
    number = width // PAIR
    block = 256
    wide = 2 * PAIR
    steps = width // wide
    pair = lambda i: jnp.minimum(i, number - 1)
    column = lambda base: pl.BlockSpec((LEN, PAIR), lambda i: (0, base + pair(i)))
    terms = term_shapes(width, 3 * number * PAIR, by_stage)
    return kernel_call(
        functools.partial(attend_back_kernel, block, number, len(terms)),
        [place, docs.reshape(1, LEN), docs.reshape(LEN, 1), mixed, mixed, mixed, attended, grad_o, lse, hidden],
        after,
        grid=(number + steps,),
        in_specs=[
            SMEM,
            whole((1, LEN)),
            whole((LEN, 1)),
            column(0),
            column(number),
            column(2 * number),
            column(0),
            column(0),
            pl.BlockSpec((1, 2, LEN), lambda i: (pair(i), 0, 0)),
            ANY,
        ],
        out_specs=[column(0)] * 3 + [ANY] * len(terms),
        out_shape=[jax.ShapeDtypeStruct((LEN, PAIR * number), BF16)] * 3 + terms,
        scratch_shapes=[
            pltpu.VMEM((LEN, LEN), F32),
            pltpu.VMEM((LEN, PAIR), F32),
            pltpu.VMEM((LEN, PAIR), F32),
            pltpu.VMEM((3, LEN, PAIR * number), BF16),
            pltpu.VMEM((LEN, width), BF16),
            pltpu.VMEM((2, 3, width, wide), BF16),
            pltpu.SemaphoreType.DMA,
            pltpu.SemaphoreType.DMA((2,)),
        ],
        compiler_params=params(56),
        cost_estimate=cost(42e9, 20e6),
        name="attend_back",
    )


def first_back_kernel(place, x, grad_r, gain, *rest):
    parts, pieces, rest = rest[:3], rest[3:-4], rest[-4:]
    grad_x, sums, weight, sem = rest
    width = x.shape[1]

    @pl.when(pl.program_id(0) == 0)
    def _():
        fetch(place, pieces, 0, 0, 3 * width // 2, weight, sem)()
        sums[...] = jnp.zeros_like(sums)

    grad_h = dot(parts[0][...], weight[:, :width], NT)
    for index in (1, 2):
        grad_h += dot(parts[index][...], weight[:, index * width : (index + 1) * width], NT)
    for at, part in ((2, parts[0]), (3, parts[2])):
        sums[at : at + 1, :] += jnp.sum(part[...].astype(F32), 0, keepdims=True)
    pulled, gains, shifts = norm_back(x[...].astype(F32), gain[...], grad_h)
    grad_x[...] = grad_r[...] + pulled
    sums[0:1, :] += gains
    sums[1:2, :] += shifts


def first_back(place, x, grad_r, gain, parts, pieces, after=()):
    count, width = x.shape
    block = 256
    return kernel_call(
        first_back_kernel,
        [place, x, grad_r, gain, *parts, *pieces],
        after,
        grid=(count // block,),
        in_specs=[SMEM, rows(block, width), rows(block, width), whole((1, width))]
        + [rows(block, part.shape[1]) for part in parts]
        + [HBM] * len(pieces),
        out_specs=[rows(block, width), whole((4, width))],
        out_shape=[jax.ShapeDtypeStruct((count, width), F32), jax.ShapeDtypeStruct((4, width), F32)],
        scratch_shapes=[pltpu.VMEM((width, 3 * width), BF16), pltpu.SemaphoreType.DMA],
        compiler_params=params(56),
        cost_estimate=cost(6 * count * width * width, 16e6),
        name="first_back",
    )


def pack_kernel(*refs):
    vectors, out = refs[:-1], refs[-1]
    devices, lanes = out.shape
    width = vectors[0].shape[1]
    unit = lanes // 12
    rows_of = [
        vector[row : row + 1, first : first + width]
        for vector in vectors
        for row in range(vector.shape[0])
        for first in range(0, vector.shape[1], width)
    ]
    total = jnp.zeros((devices, 12 * unit + (-12 * unit) % 128), F32)
    full = total.shape[1]
    at, base = 0, 0
    for span in (1, 1, 2, 1, 1, 1, 4, 1):
        size = span * unit + (-span * unit) % 128
        shape = (size, width)
        spreads = []
        for index in range(span):
            mine = owner((devices, width), span * unit, index * width)
            spreads.append(jnp.where(mine, rows_of[at + index], 0.0))
        at += span
        found = jnp.zeros((devices, size), F32)
        for index, spread in enumerate(spreads):
            pick = one_hot(shape, 0, span * unit, index * width).astype(BF16)
            high = spread.astype(BF16)
            low = (spread - high.astype(F32)).astype(BF16)
            both = dot(jnp.concatenate([high, low], 0), pick, NT)
            found = found + both[:devices] + both[devices:]
        if size < full:
            found = jnp.concatenate([found, jnp.zeros((devices, full - size), F32)], 1)
        total = total + (found if base == 0 else pltpu.roll(found, base * unit, 1))
        base += span
    out[...] = total[:, :lanes]


def pack(vectors, devices):
    lanes = sum(v.size for v in vectors) // devices
    return pl.pallas_call(
        pack_kernel,
        out_shape=jax.ShapeDtypeStruct((devices, lanes), F32),
        compiler_params=params(16),
        name="pack",
    )(*vectors)


def staged(
    tokens,
    doc_ids,
    d_out,
    ln1_gain,
    ln1_shift,
    qkv_weight,
    qv_bias,
    out_weight,
    out_bias,
    ln2_gain,
    ln2_shift,
    fc_weight,
    fc_bias,
    proj_weight,
    proj_bias,
):
    width = tokens.shape[1]
    depth = fc_weight.shape[1]
    devices = lax.axis_size("dp") * lax.axis_size("fsdp")
    index = lax.axis_index("dp") * lax.axis_size("fsdp") + lax.axis_index("fsdp")
    core = index & 1
    place = jnp.stack([index >> 1, core]).astype(jnp.int32)
    by_stage = (lax.axis_size("dp"), lax.axis_size("fsdp")) == (8, 4)

    smalls = [ln1_gain, ln1_shift, qv_bias, out_bias, ln2_gain, ln2_shift, fc_bias, proj_bias]
    smalls = jnp.concatenate([v.astype(F32).reshape(1, -1) for v in smalls], 1).reshape(-1)
    if by_stage:
        extra = jnp.pad(smalls, (0, -smalls.size % 128)).reshape(-1, 128).astype(BF16)
        extra = jnp.pad(extra, ((0, qkv_weight.shape[0] - extra.shape[0]), (0, 0)))
        first_block = pair_block(qkv_weight, core, extra)
        out_weight, fc_weight, proj_weight = tie([out_weight, fc_weight, proj_weight], first_block)
        wide_block = jnp.concatenate([pair_block(out_weight, core), pair_block(fc_weight, core)], 1)
        proj_block = pair_block(proj_weight, core)
        first_column = jnp.stack([first_block] + by_z([first_block] * 3))
        (wide_block,) = tie([wide_block], first_column)
        first_got, wide_got, (proj_near,) = meet(
            by_xy([first_column] * 3), by_z([wide_block] * 3), [swap(tie([proj_block], first_column)[0], Z0)]
        )
        first_pieces = gather_core([first_column, *first_got])
        wide_column = jnp.stack([wide_block] + wide_got)
        wide_got = by_xy([wide_column] * 3)
        (proj_block,) = tie([proj_block], wide_column)
        proj_got = [swap(proj_block, bits) for bits in (Z1, Z0 | Z1)]
    else:
        first_pieces, proj_pieces = [gather_all(qkv_weight)], [gather_all(proj_weight)]
        wide_pieces = [gather_all(w) for w in (out_weight, fc_weight)]
        wide_column = None
        first_pieces = first_pieces + [gather_all(smalls.reshape(1, -1).astype(BF16))]
    hold = lambda *some: list(some) if by_stage else []
    row = lambda at, count=1: vectors[at : at + count].reshape(1, -1)

    found = project_attend(place, tokens, doc_ids, first_pieces, after=hold(wide_column) if by_stage else [])
    if by_stage:
        found, wide_got, proj_got = meet(found, wide_got, proj_got)
        proj_column = jnp.stack([proj_block, proj_near] + proj_got)
        proj_got = by_xy([proj_column] * 3)
        wide_pieces = gather_core([wide_column, *wide_got])
    mixed, h_one, attended, lse, vectors = found

    found = widen(
        place,
        tokens,
        attended,
        row(4),
        row(5),
        row(6),
        row(7, 4),
        d_out,
        wide_pieces,
        after=hold(proj_column) if by_stage else [],
    )
    if by_stage:
        found, proj_got = meet(found, proj_got)
        proj_pieces = gather_core([proj_column, *proj_got])
        proj_sums = scatter_core(found[4:])
        proj_got = by_xy(proj_sums[1:])
    resid, h_two, slope, active, *proj_terms = found

    found = narrow(
        place,
        resid,
        active,
        slope,
        d_out,
        row(11),
        row(5),
        h_two,
        attended,
        wide_pieces,
        proj_pieces,
        after=hold(*proj_sums) if by_stage else [],
    )
    if by_stage:
        found, proj_got = meet(found, proj_got)
        proj_sums = sum_xy(proj_sums, proj_got)
        proj_got = by_z(proj_sums[1:])
        wide_sums = scatter_core(found[8:])
        wide_got = by_xy(wide_sums[1:])
    result, grad_r, grad_o, fc_sum, proj_sum, gain_two, shift_two, out_sum, *wide_terms = found

    found = attend_back(
        place,
        mixed,
        attended,
        grad_o,
        lse,
        doc_ids,
        h_one,
        by_stage,
        after=hold(*proj_sums, *wide_sums) if by_stage else [],
    )
    if by_stage:
        found, wide_got, proj_got = meet(found, wide_got, proj_got)
        wide_sums = sum_xy(wide_sums, wide_got)
        wide_got = by_z(wide_sums[1:])
        qkv_sums = scatter_core(found[3:])
        qkv_got = by_xy(qkv_sums[1:])
    *grads, qkv_terms = found[:4]

    found = first_back(
        place,
        tokens,
        grad_r,
        row(0),
        grads,
        first_pieces[:8] if by_stage else first_pieces[:1],
        after=hold(*qkv_sums, *wide_sums) if by_stage else [],
    )
    if by_stage:
        found, wide_got, qkv_got = meet(found, wide_got, qkv_got)
    grad_x, first_sums = found
    sums = [first_sums, out_sum, gain_two, shift_two, fc_sum, proj_sum]
    table = pack(sums, devices)
    if by_stage:
        qkv_sums = sum_xy(qkv_sums, qkv_got)
        table = scatter_small(tie([table], *qkv_sums)[0], index, (Z1, Z0, Y, X))
        (table,), qkv_got = meet([table], by_z(qkv_sums[1:]))
        proj_grad, wide_grad = add(proj_sums[0], *proj_got), add(wide_sums[0], *wide_got)
    else:
        own = scatter_all(table).reshape(-1)
        proj_grad, wide_grad, qkv_grad = (
            scatter_all(terms.astype(F32)) for terms in (proj_terms[0], wide_terms[0], qkv_terms)
        )

    def sides(grad):
        if by_stage:
            return own_rows(grad, core)
        return jnp.split(grad, 2, 1)

    proj_grad = jnp.concatenate(sides(proj_grad), 1)
    both = sides(wide_grad)
    half = depth // 2
    fc_grad = jnp.concatenate([side[:, :half] for side in both], 1)
    out_grad = jnp.concatenate([side[:, half:] for side in both], 1)
    if by_stage:
        own = scatter_small(table, index, (CORE,)).reshape(-1)
        qkv_grad = add(qkv_sums[0], *qkv_got)
    both = sides(qkv_grad)
    qkv_grad = jnp.concatenate(
        [side[:, lane : lane + PAIR] for lane in range(0, both[0].shape[1], PAIR) for side in both], 1
    )
    n = width // devices
    spots = (0, n, 2 * n, 4 * n, 5 * n, 6 * n, 7 * n, 11 * n, 12 * n)
    s = [own[a:b] for a, b in zip(spots[:-1], spots[1:])]
    return (
        result,
        grad_x,
        s[0],
        s[1],
        qkv_grad,
        s[2],
        out_grad,
        s[3],
        s[4],
        s[5],
        fc_grad,
        s[6],
        proj_grad,
        s[7],
    )


def solution(mesh):
    every, block = P(AXES), P(AXES, None)
    ins = (block, every, block, every, every, block, every, block, every, every, every, block, every, block, every)
    outs = (block, block, every, every, block, every, block, every, every, every, block, every, block, every)
    return jax.shard_map(staged, mesh=mesh, in_specs=ins, out_specs=outs, check_vma=False)
```

```python
import functools
import math

import jax
import jax.numpy as jnp
from jax import lax
from jax.experimental import pallas as pl
from jax.experimental.pallas import tpu as pltpu
from jax.sharding import PartitionSpec as P

HD = 64
LEN = 1024
PAIR = 2 * HD
EPS = 1e-05
NEG = -1e30
AXES = ("dp", "fsdp")

F32 = jnp.float32
BF16 = jnp.bfloat16
NN = (((1,), (0,)), ((), ()))
NT = (((1,), (1,)), ((), ()))
TN = (((0,), (0,)), ((), ()))
ANY = pl.BlockSpec(memory_space=pl.ANY)
HBM = pl.BlockSpec(memory_space=pltpu.HBM)
SMEM = pl.BlockSpec(memory_space=pltpu.SMEM)

CORE, X, Y, Z0, Z1 = 1, 2, 4, 8, 16
CX, CY, CZ0, CZ1 = 1, 2, 4, 8
GROUPS = tuple(tuple(near | far for far in (0, CZ0, CZ1, CZ0 | CZ1)) for near in (0, CX, CY, CX | CY))


def dot(a, b, dims):
    return lax.dot_general(a, b, dims, preferred_element_type=F32)


def params(size):
    return pltpu.CompilerParams(vmem_limit_bytes=size << 20)


def cost(flops, size):
    return pl.CostEstimate(flops=int(flops), bytes_accessed=int(size), transcendentals=0)


def whole(shape):
    return pl.BlockSpec(shape, lambda *g: (0,) * len(shape))


def rows(block, width):
    return pl.BlockSpec((block, width), lambda i: (i, 0))


def swap(array, bit):
    count = lax.axis_size("dp") * lax.axis_size("fsdp")
    return lax.ppermute(array, AXES, [(i, i ^ bit) for i in range(count)])


def halves(array, core):
    width = array.shape[1] // 2
    low, high = array[:, :width], array[:, width:]
    first = core == 0
    return jnp.where(first, low, high), jnp.where(first, high, low)


def pair_block(array, core, extra=None):
    keep, send = halves(array, core)
    if extra is not None:
        keep, send = jnp.concatenate([keep, extra], 1), jnp.concatenate([send, extra], 1)
    other = swap(send, CORE)
    first = core == 0
    return jnp.concatenate([jnp.where(first, keep, other), jnp.where(first, other, keep)], 0)


def by_z(parts):
    return [swap(part, bits) for part, bits in zip(parts, (Z0, Z1, Z0 | Z1))]


def by_xy(parts):
    return [swap(part, bits) for part, bits in zip(parts, (X, Y, X | Y))]


def gather_core(own):
    return [*own, *(swap(piece, CORE) for piece in own)]


def add(*terms):
    return functools.reduce(lambda a, b: a + b, [t.astype(F32) for t in terms])


def scatter_core(terms):
    mine, other = terms
    got = swap(other, CORE)
    return [add(mine[g], got[g]).astype(BF16) for g in range(4)]


def sum_xy(sums, got):
    return [add(*(part[spot] for part in [sums[0], *got])).astype(BF16) for spot in range(4)]


def tie(arrays, *others):
    if not others:
        return list(arrays)
    return list(lax.optimization_barrier((*arrays, *others))[: len(arrays)])


def meet(*lists):
    found = iter(lax.optimization_barrier(tuple(array for arrays in lists for array in arrays)))
    return [[next(found) for _ in arrays] for arrays in lists]


def kernel_call(kernel, inputs, after, **how):
    return pl.pallas_call(kernel, **how)(*tie(inputs[:1], *after), *inputs[1:])


def own_rows(block, core):
    count = block.shape[0] // 2
    low, high = block[:count], block[count:]
    first = core == 0
    keep = jnp.where(first, low, high)
    got = swap(jnp.where(first, high, low), CORE)
    return jnp.where(first, keep, got), jnp.where(first, got, keep)


def gather_all(array):
    return lax.all_gather(array, AXES, axis=0, tiled=True)


def scatter_all(array):
    return lax.psum_scatter(array, AXES, scatter_dimension=0, tiled=True)


def scatter_small(table, index, bits):
    for bit in bits:
        count = table.shape[0] // 2
        low = (index & bit) == 0
        keep = jnp.where(low, table[:count], table[count:])
        send = jnp.where(low, table[count:], table[:count])
        table = keep + swap(send, bit)
    return table


def fetch(place, pieces, which, lane, width, into, sem):
    if len(pieces) < 8:
        pltpu.make_async_copy(pieces[which], into, sem).start()
        return lambda: pltpu.make_async_copy(into, into, sem).wait()
    chip, core = place[0], place[1]
    step = into.shape[0] // 16
    for side in range(2):
        half = core if side == 0 else 1 - core
        column = pl.ds(pl.multiple_of(half * width, 128), width)
        for group in range(4):
            for spot, relative in enumerate(GROUPS[group]):
                owner = lax.bitwise_xor(chip, relative)
                pltpu.make_async_copy(
                    pieces[4 * side + group].at[spot, :, pl.ds(lane, width)],
                    into.at[pl.ds(pl.multiple_of(owner * step, step), step), column],
                    sem,
                ).start()
    return lambda: pltpu.make_async_copy(into, into, sem).wait()


def normal(v):
    center = v - jnp.mean(v, -1, keepdims=True)
    spread = jnp.mean(center * center, -1, keepdims=True)
    factor = lax.rsqrt(spread + EPS)
    return center * factor, factor


def one_hot(shape, base, span, first):
    lane = lax.broadcasted_iota(jnp.int32, shape, 0)
    element = lax.broadcasted_iota(jnp.int32, (1, shape[1]), 1) + first
    return lane == base + lax.rem(element, span)


def owner(shape, span, first):
    element = lax.broadcasted_iota(jnp.int32, (1, shape[1]), 1) + first
    return lax.broadcasted_iota(jnp.int32, shape, 0) == element // span


def unpack_rows(table, out, lanes):
    devices, full = table.shape
    width = out.shape[1]
    unit = lanes // 12
    wide = table.astype(F32)
    spans = (1, 1, 2, 1, 1, 1, 4, 1)
    for span in (1, 2, 4):
        starts = [sum(spans[:i]) for i, one in enumerate(spans) if one == span]
        parts = [
            (wide if start == 0 else pltpu.roll(wide, full - start * unit, 1))[:, :128].astype(BF16) for start in starts
        ]
        pick = one_hot((128, width), 0, span * unit, 0).astype(BF16)
        values = dot(jnp.concatenate(parts, 0), pick, NN)
        for index, start in enumerate(starts):
            value = values[index * devices : (index + 1) * devices]
            for row in range(span):
                mine = owner((devices, width), span * unit, row * width)
                out[start + row : start + row + 1, :] = jnp.sum(jnp.where(mine, value, 0.0), 0, keepdims=True)


def unpack_blocks(place, pieces, out, kept, sem):
    lane = pieces[0].shape[2] - 128
    chip = place[0]
    step = pieces[0].shape[1]
    for group in range(4):
        for spot, relative in enumerate(GROUPS[group]):
            there = pl.ds(pl.multiple_of(lax.bitwise_xor(chip, relative) * step, step), step)
            pltpu.make_async_copy(pieces[group].at[spot, :, pl.ds(lane, 128)], kept.at[there, :], sem).start()
    finish(kept, sem)
    width = out.shape[1]
    devices = width // (step // 2)
    lanes = 12 * step // 2
    parts = []
    for part in range(-(-lanes // 128)):
        shape = (devices, width)
        device = lax.broadcasted_iota(jnp.int32, shape, 0)
        pick = lax.broadcasted_iota(jnp.int32, shape, 1) == device * (step // 2) + part
        parts.append(dot(pick.astype(BF16), kept[...], NN).astype(BF16))
    unpack_rows(jnp.concatenate(parts, 1), out, lanes)


def allowed(q_doc, k_doc, first, shape, q_dim):
    q_pos = lax.broadcasted_iota(jnp.int32, shape, q_dim) + first
    k_pos = lax.broadcasted_iota(jnp.int32, shape, 1 - q_dim)
    allow = ((k_pos <= q_pos) & (q_doc == k_doc) & (k_doc > 0)) | (k_pos == q_pos)
    return jnp.where(allow, 0.0, NEG)


def project_attend_kernel(steps, block, place, x, q_docs, k_docs, *rest):
    pieces, rest = rest[:-12], rest[-12:]
    mixed, hidden, out, lse, vectors, kept, bias, weight, small, sem, kept_sem, small_sem = rest
    width = x.shape[1]
    size = x.shape[0]
    step = pl.program_id(0)

    @pl.when(step == 0)
    def _():
        wait = fetch(place, pieces, 0, 0, 3 * width // 2, weight, sem)
        if len(pieces) == 8:
            unpack_blocks(place, pieces[:4], vectors, small, small_sem)
        else:
            unpack_rows(pieces[1][...], vectors, 12 * vectors.shape[1] // pieces[1].shape[0])
        for i in range(LEN // block):
            sl, reach = slice(i * block, (i + 1) * block), (i + 1) * block
            bias[sl, :reach] = allowed(q_docs[sl, :], k_docs[:, :reach], i * block, (block, reach), 0)
        wait()

    @pl.when(step < steps)
    def _():
        unit, _ = normal(x[...].astype(F32))
        h = (unit * vectors[0:1, :] + vectors[1:2, :]).astype(BF16)
        hidden[...] = h
        scale = 1.0 / math.sqrt(HD)
        here = pl.ds(pl.multiple_of(step * size, size), size)
        for part in range(3):
            sl = slice(part * width, (part + 1) * width)
            value = dot(h, weight[:, sl], NN)
            if part == 0:
                value = (value + vectors[2:3, :]).astype(BF16).astype(F32) * scale
            if part == 2:
                value = value + vectors[3:4, :]
            kept[here, sl] = value.astype(BF16)
        pltpu.make_async_copy(kept.at[here, :], mixed.at[here, :], kept_sem).start()

    @pl.when(step >= steps)
    def _():
        lane = (step - steps) * PAIR
        q_at, k_at, v_at = (pl.ds(pl.multiple_of(lane + part * width, PAIR), PAIR) for part in range(3))
        low = lax.broadcasted_iota(jnp.int32, (block, PAIR), 1) < HD
        for i in range(LEN // block):
            sl, reach = slice(i * block, (i + 1) * block), (i + 1) * block
            q = kept[sl, q_at]
            outs, logs = [], []
            for head in range(2):
                q_one = jnp.where(low if head == 0 else ~low, q, jnp.zeros_like(q))
                score = dot(q_one, kept[:reach, k_at], NT) + bias[sl, :reach]
                top = jnp.max(score, -1, keepdims=True)
                expo = jnp.exp(score - top)
                total = jnp.sum(expo, -1, keepdims=True)
                outs.append(dot(expo.astype(BF16), kept[:reach, v_at], NN) / total)
                logs.append(top + jnp.log(total))
            out[sl, :] = jnp.where(low, outs[0], outs[1]).astype(BF16)
            turned = jnp.where(low, logs[0], logs[1]).T
            lse[0, 0:1, sl] = turned[0:1, :]
            lse[0, 1:2, sl] = turned[HD : HD + 1, :]

    @pl.when(step == pl.num_programs(0) - 1)
    def _():
        finish(kept, kept_sem)


def project_attend(place, x, docs, pieces, after=()):
    count, width = x.shape
    size, block = 256, 512
    steps = count // size
    pairs = width // PAIR
    early = lambda i: (jnp.minimum(i, steps - 1), 0)
    late = lambda i: jnp.maximum(i - steps, 0)
    return kernel_call(
        functools.partial(project_attend_kernel, steps, block),
        [place, x, docs.reshape(LEN, 1), docs.reshape(1, LEN), *pieces],
        after,
        grid=(steps + pairs,),
        in_specs=[SMEM, pl.BlockSpec((size, width), early), whole((LEN, 1)), whole((1, LEN))]
        + ([HBM] * 8 if len(pieces) == 8 else [HBM, whole(pieces[1].shape)]),
        out_specs=[
            HBM,
            pl.BlockSpec((size, width), early),
            pl.BlockSpec((LEN, PAIR), lambda i: (0, late(i))),
            pl.BlockSpec((1, 2, LEN), lambda i: (late(i), 0, 0)),
            whole((12, width)),
        ],
        out_shape=[
            pltpu.HBM((count, 3 * width), BF16),
            pltpu.HBM((count, width), BF16),
            jax.ShapeDtypeStruct((count, width), BF16),
            jax.ShapeDtypeStruct((pairs, 2, LEN), F32),
            jax.ShapeDtypeStruct((12, width), F32),
        ],
        scratch_shapes=[
            pltpu.VMEM((count, 3 * width), BF16),
            pltpu.VMEM((LEN, LEN), F32),
            pltpu.VMEM((width, 3 * width), BF16),
            pltpu.VMEM((width, 128), BF16),
            pltpu.SemaphoreType.DMA,
            pltpu.SemaphoreType.DMA,
            pltpu.SemaphoreType.DMA,
        ],
        compiler_params=params(26),
        cost_estimate=cost(28e9, 20e6),
        name="project_attend",
    )


def norm_back(v, gain, grad):
    unit, factor = normal(v)
    g = grad * gain
    pulled = factor * (g - jnp.mean(g, -1, keepdims=True) - unit * jnp.mean(g * unit, -1, keepdims=True))
    return pulled, jnp.sum(grad * unit, 0, keepdims=True), jnp.sum(grad, 0, keepdims=True)


def send(place, tile, column, width, outs, lane, half, first, sem):
    here = pl.ds(column, width)
    if len(outs) == 1:
        per_half = outs[0].shape[1] // 2
        at = pl.ds(pl.multiple_of(half * per_half + lane, 128), width)
        top = pl.ds(pl.multiple_of(first * (outs[0].shape[0] // 16), 16), tile.shape[0])
        pltpu.make_async_copy(tile.at[:, here], outs[0].at[top, at], sem).start()
        return
    chip, core = place[0], place[1]
    step = outs[0].shape[2]
    at = pl.ds(pl.multiple_of(lane, 128), width)
    for index in range(tile.shape[0] // step):
        relative = lax.bitwise_xor(chip, first + index)
        group, spot = lax.bitwise_and(relative, 3), lax.shift_right_logical(relative, 2)
        source = tile.at[pl.ds(index * step, step), here]
        for own, target in ((True, outs[0]), (False, outs[1])):
            copy = pltpu.make_async_copy(source, target.at[group, spot, :, at], sem)
            pl.when((half == core) == own)(copy.start)


def finish(ref, sem):
    pltpu.make_async_copy(ref, ref, sem).wait()


def term_shapes(tall, wide, by_stage):
    if by_stage:
        return [jax.ShapeDtypeStruct((4, 4, tall // 16, wide // 2), BF16)] * 2
    return [jax.ShapeDtypeStruct((tall, wide), BF16)]


def widen_kernel(steps, terms, place, x, attended, out_bias, gain, shift, fc_bias, cot, *rest):
    count = terms + 15
    pieces, rest = rest[:-count], rest[-count:]
    resid, hidden, slope, active = rest[:4]
    outs, rest = rest[4 : 4 + terms], rest[4 + terms :]
    w_out, w_fc, kept, bent, grad, stage, weight_sems, kept_sem, bent_sem, grad_sem, sems = rest
    size, width = x.shape
    depth = w_fc.shape[1]
    step = pl.program_id(0)
    here = pl.ds(pl.multiple_of(lax.rem(step, steps) * size, size), size)

    @pl.when(step == 0)
    def _():
        wait_out = fetch(place, pieces, 0, 0, width // 2, w_out, weight_sems.at[0])
        wait_fc = fetch(place, pieces, 1, width // 2, depth // 2, w_fc, weight_sems.at[1])
        pltpu.make_async_copy(cot, grad, grad_sem).start()
        wait_out()
        wait_fc()

    @pl.when(step < steps)
    def _():
        r = x[...].astype(F32) + dot(attended[...], w_out[...], NN) + out_bias[...]
        resid[...] = r
        unit, _ = normal(r)
        h = (unit * gain[...] + shift[...]).astype(BF16)
        hidden[...] = h
        c = math.sqrt(2.0 / math.pi)
        for first in range(0, depth, width):
            sl = slice(first, first + width)
            u = dot(h, w_fc[:, sl], NN) + fc_bias[:, sl]
            bend = (c * 0.044715) * (u * u) + c
            half = 0.5 * jnp.tanh(u * bend) + 0.5
            value = u * half
            kept[here, sl] = value.astype(BF16)
            bent[here, sl] = (half + value * (1.0 - half) * (6.0 * bend - 4.0 * c)).astype(BF16)
        pltpu.make_async_copy(kept.at[here, :], active.at[here, :], kept_sem).start()
        pltpu.make_async_copy(bent.at[here, :], slope.at[here, :], bent_sem).start()

    @pl.when(step >= steps)
    def _():
        tile = step - steps
        slot = lax.rem(tile, 2)

        @pl.when(tile == 0)
        def _():
            finish(grad, grad_sem)

        @pl.when(tile >= 2)
        def _():
            finish(stage.at[slot], sems.at[slot])

        tall = stage.shape[1]
        part = kept[:, pl.ds(pl.multiple_of(tile * tall, tall), tall)]
        stage[slot] = dot(part, grad[...], TN).astype(BF16)
        chips = tall * 16 // depth
        for half in range(2):
            send(place, stage.at[slot], half * (width // 2), width // 2, outs, 0, half, tile * chips, sems.at[slot])

        @pl.when(tile == depth // tall - 1)
        def _():
            finish(stage.at[slot], sems.at[slot])
            finish(stage.at[1 - slot], sems.at[1 - slot])
            finish(kept, kept_sem)
            finish(bent, bent_sem)


def widen(place, x, attended, out_bias, gain, shift, fc_bias, cot, pieces, after=()):
    count, width = x.shape
    depth = fc_bias.shape[1]
    size, tall = 256, width
    steps = count // size
    early = lambda i: (jnp.minimum(i, steps - 1), 0)
    block = lambda wide: pl.BlockSpec((size, wide), early)
    terms = term_shapes(depth, width, len(pieces) == 8)
    return kernel_call(
        functools.partial(widen_kernel, steps, len(terms)),
        [place, x, attended, out_bias, gain, shift, fc_bias, cot, *pieces],
        after,
        grid=(steps + depth // tall,),
        in_specs=[SMEM, block(width), block(width)]
        + [whole((1, width))] * 3
        + [whole((1, depth)), ANY]
        + [HBM] * len(pieces),
        out_specs=[block(width), block(width), HBM, HBM] + [ANY] * len(terms),
        out_shape=[
            pltpu.HBM((count, width), F32),
            jax.ShapeDtypeStruct((count, width), BF16),
            pltpu.HBM((count, depth), BF16),
            pltpu.HBM((count, depth), BF16),
        ]
        + terms,
        scratch_shapes=[
            pltpu.VMEM((width, width), BF16),
            pltpu.VMEM((width, depth), BF16),
            pltpu.VMEM((count, depth), BF16),
            pltpu.VMEM((count, depth), BF16),
            pltpu.VMEM((count, width), BF16),
            pltpu.VMEM((2, tall, width), BF16),
            pltpu.SemaphoreType.DMA((2,)),
            pltpu.SemaphoreType.DMA,
            pltpu.SemaphoreType.DMA,
            pltpu.SemaphoreType.DMA,
            pltpu.SemaphoreType.DMA((2,)),
        ],
        compiler_params=params(32),
        cost_estimate=cost(2 * count * width * (width + 2 * depth), 30e6),
        name="widen",
    )


def narrow_kernel(steps, terms, sides, place, resid, active, slope, cot, proj_bias, gain, hidden, attended, *rest):
    count = terms + 19
    pieces, rest = rest[:-count], rest[-count:]
    wide_pieces, proj_pieces = pieces[:sides], pieces[sides:]
    result, grad_r, grad_o, fc_sum, proj_sum, gain_sum, shift_sum, bias_sum = rest[:8]
    outs, rest = rest[8 : 8 + terms], rest[8 + terms :]
    w_proj, w_fc, w_out, du, dt, h_kept, o_kept, stage, weight_sems, kept_sems, sems = rest
    size, width = resid.shape
    depth = active.shape[1]
    step = pl.program_id(0)
    here = pl.ds(pl.multiple_of(lax.rem(step, steps) * size, size), size)

    @pl.when(step == 0)
    def _():
        wait_proj = fetch(place, proj_pieces, 0, 0, width // 2, w_proj, weight_sems.at[0])
        wait_fc = fetch(place, wide_pieces, 1, width // 2, depth // 2, w_fc, weight_sems.at[1])
        wait_out = fetch(place, wide_pieces, 0, 0, width // 2, w_out, weight_sems.at[2])
        pltpu.make_async_copy(hidden, h_kept, kept_sems.at[0]).start()
        pltpu.make_async_copy(attended, o_kept, kept_sems.at[1]).start()
        for total in (fc_sum, proj_sum, gain_sum, shift_sum, bias_sum):
            total[...] = jnp.zeros_like(total)
        wait_proj()
        wait_fc()
        wait_out()

    @pl.when(step < steps)
    def _():
        g = cot[...]
        for first in range(0, depth, width):
            sl = slice(first, first + width)
            part = (dot(g, w_proj[sl, :], NT) * slope[:, sl].astype(F32)).astype(BF16)
            du[here, sl] = part
            fc_sum[:, sl] += jnp.sum(part.astype(F32), 0, keepdims=True)
        r = resid[...]
        result[...] = (r + dot(active[...], w_proj[...], NN) + proj_bias[...]).astype(BF16)
        wide = g.astype(F32)
        proj_sum[...] += jnp.sum(wide, 0, keepdims=True)
        grad_h = dot(du[here, :], w_fc[...], NT)
        pulled, gains, shifts = norm_back(r, gain[...], grad_h)
        total = wide + pulled
        grad_r[...] = total
        low = total.astype(BF16)
        dt[here, :] = low
        gain_sum[...] += gains
        shift_sum[...] += shifts
        bias_sum[...] += jnp.sum(low.astype(F32), 0, keepdims=True)
        grad_o[...] = dot(low, w_out[...], NT).astype(BF16)

    tiles = depth // width

    @pl.when(step >= steps)
    def _():
        tile = step - steps
        slot = lax.rem(tile, 2)

        @pl.when(tile == 0)
        def _():
            finish(h_kept, kept_sems.at[0])
            finish(o_kept, kept_sems.at[1])

        @pl.when(tile >= 2)
        def _():
            finish(stage.at[slot], sems.at[slot])

        @pl.when(tile < tiles)
        def _():
            part = du[:, pl.ds(pl.multiple_of(lax.rem(tile, tiles) * width, width), width)]
            stage[slot] = dot(h_kept[...], part, TN).astype(BF16)
            lane = lax.rem(tile, tiles // 2) * width
            send(place, stage.at[slot], 0, width, outs, lane, tile // (tiles // 2), 0, sems.at[slot])

        @pl.when(tile == tiles)
        def _():
            stage[slot] = dot(o_kept[...], dt[...], TN).astype(BF16)
            for half in range(2):
                send(place, stage.at[slot], half * (width // 2), width // 2, outs, depth // 2, half, 0, sems.at[slot])
            finish(stage.at[slot], sems.at[slot])
            finish(stage.at[1 - slot], sems.at[1 - slot])


def narrow(place, resid, active, slope, cot, proj_bias, gain, hidden, attended, wide_pieces, proj_pieces, after=()):
    count, width = resid.shape
    depth = active.shape[1]
    size = 256
    steps = count // size
    early = lambda i: (jnp.minimum(i, steps - 1), 0)
    block = lambda wide: pl.BlockSpec((size, wide), early)
    pieces = [*wide_pieces, *proj_pieces]
    terms = term_shapes(width, width + depth, len(proj_pieces) == 8)
    return kernel_call(
        functools.partial(narrow_kernel, steps, len(terms), len(wide_pieces)),
        [place, resid, active, slope, cot, proj_bias, gain, hidden, attended, *pieces],
        after,
        grid=(steps + depth // width + 1,),
        in_specs=[SMEM, block(width), block(depth), block(depth), block(width)]
        + [whole((1, width))] * 2
        + [ANY] * 2 + [HBM] * len(pieces),
        out_specs=[block(width)] * 3
        + [whole((1, depth))]
        + [whole((1, width))] * 4
        + [ANY] * len(terms),
        out_shape=[
            jax.ShapeDtypeStruct((count, width), BF16),
            jax.ShapeDtypeStruct((count, width), F32),
            jax.ShapeDtypeStruct((count, width), BF16),
            jax.ShapeDtypeStruct((1, depth), F32),
        ]
        + [jax.ShapeDtypeStruct((1, width), F32)] * 4
        + terms,
        scratch_shapes=[
            pltpu.VMEM((depth, width), BF16),
            pltpu.VMEM((width, depth), BF16),
            pltpu.VMEM((width, width), BF16),
            pltpu.VMEM((count, depth), BF16),
            pltpu.VMEM((count, width), BF16),
            pltpu.VMEM((count, width), BF16),
            pltpu.VMEM((count, width), BF16),
            pltpu.VMEM((2, width, width), BF16),
            pltpu.SemaphoreType.DMA((3,)),
            pltpu.SemaphoreType.DMA((2,)),
            pltpu.SemaphoreType.DMA((2,)),
        ],
        compiler_params=params(40),
        cost_estimate=cost(2 * count * width * (2 * width + 4 * depth), 40e6),
        name="narrow",
    )


def attend_back_kernel(block, number, terms, place, q_docs, k_docs, q_all, k_all, v_all, o_all, g_all, lse, hidden, *rest):
    dq, dk, dv = rest[:3]
    outs, rest = rest[3 : 3 + terms], rest[3 + terms :]
    bias, k_sum, v_sum, kept, h_kept, stage, sem, sems = rest
    count = LEN // block
    step = pl.program_id(0)

    @pl.when(step == 0)
    def _():
        pltpu.make_async_copy(hidden, h_kept, sem).start()
        for i in range(count):
            sl, reach = slice(i * block, (i + 1) * block), (i + 1) * block
            bias[:reach, sl] = allowed(q_docs[:, sl], k_docs[:reach, :], i * block, (reach, block), 1)

    @pl.when(step < number)
    def _():
        low = lax.broadcasted_iota(jnp.int32, (block, PAIR), 1) < HD
        low_all = lax.broadcasted_iota(jnp.int32, (LEN, PAIR), 1) < HD
        keys = k_all[...]
        key_one = [jnp.where(low_all, keys, jnp.zeros_like(keys)), jnp.where(low_all, jnp.zeros_like(keys), keys)]
        at = pl.ds(pl.multiple_of(lax.rem(step, number) * PAIR, PAIR), PAIR)
        for i in reversed(range(count)):
            sl, reach = slice(i * block, (i + 1) * block), (i + 1) * block
            q, grad = q_all[sl, :], g_all[sl, :]
            turned = (grad.astype(F32) * o_all[sl, :].astype(F32)).T
            parts = []
            for head in range(2):
                lane = low if head == 0 else ~low
                q_one = jnp.where(lane, q, jnp.zeros_like(q))
                g_one = jnp.where(lane, grad, jnp.zeros_like(grad))
                inner = jnp.sum(turned[head * HD : (head + 1) * HD, :], 0, keepdims=True)
                score = dot(k_all[:reach, :], q_one, NT) + bias[:reach, sl]
                prob = jnp.exp(score - lse[0, head : head + 1, sl])
                v_part = dot(prob.astype(BF16), g_one, NN)
                slope = dot(v_all[:reach, :], g_one, NT)
                dscore = (prob * (slope - inner)).astype(BF16)
                k_part = dot(dscore, q_one, NN)
                if i == count - 1 and head == 0:
                    k_sum[...] = k_part
                    v_sum[...] = v_part
                else:
                    k_sum[:reach, :] += k_part
                    v_sum[:reach, :] += v_part
                parts.append(dot(dscore, key_one[head][:reach], TN))
            part = ((parts[0] + parts[1]) * (1.0 / math.sqrt(HD))).astype(BF16)
            dq[sl, :] = part
            kept[0, sl, at] = part
        for index, (ref, total) in enumerate(((dk, k_sum), (dv, v_sum))):
            part = total[...].astype(BF16)
            ref[...] = part
            kept[1 + index, :, at] = part

    wide = stage.shape[3]

    @pl.when(step >= number)
    def _():
        tile = step - number
        slot = lax.rem(tile, 2)

        @pl.when(tile == 0)
        def _():
            finish(h_kept, sem)

        @pl.when(tile >= 2)
        def _():
            finish(stage.at[slot], sems.at[slot])

        for index in range(3):
            part = kept[index, :, pl.ds(pl.multiple_of(tile * wide, wide), wide)]
            stage[slot, index] = dot(h_kept[...], part, TN).astype(BF16)
        for index in range(3):
            for half in range(2):
                send(
                    place,
                    stage.at[slot, index],
                    half * (wide // 2),
                    wide // 2,
                    outs,
                    index * (number * PAIR // 2) + tile * (wide // 2),
                    half,
                    0,
                    sems.at[slot],
                )

        @pl.when(tile == number * PAIR // wide - 1)
        def _():
            finish(stage.at[slot], sems.at[slot])
            if number * PAIR // wide > 1:
                finish(stage.at[1 - slot], sems.at[1 - slot])


def attend_back(place, mixed, attended, grad_o, lse, docs, hidden, by_stage, after=()):
    width = attended.shape[1]
    number = width // PAIR
    block = 256
    wide = 2 * PAIR
    steps = width // wide
    pair = lambda i: jnp.minimum(i, number - 1)
    column = lambda base: pl.BlockSpec((LEN, PAIR), lambda i: (0, base + pair(i)))
    terms = term_shapes(width, 3 * number * PAIR, by_stage)
    return kernel_call(
        functools.partial(attend_back_kernel, block, number, len(terms)),
        [place, docs.reshape(1, LEN), docs.reshape(LEN, 1), mixed, mixed, mixed, attended, grad_o, lse, hidden],
        after,
        grid=(number + steps,),
        in_specs=[
            SMEM,
            whole((1, LEN)),
            whole((LEN, 1)),
            column(0),
            column(number),
            column(2 * number),
            column(0),
            column(0),
            pl.BlockSpec((1, 2, LEN), lambda i: (pair(i), 0, 0)),
            ANY,
        ],
        out_specs=[column(0)] * 3 + [ANY] * len(terms),
        out_shape=[jax.ShapeDtypeStruct((LEN, PAIR * number), BF16)] * 3 + terms,
        scratch_shapes=[
            pltpu.VMEM((LEN, LEN), F32),
            pltpu.VMEM((LEN, PAIR), F32),
            pltpu.VMEM((LEN, PAIR), F32),
            pltpu.VMEM((3, LEN, PAIR * number), BF16),
            pltpu.VMEM((LEN, width), BF16),
            pltpu.VMEM((2, 3, width, wide), BF16),
            pltpu.SemaphoreType.DMA,
            pltpu.SemaphoreType.DMA((2,)),
        ],
        compiler_params=params(56),
        cost_estimate=cost(42e9, 20e6),
        name="attend_back",
    )


def first_back_kernel(place, x, grad_r, gain, *rest):
    parts, pieces, rest = rest[:3], rest[3:-4], rest[-4:]
    grad_x, sums, weight, sem = rest
    width = x.shape[1]

    @pl.when(pl.program_id(0) == 0)
    def _():
        fetch(place, pieces, 0, 0, 3 * width // 2, weight, sem)()
        sums[...] = jnp.zeros_like(sums)

    grad_h = dot(parts[0][...], weight[:, :width], NT)
    for index in (1, 2):
        grad_h += dot(parts[index][...], weight[:, index * width : (index + 1) * width], NT)
    for at, part in ((2, parts[0]), (3, parts[2])):
        sums[at : at + 1, :] += jnp.sum(part[...].astype(F32), 0, keepdims=True)
    pulled, gains, shifts = norm_back(x[...].astype(F32), gain[...], grad_h)
    grad_x[...] = grad_r[...] + pulled
    sums[0:1, :] += gains
    sums[1:2, :] += shifts


def first_back(place, x, grad_r, gain, parts, pieces, after=()):
    count, width = x.shape
    block = 256
    return kernel_call(
        first_back_kernel,
        [place, x, grad_r, gain, *parts, *pieces],
        after,
        grid=(count // block,),
        in_specs=[SMEM, rows(block, width), rows(block, width), whole((1, width))]
        + [rows(block, part.shape[1]) for part in parts]
        + [HBM] * len(pieces),
        out_specs=[rows(block, width), whole((4, width))],
        out_shape=[jax.ShapeDtypeStruct((count, width), F32), jax.ShapeDtypeStruct((4, width), F32)],
        scratch_shapes=[pltpu.VMEM((width, 3 * width), BF16), pltpu.SemaphoreType.DMA],
        compiler_params=params(56),
        cost_estimate=cost(6 * count * width * width, 16e6),
        name="first_back",
    )


def pack_kernel(*refs):
    vectors, out = refs[:-1], refs[-1]
    devices, lanes = out.shape
    width = vectors[0].shape[1]
    unit = lanes // 12
    rows_of = [
        vector[row : row + 1, first : first + width]
        for vector in vectors
        for row in range(vector.shape[0])
        for first in range(0, vector.shape[1], width)
    ]
    total = jnp.zeros((devices, 12 * unit + (-12 * unit) % 128), F32)
    full = total.shape[1]
    at, base = 0, 0
    for span in (1, 1, 2, 1, 1, 1, 4, 1):
        size = span * unit + (-span * unit) % 128
        shape = (size, width)
        spreads = []
        for index in range(span):
            mine = owner((devices, width), span * unit, index * width)
            spreads.append(jnp.where(mine, rows_of[at + index], 0.0))
        at += span
        found = jnp.zeros((devices, size), F32)
        for index, spread in enumerate(spreads):
            pick = one_hot(shape, 0, span * unit, index * width).astype(BF16)
            high = spread.astype(BF16)
            low = (spread - high.astype(F32)).astype(BF16)
            both = dot(jnp.concatenate([high, low], 0), pick, NT)
            found = found + both[:devices] + both[devices:]
        if size < full:
            found = jnp.concatenate([found, jnp.zeros((devices, full - size), F32)], 1)
        total = total + (found if base == 0 else pltpu.roll(found, base * unit, 1))
        base += span
    out[...] = total[:, :lanes]


def pack(vectors, devices):
    lanes = sum(v.size for v in vectors) // devices
    return pl.pallas_call(
        pack_kernel,
        out_shape=jax.ShapeDtypeStruct((devices, lanes), F32),
        compiler_params=params(16),
        name="pack",
    )(*vectors)


def staged(
    tokens,
    doc_ids,
    d_out,
    ln1_gain,
    ln1_shift,
    qkv_weight,
    qv_bias,
    out_weight,
    out_bias,
    ln2_gain,
    ln2_shift,
    fc_weight,
    fc_bias,
    proj_weight,
    proj_bias,
):
    width = tokens.shape[1]
    depth = fc_weight.shape[1]
    devices = lax.axis_size("dp") * lax.axis_size("fsdp")
    index = lax.axis_index("dp") * lax.axis_size("fsdp") + lax.axis_index("fsdp")
    core = index & 1
    place = jnp.stack([index >> 1, core]).astype(jnp.int32)
    by_stage = (lax.axis_size("dp"), lax.axis_size("fsdp")) == (8, 4)

    smalls = [ln1_gain, ln1_shift, qv_bias, out_bias, ln2_gain, ln2_shift, fc_bias, proj_bias]
    smalls = jnp.concatenate([v.astype(F32).reshape(1, -1) for v in smalls], 1).reshape(-1)
    if by_stage:
        extra = jnp.pad(smalls, (0, -smalls.size % 128)).reshape(-1, 128).astype(BF16)
        extra = jnp.pad(extra, ((0, qkv_weight.shape[0] - extra.shape[0]), (0, 0)))
        first_block = pair_block(qkv_weight, core, extra)
        out_weight, fc_weight, proj_weight = tie([out_weight, fc_weight, proj_weight], first_block)
        wide_block = jnp.concatenate([pair_block(out_weight, core), pair_block(fc_weight, core)], 1)
        proj_block = pair_block(proj_weight, core)
        first_column = jnp.stack([first_block] + by_z([first_block] * 3))
        (wide_block,) = tie([wide_block], first_column)
        first_got, wide_got, (proj_near,) = meet(
            by_xy([first_column] * 3), by_z([wide_block] * 3), [swap(tie([proj_block], first_column)[0], Z0)]
        )
        first_pieces = gather_core([first_column, *first_got])
        wide_column = jnp.stack([wide_block] + wide_got)
        wide_got = by_xy([wide_column] * 3)
        (proj_block,) = tie([proj_block], wide_column)
        proj_got = [swap(proj_block, bits) for bits in (Z1, Z0 | Z1)]
    else:
        first_pieces, proj_pieces = [gather_all(qkv_weight)], [gather_all(proj_weight)]
        wide_pieces = [gather_all(w) for w in (out_weight, fc_weight)]
        wide_column = None
        table = gather_all(smalls.reshape(1, -1).astype(BF16))
        first_pieces = first_pieces + [jnp.pad(table, ((0, 0), (0, -table.shape[1] % 128)))]
    hold = lambda *some: list(some) if by_stage else []
    row = lambda at, count=1: vectors[at : at + count].reshape(1, -1)

    found = project_attend(place, tokens, doc_ids, first_pieces, after=hold(wide_column) if by_stage else [])
    if by_stage:
        found, wide_got, proj_got = meet(found, wide_got, proj_got)
        proj_column = jnp.stack([proj_block, proj_near] + proj_got)
        proj_got = by_xy([proj_column] * 3)
        wide_pieces = gather_core([wide_column, *wide_got])
    mixed, h_one, attended, lse, vectors = found

    found = widen(
        place,
        tokens,
        attended,
        row(4),
        row(5),
        row(6),
        row(7, 4),
        d_out,
        wide_pieces,
        after=hold(proj_column) if by_stage else [],
    )
    if by_stage:
        found, proj_got = meet(found, proj_got)
        proj_pieces = gather_core([proj_column, *proj_got])
        proj_sums = scatter_core(found[4:])
        proj_got = by_xy(proj_sums[1:])
    resid, h_two, slope, active, *proj_terms = found

    found = narrow(
        place,
        resid,
        active,
        slope,
        d_out,
        row(11),
        row(5),
        h_two,
        attended,
        wide_pieces,
        proj_pieces,
        after=hold(*proj_sums) if by_stage else [],
    )
    if by_stage:
        found, proj_got = meet(found, proj_got)
        proj_sums = sum_xy(proj_sums, proj_got)
        proj_got = by_z(proj_sums[1:])
        wide_sums = scatter_core(found[8:])
        wide_got = by_xy(wide_sums[1:])
    result, grad_r, grad_o, fc_sum, proj_sum, gain_two, shift_two, out_sum, *wide_terms = found

    found = attend_back(
        place,
        mixed,
        attended,
        grad_o,
        lse,
        doc_ids,
        h_one,
        by_stage,
        after=hold(*proj_sums, *wide_sums) if by_stage else [],
    )
    if by_stage:
        found, wide_got, proj_got = meet(found, wide_got, proj_got)
        wide_sums = sum_xy(wide_sums, wide_got)
        wide_got = by_z(wide_sums[1:])
        qkv_sums = scatter_core(found[3:])
        qkv_got = by_xy(qkv_sums[1:])
    *grads, qkv_terms = found[:4]

    found = first_back(
        place,
        tokens,
        grad_r,
        row(0),
        grads,
        first_pieces[:8] if by_stage else first_pieces[:1],
        after=hold(*qkv_sums, *wide_sums) if by_stage else [],
    )
    if by_stage:
        found, wide_got, qkv_got = meet(found, wide_got, qkv_got)
    grad_x, first_sums = found
    sums = [first_sums, out_sum, gain_two, shift_two, fc_sum, proj_sum]
    table = pack(sums, devices)
    if by_stage:
        qkv_sums = sum_xy(qkv_sums, qkv_got)
        table = scatter_small(tie([table], *qkv_sums)[0], index, (Z1, Z0, Y, X))
        (table,), qkv_got = meet([table], by_z(qkv_sums[1:]))
        proj_grad, wide_grad = add(proj_sums[0], *proj_got), add(wide_sums[0], *wide_got)
    else:
        own = scatter_all(table).reshape(-1)
        proj_grad, wide_grad, qkv_grad = (
            scatter_all(terms.astype(F32)) for terms in (proj_terms[0], wide_terms[0], qkv_terms)
        )

    def sides(grad):
        if by_stage:
            return own_rows(grad, core)
        return jnp.split(grad, 2, 1)

    proj_grad = jnp.concatenate(sides(proj_grad), 1)
    both = sides(wide_grad)
    half = depth // 2
    fc_grad = jnp.concatenate([side[:, :half] for side in both], 1)
    out_grad = jnp.concatenate([side[:, half:] for side in both], 1)
    if by_stage:
        own = scatter_small(table, index, (CORE,)).reshape(-1)
        qkv_grad = add(qkv_sums[0], *qkv_got)
    both = sides(qkv_grad)
    qkv_grad = jnp.concatenate(
        [side[:, lane : lane + PAIR] for lane in range(0, both[0].shape[1], PAIR) for side in both], 1
    )
    n = width // devices
    spots = (0, n, 2 * n, 4 * n, 5 * n, 6 * n, 7 * n, 11 * n, 12 * n)
    s = [own[a:b] for a, b in zip(spots[:-1], spots[1:])]
    return (
        result,
        grad_x,
        s[0],
        s[1],
        qkv_grad,
        s[2],
        out_grad,
        s[3],
        s[4],
        s[5],
        fc_grad,
        s[6],
        proj_grad,
        s[7],
    )


def solution(mesh):
    every, block = P(AXES), P(AXES, None)
    ins = (block, every, block, every, every, block, every, block, every, every, every, block, every, block, every)
    outs = (block, block, every, every, block, every, block, every, every, every, block, every, block, every)
    return jax.shard_map(staged, mesh=mesh, in_specs=ins, out_specs=outs, check_vma=False)
```

```python
import functools
import math

import jax
import jax.numpy as jnp
from jax import lax
from jax.experimental import pallas as pl
from jax.experimental.pallas import tpu as pltpu
from jax.sharding import PartitionSpec as P

HD = 64
LEN = 1024
PAIR = 2 * HD
EPS = 1e-05
NEG = -1e30
AXES = ("dp", "fsdp")

F32 = jnp.float32
BF16 = jnp.bfloat16
NN = (((1,), (0,)), ((), ()))
NT = (((1,), (1,)), ((), ()))
TN = (((0,), (0,)), ((), ()))
ANY = pl.BlockSpec(memory_space=pl.ANY)
HBM = pl.BlockSpec(memory_space=pltpu.HBM)
SMEM = pl.BlockSpec(memory_space=pltpu.SMEM)

CORE, X, Y, Z0, Z1 = 1, 2, 4, 8, 16
CX, CY, CZ0, CZ1 = 1, 2, 4, 8
GROUPS = tuple(tuple(near | far for far in (0, CZ0, CZ1, CZ0 | CZ1)) for near in (0, CX, CY, CX | CY))


def dot(a, b, dims):
    return lax.dot_general(a, b, dims, preferred_element_type=F32)


def params(size):
    return pltpu.CompilerParams(vmem_limit_bytes=size << 20)


def cost(flops, size):
    return pl.CostEstimate(flops=int(flops), bytes_accessed=int(size), transcendentals=0)


def whole(shape):
    return pl.BlockSpec(shape, lambda *g: (0,) * len(shape))


def rows(block, width):
    return pl.BlockSpec((block, width), lambda i: (i, 0))


def swap(array, bit):
    count = lax.axis_size("dp") * lax.axis_size("fsdp")
    return lax.ppermute(array, AXES, [(i, i ^ bit) for i in range(count)])


def halves(array, core):
    width = array.shape[1] // 2
    low, high = array[:, :width], array[:, width:]
    first = core == 0
    return jnp.where(first, low, high), jnp.where(first, high, low)


def pair_block(array, core, extra=None):
    keep, send = halves(array, core)
    if extra is not None:
        keep, send = jnp.concatenate([keep, extra], 1), jnp.concatenate([send, extra], 1)
    other = swap(send, CORE)
    first = core == 0
    return jnp.concatenate([jnp.where(first, keep, other), jnp.where(first, other, keep)], 0)


def by_z(parts):
    return [swap(part, bits) for part, bits in zip(parts, (Z0, Z1, Z0 | Z1))]


def by_xy(parts):
    return [swap(part, bits) for part, bits in zip(parts, (X, Y, X | Y))]


def gather_core(own):
    return [*own, *(swap(piece, CORE) for piece in own)]


def add(*terms):
    return functools.reduce(lambda a, b: a + b, [t.astype(F32) for t in terms])


def scatter_core(terms):
    mine, other = terms
    got = swap(other, CORE)
    return [add(mine[g], got[g]).astype(BF16) for g in range(4)]


def sum_xy(sums, got):
    return [add(*(part[spot] for part in [sums[0], *got])).astype(BF16) for spot in range(4)]


def tie(arrays, *others):
    if not others:
        return list(arrays)
    return list(lax.optimization_barrier((*arrays, *others))[: len(arrays)])


def meet(*lists):
    found = iter(lax.optimization_barrier(tuple(array for arrays in lists for array in arrays)))
    return [[next(found) for _ in arrays] for arrays in lists]


def kernel_call(kernel, inputs, after, **how):
    return pl.pallas_call(kernel, **how)(*tie(inputs[:1], *after), *inputs[1:])


def own_rows(block, core):
    count = block.shape[0] // 2
    low, high = block[:count], block[count:]
    first = core == 0
    keep = jnp.where(first, low, high)
    got = swap(jnp.where(first, high, low), CORE)
    return jnp.where(first, keep, got), jnp.where(first, got, keep)


def gather_all(array):
    return lax.all_gather(array, AXES, axis=0, tiled=True)


def scatter_all(array):
    return lax.psum_scatter(array, AXES, scatter_dimension=0, tiled=True)


def scatter_small(table, index, bits):
    for bit in bits:
        count = table.shape[0] // 2
        low = (index & bit) == 0
        keep = jnp.where(low, table[:count], table[count:])
        send = jnp.where(low, table[count:], table[:count])
        table = keep + swap(send, bit)
    return table


def fetch(place, pieces, which, lane, width, into, sem):
    if len(pieces) < 8:
        pltpu.make_async_copy(pieces[which], into, sem).start()
        return lambda: pltpu.make_async_copy(into, into, sem).wait()
    chip, core = place[0], place[1]
    step = into.shape[0] // 16
    for side in range(2):
        half = core if side == 0 else 1 - core
        column = pl.ds(pl.multiple_of(half * width, 128), width)
        for group in range(4):
            for spot, relative in enumerate(GROUPS[group]):
                owner = lax.bitwise_xor(chip, relative)
                pltpu.make_async_copy(
                    pieces[4 * side + group].at[spot, :, pl.ds(lane, width)],
                    into.at[pl.ds(pl.multiple_of(owner * step, step), step), column],
                    sem,
                ).start()
    return lambda: pltpu.make_async_copy(into, into, sem).wait()


def normal(v):
    center = v - jnp.mean(v, -1, keepdims=True)
    spread = jnp.mean(center * center, -1, keepdims=True)
    factor = lax.rsqrt(spread + EPS)
    return center * factor, factor


def one_hot(shape, base, span, first):
    lane = lax.broadcasted_iota(jnp.int32, shape, 0)
    element = lax.broadcasted_iota(jnp.int32, (1, shape[1]), 1) + first
    return lane == base + lax.rem(element, span)


def owner(shape, span, first):
    element = lax.broadcasted_iota(jnp.int32, (1, shape[1]), 1) + first
    return lax.broadcasted_iota(jnp.int32, shape, 0) == element // span


def unpack_rows(table, out, lanes):
    devices, full = table.shape
    width = out.shape[1]
    unit = lanes // 12
    wide = table.astype(F32)
    spans = (1, 1, 2, 1, 1, 1, 4, 1)
    for span in (1, 2, 4):
        starts = [sum(spans[:i]) for i, one in enumerate(spans) if one == span]
        parts = [
            (wide if start == 0 else pltpu.roll(wide, full - start * unit, 1))[:, :128].astype(BF16) for start in starts
        ]
        pick = one_hot((128, width), 0, span * unit, 0).astype(BF16)
        values = dot(jnp.concatenate(parts, 0), pick, NN)
        for index, start in enumerate(starts):
            value = values[index * devices : (index + 1) * devices]
            for row in range(span):
                mine = owner((devices, width), span * unit, row * width)
                out[start + row : start + row + 1, :] = jnp.sum(jnp.where(mine, value, 0.0), 0, keepdims=True)


def unpack_blocks(place, pieces, out, kept, sem):
    lane = pieces[0].shape[2] - 128
    chip = place[0]
    step = pieces[0].shape[1]
    for group in range(4):
        for spot, relative in enumerate(GROUPS[group]):
            there = pl.ds(pl.multiple_of(lax.bitwise_xor(chip, relative) * step, step), step)
            pltpu.make_async_copy(pieces[group].at[spot, :, pl.ds(lane, 128)], kept.at[there, :], sem).start()
    finish(kept, sem)
    width = out.shape[1]
    devices = width // (step // 2)
    lanes = 12 * step // 2
    parts = []
    for part in range(-(-lanes // 128)):
        shape = (devices, width)
        device = lax.broadcasted_iota(jnp.int32, shape, 0)
        pick = lax.broadcasted_iota(jnp.int32, shape, 1) == device * (step // 2) + part
        parts.append(dot(pick.astype(BF16), kept[...], NN).astype(BF16))
    unpack_rows(jnp.concatenate(parts, 1), out, lanes)


def allowed(q_doc, k_doc, first, shape, q_dim):
    q_pos = lax.broadcasted_iota(jnp.int32, shape, q_dim) + first
    k_pos = lax.broadcasted_iota(jnp.int32, shape, 1 - q_dim)
    allow = ((k_pos <= q_pos) & (q_doc == k_doc) & (k_doc > 0)) | (k_pos == q_pos)
    return jnp.where(allow, 0.0, NEG)


def project_attend_kernel(steps, block, place, x, q_docs, k_docs, *rest):
    pieces, rest = rest[:-12], rest[-12:]
    mixed, hidden, out, lse, vectors, kept, bias, weight, small, sem, kept_sem, small_sem = rest
    width = x.shape[1]
    size = x.shape[0]
    step = pl.program_id(0)

    @pl.when(step == 0)
    def _():
        wait = fetch(place, pieces, 0, 0, 3 * width // 2, weight, sem)
        if len(pieces) == 8:
            unpack_blocks(place, pieces[:4], vectors, small, small_sem)
        else:
            unpack_rows(pieces[1][...], vectors, 12 * vectors.shape[1] // pieces[1].shape[0])
        for i in range(LEN // block):
            sl, reach = slice(i * block, (i + 1) * block), (i + 1) * block
            bias[sl, :reach] = allowed(q_docs[sl, :], k_docs[:, :reach], i * block, (block, reach), 0)
        wait()

    @pl.when(step < steps)
    def _():
        unit, _ = normal(x[...].astype(F32))
        h = (unit * vectors[0:1, :] + vectors[1:2, :]).astype(BF16)
        hidden[...] = h
        scale = 1.0 / math.sqrt(HD)
        here = pl.ds(pl.multiple_of(step * size, size), size)
        for part in range(3):
            sl = slice(part * width, (part + 1) * width)
            value = dot(h, weight[:, sl], NN)
            if part == 0:
                value = (value + vectors[2:3, :]).astype(BF16).astype(F32) * scale
            if part == 2:
                value = value + vectors[3:4, :]
            kept[here, sl] = value.astype(BF16)
        pltpu.make_async_copy(kept.at[here, :], mixed.at[here, :], kept_sem).start()

    @pl.when(step >= steps)
    def _():
        lane = (step - steps) * PAIR
        q_at, k_at, v_at = (pl.ds(pl.multiple_of(lane + part * width, PAIR), PAIR) for part in range(3))
        low = lax.broadcasted_iota(jnp.int32, (block, PAIR), 1) < HD
        for i in range(LEN // block):
            sl, reach = slice(i * block, (i + 1) * block), (i + 1) * block
            q = kept[sl, q_at]
            outs, logs = [], []
            for head in range(2):
                q_one = jnp.where(low if head == 0 else ~low, q, jnp.zeros_like(q))
                score = dot(q_one, kept[:reach, k_at], NT) + bias[sl, :reach]
                top = jnp.max(score, -1, keepdims=True)
                expo = jnp.exp(score - top)
                total = jnp.sum(expo, -1, keepdims=True)
                outs.append(dot(expo.astype(BF16), kept[:reach, v_at], NN) / total)
                logs.append(top + jnp.log(total))
            out[sl, :] = jnp.where(low, outs[0], outs[1]).astype(BF16)
            turned = jnp.where(low, logs[0], logs[1]).T
            lse[0, 0:1, sl] = turned[0:1, :]
            lse[0, 1:2, sl] = turned[HD : HD + 1, :]

    @pl.when(step == pl.num_programs(0) - 1)
    def _():
        finish(kept, kept_sem)


def project_attend(place, x, docs, pieces, after=()):
    count, width = x.shape
    size, block = 256, 512
    steps = count // size
    pairs = width // PAIR
    early = lambda i: (jnp.minimum(i, steps - 1), 0)
    late = lambda i: jnp.maximum(i - steps, 0)
    return kernel_call(
        functools.partial(project_attend_kernel, steps, block),
        [place, x, docs.reshape(LEN, 1), docs.reshape(1, LEN), *pieces],
        after,
        grid=(steps + pairs,),
        in_specs=[SMEM, pl.BlockSpec((size, width), early), whole((LEN, 1)), whole((1, LEN))]
        + ([HBM] * 8 if len(pieces) == 8 else [HBM, whole(pieces[1].shape)]),
        out_specs=[
            HBM,
            pl.BlockSpec((size, width), early),
            pl.BlockSpec((LEN, PAIR), lambda i: (0, late(i))),
            pl.BlockSpec((1, 2, LEN), lambda i: (late(i), 0, 0)),
            whole((12, width)),
        ],
        out_shape=[
            pltpu.HBM((count, 3 * width), BF16),
            pltpu.HBM((count, width), BF16),
            jax.ShapeDtypeStruct((count, width), BF16),
            jax.ShapeDtypeStruct((pairs, 2, LEN), F32),
            jax.ShapeDtypeStruct((12, width), F32),
        ],
        scratch_shapes=[
            pltpu.VMEM((count, 3 * width), BF16),
            pltpu.VMEM((LEN, LEN), F32),
            pltpu.VMEM((width, 3 * width), BF16),
            pltpu.VMEM((width, 128), BF16),
            pltpu.SemaphoreType.DMA,
            pltpu.SemaphoreType.DMA,
            pltpu.SemaphoreType.DMA,
        ],
        compiler_params=params(26),
        cost_estimate=cost(28e9, 20e6),
        name="project_attend",
    )


def norm_back(v, gain, grad):
    unit, factor = normal(v)
    g = grad * gain
    pulled = factor * (g - jnp.mean(g, -1, keepdims=True) - unit * jnp.mean(g * unit, -1, keepdims=True))
    return pulled, jnp.sum(grad * unit, 0, keepdims=True), jnp.sum(grad, 0, keepdims=True)


def send(place, tile, column, width, outs, lane, half, first, sem):
    here = pl.ds(column, width)
    if len(outs) == 1:
        per_half = outs[0].shape[1] // 2
        at = pl.ds(pl.multiple_of(half * per_half + lane, 128), width)
        top = pl.ds(pl.multiple_of(first * (outs[0].shape[0] // 16), 16), tile.shape[0])
        pltpu.make_async_copy(tile.at[:, here], outs[0].at[top, at], sem).start()
        return
    chip, core = place[0], place[1]
    step = outs[0].shape[2]
    at = pl.ds(pl.multiple_of(lane, 128), width)
    for index in range(tile.shape[0] // step):
        relative = lax.bitwise_xor(chip, first + index)
        group, spot = lax.bitwise_and(relative, 3), lax.shift_right_logical(relative, 2)
        source = tile.at[pl.ds(index * step, step), here]
        for own, target in ((True, outs[0]), (False, outs[1])):
            copy = pltpu.make_async_copy(source, target.at[group, spot, :, at], sem)
            pl.when((half == core) == own)(copy.start)


def finish(ref, sem):
    pltpu.make_async_copy(ref, ref, sem).wait()


def term_shapes(tall, wide, by_stage):
    if by_stage:
        return [jax.ShapeDtypeStruct((4, 4, tall // 16, wide // 2), BF16)] * 2
    return [jax.ShapeDtypeStruct((tall, wide), BF16)]


def widen_kernel(steps, terms, place, x, attended, out_bias, gain, shift, fc_bias, cot, *rest):
    count = terms + 15
    pieces, rest = rest[:-count], rest[-count:]
    resid, hidden, slope, active = rest[:4]
    outs, rest = rest[4 : 4 + terms], rest[4 + terms :]
    w_out, w_fc, kept, bent, grad, stage, weight_sems, kept_sem, bent_sem, grad_sem, sems = rest
    size, width = x.shape
    depth = w_fc.shape[1]
    step = pl.program_id(0)
    here = pl.ds(pl.multiple_of(lax.rem(step, steps) * size, size), size)

    @pl.when(step == 0)
    def _():
        wait_out = fetch(place, pieces, 0, 0, width // 2, w_out, weight_sems.at[0])
        wait_fc = fetch(place, pieces, 1, width // 2, depth // 2, w_fc, weight_sems.at[1])
        pltpu.make_async_copy(cot, grad, grad_sem).start()
        wait_out()
        wait_fc()

    @pl.when(step < steps)
    def _():
        r = x[...].astype(F32) + dot(attended[...], w_out[...], NN) + out_bias[...]
        resid[...] = r
        unit, _ = normal(r)
        h = (unit * gain[...] + shift[...]).astype(BF16)
        hidden[...] = h
        c = math.sqrt(2.0 / math.pi)
        for first in range(0, depth, width):
            sl = slice(first, first + width)
            u = dot(h, w_fc[:, sl], NN) + fc_bias[:, sl]
            bend = (c * 0.044715) * (u * u) + c
            half = 0.5 * jnp.tanh(u * bend) + 0.5
            value = u * half
            kept[here, sl] = value.astype(BF16)
            bent[here, sl] = (half + value * (1.0 - half) * (6.0 * bend - 4.0 * c)).astype(BF16)
        pltpu.make_async_copy(kept.at[here, :], active.at[here, :], kept_sem).start()
        pltpu.make_async_copy(bent.at[here, :], slope.at[here, :], bent_sem).start()

    @pl.when(step >= steps)
    def _():
        tile = step - steps
        slot = lax.rem(tile, 2)

        @pl.when(tile == 0)
        def _():
            finish(grad, grad_sem)

        @pl.when(tile >= 2)
        def _():
            finish(stage.at[slot], sems.at[slot])

        tall = stage.shape[1]
        part = kept[:, pl.ds(pl.multiple_of(tile * tall, tall), tall)]
        stage[slot] = dot(part, grad[...], TN).astype(BF16)
        chips = tall * 16 // depth
        for half in range(2):
            send(place, stage.at[slot], half * (width // 2), width // 2, outs, 0, half, tile * chips, sems.at[slot])

        @pl.when(tile == depth // tall - 1)
        def _():
            finish(stage.at[slot], sems.at[slot])
            finish(stage.at[1 - slot], sems.at[1 - slot])
            finish(kept, kept_sem)
            finish(bent, bent_sem)


def widen(place, x, attended, out_bias, gain, shift, fc_bias, cot, pieces, after=()):
    count, width = x.shape
    depth = fc_bias.shape[1]
    size, tall = 256, width
    steps = count // size
    early = lambda i: (jnp.minimum(i, steps - 1), 0)
    block = lambda wide: pl.BlockSpec((size, wide), early)
    terms = term_shapes(depth, width, len(pieces) == 8)
    return kernel_call(
        functools.partial(widen_kernel, steps, len(terms)),
        [place, x, attended, out_bias, gain, shift, fc_bias, cot, *pieces],
        after,
        grid=(steps + depth // tall,),
        in_specs=[SMEM, block(width), block(width)]
        + [whole((1, width))] * 3
        + [whole((1, depth)), ANY]
        + [HBM] * len(pieces),
        out_specs=[block(width), block(width), HBM, HBM] + [ANY] * len(terms),
        out_shape=[
            pltpu.HBM((count, width), F32),
            jax.ShapeDtypeStruct((count, width), BF16),
            pltpu.HBM((count, depth), BF16),
            pltpu.HBM((count, depth), BF16),
        ]
        + terms,
        scratch_shapes=[
            pltpu.VMEM((width, width), BF16),
            pltpu.VMEM((width, depth), BF16),
            pltpu.VMEM((count, depth), BF16),
            pltpu.VMEM((count, depth), BF16),
            pltpu.VMEM((count, width), BF16),
            pltpu.VMEM((2, tall, width), BF16),
            pltpu.SemaphoreType.DMA((2,)),
            pltpu.SemaphoreType.DMA,
            pltpu.SemaphoreType.DMA,
            pltpu.SemaphoreType.DMA,
            pltpu.SemaphoreType.DMA((2,)),
        ],
        compiler_params=params(32),
        cost_estimate=cost(2 * count * width * (width + 2 * depth), 30e6),
        name="widen",
    )


def narrow_kernel(steps, terms, sides, place, resid, active, slope, cot, proj_bias, gain, hidden, attended, *rest):
    count = terms + 19
    pieces, rest = rest[:-count], rest[-count:]
    wide_pieces, proj_pieces = pieces[:sides], pieces[sides:]
    result, grad_r, grad_o, fc_sum, proj_sum, gain_sum, shift_sum, bias_sum = rest[:8]
    outs, rest = rest[8 : 8 + terms], rest[8 + terms :]
    w_proj, w_fc, w_out, du, dt, h_kept, o_kept, stage, weight_sems, kept_sems, sems = rest
    size, width = resid.shape
    depth = active.shape[1]
    step = pl.program_id(0)
    here = pl.ds(pl.multiple_of(lax.rem(step, steps) * size, size), size)

    @pl.when(step == 0)
    def _():
        wait_proj = fetch(place, proj_pieces, 0, 0, width // 2, w_proj, weight_sems.at[0])
        wait_fc = fetch(place, wide_pieces, 1, width // 2, depth // 2, w_fc, weight_sems.at[1])
        wait_out = fetch(place, wide_pieces, 0, 0, width // 2, w_out, weight_sems.at[2])
        pltpu.make_async_copy(hidden, h_kept, kept_sems.at[0]).start()
        pltpu.make_async_copy(attended, o_kept, kept_sems.at[1]).start()
        for total in (fc_sum, proj_sum, gain_sum, shift_sum, bias_sum):
            total[...] = jnp.zeros_like(total)
        wait_proj()
        wait_fc()
        wait_out()

    @pl.when(step < steps)
    def _():
        g = cot[...]
        for first in range(0, depth, width):
            sl = slice(first, first + width)
            part = (dot(g, w_proj[sl, :], NT) * slope[:, sl].astype(F32)).astype(BF16)
            du[here, sl] = part
            fc_sum[:, sl] += jnp.sum(part.astype(F32), 0, keepdims=True)
        r = resid[...]
        result[...] = (r + dot(active[...], w_proj[...], NN) + proj_bias[...]).astype(BF16)
        wide = g.astype(F32)
        proj_sum[...] += jnp.sum(wide, 0, keepdims=True)
        grad_h = dot(du[here, :], w_fc[...], NT)
        pulled, gains, shifts = norm_back(r, gain[...], grad_h)
        total = wide + pulled
        grad_r[...] = total
        low = total.astype(BF16)
        dt[here, :] = low
        gain_sum[...] += gains
        shift_sum[...] += shifts
        bias_sum[...] += jnp.sum(low.astype(F32), 0, keepdims=True)
        grad_o[...] = dot(low, w_out[...], NT).astype(BF16)

    tiles = depth // width

    @pl.when(step >= steps)
    def _():
        tile = step - steps
        slot = lax.rem(tile, 2)

        @pl.when(tile == 0)
        def _():
            finish(h_kept, kept_sems.at[0])
            finish(o_kept, kept_sems.at[1])

        @pl.when(tile >= 2)
        def _():
            finish(stage.at[slot], sems.at[slot])

        @pl.when(tile < tiles)
        def _():
            part = du[:, pl.ds(pl.multiple_of(lax.rem(tile, tiles) * width, width), width)]
            stage[slot] = dot(h_kept[...], part, TN).astype(BF16)
            lane = lax.rem(tile, tiles // 2) * width
            send(place, stage.at[slot], 0, width, outs, lane, tile // (tiles // 2), 0, sems.at[slot])

        @pl.when(tile == tiles)
        def _():
            stage[slot] = dot(o_kept[...], dt[...], TN).astype(BF16)
            for half in range(2):
                send(place, stage.at[slot], half * (width // 2), width // 2, outs, depth // 2, half, 0, sems.at[slot])
            finish(stage.at[slot], sems.at[slot])
            finish(stage.at[1 - slot], sems.at[1 - slot])


def narrow(place, resid, active, slope, cot, proj_bias, gain, hidden, attended, wide_pieces, proj_pieces, after=()):
    count, width = resid.shape
    depth = active.shape[1]
    size = 256
    steps = count // size
    early = lambda i: (jnp.minimum(i, steps - 1), 0)
    block = lambda wide: pl.BlockSpec((size, wide), early)
    pieces = [*wide_pieces, *proj_pieces]
    terms = term_shapes(width, width + depth, len(proj_pieces) == 8)
    return kernel_call(
        functools.partial(narrow_kernel, steps, len(terms), len(wide_pieces)),
        [place, resid, active, slope, cot, proj_bias, gain, hidden, attended, *pieces],
        after,
        grid=(steps + depth // width + 1,),
        in_specs=[SMEM, block(width), block(depth), block(depth), block(width)]
        + [whole((1, width))] * 2
        + [ANY] * 2 + [HBM] * len(pieces),
        out_specs=[block(width)] * 3
        + [whole((1, depth))]
        + [whole((1, width))] * 4
        + [ANY] * len(terms),
        out_shape=[
            jax.ShapeDtypeStruct((count, width), BF16),
            jax.ShapeDtypeStruct((count, width), F32),
            jax.ShapeDtypeStruct((count, width), BF16),
            jax.ShapeDtypeStruct((1, depth), F32),
        ]
        + [jax.ShapeDtypeStruct((1, width), F32)] * 4
        + terms,
        scratch_shapes=[
            pltpu.VMEM((depth, width), BF16),
            pltpu.VMEM((width, depth), BF16),
            pltpu.VMEM((width, width), BF16),
            pltpu.VMEM((count, depth), BF16),
            pltpu.VMEM((count, width), BF16),
            pltpu.VMEM((count, width), BF16),
            pltpu.VMEM((count, width), BF16),
            pltpu.VMEM((2, width, width), BF16),
            pltpu.SemaphoreType.DMA((3,)),
            pltpu.SemaphoreType.DMA((2,)),
            pltpu.SemaphoreType.DMA((2,)),
        ],
        compiler_params=params(40),
        cost_estimate=cost(2 * count * width * (2 * width + 4 * depth), 40e6),
        name="narrow",
    )


def attend_back_kernel(block, number, terms, place, q_docs, k_docs, q_all, k_all, v_all, o_all, g_all, lse, hidden, *rest):
    dq, dk, dv = rest[:3]
    outs, rest = rest[3 : 3 + terms], rest[3 + terms :]
    bias, k_sum, v_sum, kept, h_kept, stage, sem, sems = rest
    count = LEN // block
    step = pl.program_id(0)

    @pl.when(step == 0)
    def _():
        pltpu.make_async_copy(hidden, h_kept, sem).start()
        for i in range(count):
            sl, reach = slice(i * block, (i + 1) * block), (i + 1) * block
            bias[:reach, sl] = allowed(q_docs[:, sl], k_docs[:reach, :], i * block, (reach, block), 1)

    @pl.when(step < number)
    def _():
        low = lax.broadcasted_iota(jnp.int32, (block, PAIR), 1) < HD
        low_all = lax.broadcasted_iota(jnp.int32, (LEN, PAIR), 1) < HD
        keys = k_all[...]
        key_one = [jnp.where(low_all, keys, jnp.zeros_like(keys)), jnp.where(low_all, jnp.zeros_like(keys), keys)]
        at = pl.ds(pl.multiple_of(lax.rem(step, number) * PAIR, PAIR), PAIR)
        for i in reversed(range(count)):
            sl, reach = slice(i * block, (i + 1) * block), (i + 1) * block
            q, grad = q_all[sl, :], g_all[sl, :]
            turned = (grad.astype(F32) * o_all[sl, :].astype(F32)).T
            parts = []
            for head in range(2):
                lane = low if head == 0 else ~low
                q_one = jnp.where(lane, q, jnp.zeros_like(q))
                g_one = jnp.where(lane, grad, jnp.zeros_like(grad))
                inner = jnp.sum(turned[head * HD : (head + 1) * HD, :], 0, keepdims=True)
                score = dot(k_all[:reach, :], q_one, NT) + bias[:reach, sl]
                prob = jnp.exp(score - lse[0, head : head + 1, sl])
                v_part = dot(prob.astype(BF16), g_one, NN)
                slope = dot(v_all[:reach, :], g_one, NT)
                dscore = (prob * (slope - inner)).astype(BF16)
                k_part = dot(dscore, q_one, NN)
                if i == count - 1 and head == 0:
                    k_sum[...] = k_part
                    v_sum[...] = v_part
                else:
                    k_sum[:reach, :] += k_part
                    v_sum[:reach, :] += v_part
                parts.append(dot(dscore, key_one[head][:reach], TN))
            part = ((parts[0] + parts[1]) * (1.0 / math.sqrt(HD))).astype(BF16)
            dq[sl, :] = part
            kept[0, sl, at] = part
        for index, (ref, total) in enumerate(((dk, k_sum), (dv, v_sum))):
            part = total[...].astype(BF16)
            ref[...] = part
            kept[1 + index, :, at] = part

    wide = stage.shape[3]

    @pl.when(step >= number)
    def _():
        tile = step - number
        slot = lax.rem(tile, 2)

        @pl.when(tile == 0)
        def _():
            finish(h_kept, sem)

        @pl.when(tile >= 2)
        def _():
            finish(stage.at[slot], sems.at[slot])

        for index in range(3):
            part = kept[index, :, pl.ds(pl.multiple_of(tile * wide, wide), wide)]
            stage[slot, index] = dot(h_kept[...], part, TN).astype(BF16)
        for index in range(3):
            for half in range(2):
                send(
                    place,
                    stage.at[slot, index],
                    half * (wide // 2),
                    wide // 2,
                    outs,
                    index * (number * PAIR // 2) + tile * (wide // 2),
                    half,
                    0,
                    sems.at[slot],
                )

        @pl.when(tile == number * PAIR // wide - 1)
        def _():
            finish(stage.at[slot], sems.at[slot])
            if number * PAIR // wide > 1:
                finish(stage.at[1 - slot], sems.at[1 - slot])


def attend_back(place, mixed, attended, grad_o, lse, docs, hidden, by_stage, after=()):
    width = attended.shape[1]
    number = width // PAIR
    block = 256
    wide = 2 * PAIR
    steps = width // wide
    pair = lambda i: jnp.minimum(i, number - 1)
    column = lambda base: pl.BlockSpec((LEN, PAIR), lambda i: (0, base + pair(i)))
    terms = term_shapes(width, 3 * number * PAIR, by_stage)
    return kernel_call(
        functools.partial(attend_back_kernel, block, number, len(terms)),
        [place, docs.reshape(1, LEN), docs.reshape(LEN, 1), mixed, mixed, mixed, attended, grad_o, lse, hidden],
        after,
        grid=(number + steps,),
        in_specs=[
            SMEM,
            whole((1, LEN)),
            whole((LEN, 1)),
            column(0),
            column(number),
            column(2 * number),
            column(0),
            column(0),
            pl.BlockSpec((1, 2, LEN), lambda i: (pair(i), 0, 0)),
            ANY,
        ],
        out_specs=[column(0)] * 3 + [ANY] * len(terms),
        out_shape=[jax.ShapeDtypeStruct((LEN, PAIR * number), BF16)] * 3 + terms,
        scratch_shapes=[
            pltpu.VMEM((LEN, LEN), F32),
            pltpu.VMEM((LEN, PAIR), F32),
            pltpu.VMEM((LEN, PAIR), F32),
            pltpu.VMEM((3, LEN, PAIR * number), BF16),
            pltpu.VMEM((LEN, width), BF16),
            pltpu.VMEM((2, 3, width, wide), BF16),
            pltpu.SemaphoreType.DMA,
            pltpu.SemaphoreType.DMA((2,)),
        ],
        compiler_params=params(56),
        cost_estimate=cost(42e9, 20e6),
        name="attend_back",
    )


def first_back_kernel(place, x, grad_r, gain, *rest):
    parts, pieces, rest = rest[:3], rest[3:-4], rest[-4:]
    grad_x, sums, weight, sem = rest
    width = x.shape[1]

    @pl.when(pl.program_id(0) == 0)
    def _():
        fetch(place, pieces, 0, 0, 3 * width // 2, weight, sem)()
        sums[...] = jnp.zeros_like(sums)

    grad_h = dot(parts[0][...], weight[:, :width], NT)
    for index in (1, 2):
        grad_h += dot(parts[index][...], weight[:, index * width : (index + 1) * width], NT)
    for at, part in ((2, parts[0]), (3, parts[2])):
        sums[at : at + 1, :] += jnp.sum(part[...].astype(F32), 0, keepdims=True)
    pulled, gains, shifts = norm_back(x[...].astype(F32), gain[...], grad_h)
    grad_x[...] = grad_r[...] + pulled
    sums[0:1, :] += gains
    sums[1:2, :] += shifts


def first_back(place, x, grad_r, gain, parts, pieces, after=()):
    count, width = x.shape
    block = 256
    return kernel_call(
        first_back_kernel,
        [place, x, grad_r, gain, *parts, *pieces],
        after,
        grid=(count // block,),
        in_specs=[SMEM, rows(block, width), rows(block, width), whole((1, width))]
        + [rows(block, part.shape[1]) for part in parts]
        + [HBM] * len(pieces),
        out_specs=[rows(block, width), whole((4, width))],
        out_shape=[jax.ShapeDtypeStruct((count, width), F32), jax.ShapeDtypeStruct((4, width), F32)],
        scratch_shapes=[pltpu.VMEM((width, 3 * width), BF16), pltpu.SemaphoreType.DMA],
        compiler_params=params(56),
        cost_estimate=cost(6 * count * width * width, 16e6),
        name="first_back",
    )


def pack_kernel(*refs):
    vectors, out = refs[:-1], refs[-1]
    devices, lanes = out.shape
    width = vectors[0].shape[1]
    unit = lanes // 12
    rows_of = [
        vector[row : row + 1, first : first + width]
        for vector in vectors
        for row in range(vector.shape[0])
        for first in range(0, vector.shape[1], width)
    ]
    total = jnp.zeros((devices, 12 * unit + (-12 * unit) % 128), F32)
    full = total.shape[1]
    at, base = 0, 0
    for span in (1, 1, 2, 1, 1, 1, 4, 1):
        size = span * unit + (-span * unit) % 128
        shape = (size, width)
        spreads = []
        for index in range(span):
            mine = owner((devices, width), span * unit, index * width)
            spreads.append(jnp.where(mine, rows_of[at + index], 0.0))
        at += span
        found = jnp.zeros((devices, size), F32)
        for index, spread in enumerate(spreads):
            pick = one_hot(shape, 0, span * unit, index * width).astype(BF16)
            high = spread.astype(BF16)
            low = (spread - high.astype(F32)).astype(BF16)
            both = dot(jnp.concatenate([high, low], 0), pick, NT)
            found = found + both[:devices] + both[devices:]
        if size < full:
            found = jnp.concatenate([found, jnp.zeros((devices, full - size), F32)], 1)
        total = total + (found if base == 0 else pltpu.roll(found, base * unit, 1))
        base += span
    out[...] = total[:, :lanes]


def pack(vectors, devices):
    lanes = sum(v.size for v in vectors) // devices
    return pl.pallas_call(
        pack_kernel,
        out_shape=jax.ShapeDtypeStruct((devices, lanes), F32),
        compiler_params=params(16),
        name="pack",
    )(*vectors)


def staged(
    tokens,
    doc_ids,
    d_out,
    ln1_gain,
    ln1_shift,
    qkv_weight,
    qv_bias,
    out_weight,
    out_bias,
    ln2_gain,
    ln2_shift,
    fc_weight,
    fc_bias,
    proj_weight,
    proj_bias,
):
    width = tokens.shape[1]
    depth = fc_weight.shape[1]
    devices = lax.axis_size("dp") * lax.axis_size("fsdp")
    index = lax.axis_index("dp") * lax.axis_size("fsdp") + lax.axis_index("fsdp")
    core = index & 1
    place = jnp.stack([index >> 1, core]).astype(jnp.int32)
    by_stage = (lax.axis_size("dp"), lax.axis_size("fsdp")) == (8, 4)

    smalls = [ln1_gain, ln1_shift, qv_bias, out_bias, ln2_gain, ln2_shift, fc_bias, proj_bias]
    smalls = jnp.concatenate([v.astype(F32).reshape(1, -1) for v in smalls], 1).reshape(-1)
    if by_stage:
        extra = jnp.pad(smalls, (0, -smalls.size % 128)).reshape(-1, 128).astype(BF16)
        extra = jnp.pad(extra, ((0, qkv_weight.shape[0] - extra.shape[0]), (0, 0)))
        first_block = pair_block(qkv_weight, core, extra)
        out_weight, fc_weight, proj_weight = tie([out_weight, fc_weight, proj_weight], first_block)
        wide_block = jnp.concatenate([pair_block(out_weight, core), pair_block(fc_weight, core)], 1)
        proj_block = pair_block(proj_weight, core)
        first_column = jnp.stack([first_block] + by_z([first_block] * 3))
        (wide_block,) = tie([wide_block], first_column)
        (proj_block,) = tie([proj_block], first_column)
        first_got, wide_got = meet(by_xy([first_column] * 3), by_z([wide_block] * 3))
        proj_near = swap(proj_block, Z0)
        first_pieces = gather_core([first_column, *first_got])
        wide_column, proj_near = tie([jnp.stack([wide_block] + wide_got), proj_near], proj_near)
        wide_got = by_xy([wide_column] * 3)
        (proj_block,) = tie([proj_block], wide_column)
        proj_got = [swap(proj_block, bits) for bits in (Z1, Z0 | Z1)]
    else:
        first_pieces, proj_pieces = [gather_all(qkv_weight)], [gather_all(proj_weight)]
        wide_pieces = [gather_all(w) for w in (out_weight, fc_weight)]
        wide_column = None
        table = gather_all(smalls.reshape(1, -1).astype(BF16))
        first_pieces = first_pieces + [jnp.pad(table, ((0, 0), (0, -table.shape[1] % 128)))]
    hold = lambda *some: list(some) if by_stage else []
    row = lambda at, count=1: vectors[at : at + count].reshape(1, -1)

    found = project_attend(place, tokens, doc_ids, first_pieces, after=hold(wide_column) if by_stage else [])
    if by_stage:
        found, wide_got, proj_got = meet(found, wide_got, proj_got)
        proj_column = jnp.stack([proj_block, proj_near] + proj_got)
        proj_got = by_xy([proj_column] * 3)
        wide_pieces = gather_core([wide_column, *wide_got])
    mixed, h_one, attended, lse, vectors = found

    found = widen(
        place,
        tokens,
        attended,
        row(4),
        row(5),
        row(6),
        row(7, 4),
        d_out,
        wide_pieces,
        after=hold(proj_column) if by_stage else [],
    )
    if by_stage:
        found, proj_got = meet(found, proj_got)
        proj_pieces = gather_core([proj_column, *proj_got])
        proj_sums = scatter_core(found[4:])
        proj_got = by_xy(proj_sums[1:])
    resid, h_two, slope, active, *proj_terms = found

    found = narrow(
        place,
        resid,
        active,
        slope,
        d_out,
        row(11),
        row(5),
        h_two,
        attended,
        wide_pieces,
        proj_pieces,
        after=hold(*proj_sums) if by_stage else [],
    )
    if by_stage:
        found, proj_got = meet(found, proj_got)
        proj_sums = sum_xy(proj_sums, proj_got)
        proj_got = by_z(proj_sums[1:])
        wide_sums = scatter_core(found[8:])
        wide_got = by_xy(wide_sums[1:])
    result, grad_r, grad_o, fc_sum, proj_sum, gain_two, shift_two, out_sum, *wide_terms = found

    found = attend_back(
        place,
        mixed,
        attended,
        grad_o,
        lse,
        doc_ids,
        h_one,
        by_stage,
        after=hold(*proj_sums, *wide_sums) if by_stage else [],
    )
    if by_stage:
        found, wide_got, proj_got = meet(found, wide_got, proj_got)
        wide_sums = sum_xy(wide_sums, wide_got)
        wide_got = by_z(wide_sums[1:])
        qkv_sums = scatter_core(found[3:])
        qkv_got = by_xy(qkv_sums[1:])
    *grads, qkv_terms = found[:4]

    found = first_back(
        place,
        tokens,
        grad_r,
        row(0),
        grads,
        first_pieces[:8] if by_stage else first_pieces[:1],
        after=hold(*qkv_sums, *wide_sums) if by_stage else [],
    )
    if by_stage:
        found, wide_got, qkv_got = meet(found, wide_got, qkv_got)
    grad_x, first_sums = found
    sums = [first_sums, out_sum, gain_two, shift_two, fc_sum, proj_sum]
    table = pack(sums, devices)
    if by_stage:
        qkv_sums = sum_xy(qkv_sums, qkv_got)
        table = scatter_small(tie([table], *qkv_sums)[0], index, (Z1, Z0, Y, X))
        (table,), qkv_got = meet([table], by_z(qkv_sums[1:]))
        proj_grad, wide_grad = add(proj_sums[0], *proj_got), add(wide_sums[0], *wide_got)
    else:
        own = scatter_all(table).reshape(-1)
        proj_grad, wide_grad, qkv_grad = (
            scatter_all(terms.astype(F32)) for terms in (proj_terms[0], wide_terms[0], qkv_terms)
        )

    def sides(grad):
        if by_stage:
            return own_rows(grad, core)
        return jnp.split(grad, 2, 1)

    proj_grad = jnp.concatenate(sides(proj_grad), 1)
    both = sides(wide_grad)
    half = depth // 2
    fc_grad = jnp.concatenate([side[:, :half] for side in both], 1)
    out_grad = jnp.concatenate([side[:, half:] for side in both], 1)
    if by_stage:
        own = scatter_small(table, index, (CORE,)).reshape(-1)
        qkv_grad = add(qkv_sums[0], *qkv_got)
    both = sides(qkv_grad)
    qkv_grad = jnp.concatenate(
        [side[:, lane : lane + PAIR] for lane in range(0, both[0].shape[1], PAIR) for side in both], 1
    )
    n = width // devices
    spots = (0, n, 2 * n, 4 * n, 5 * n, 6 * n, 7 * n, 11 * n, 12 * n)
    s = [own[a:b] for a, b in zip(spots[:-1], spots[1:])]
    return (
        result,
        grad_x,
        s[0],
        s[1],
        qkv_grad,
        s[2],
        out_grad,
        s[3],
        s[4],
        s[5],
        fc_grad,
        s[6],
        proj_grad,
        s[7],
    )


def solution(mesh):
    every, block = P(AXES), P(AXES, None)
    ins = (block, every, block, every, every, block, every, block, every, every, every, block, every, block, every)
    outs = (block, block, every, every, block, every, block, every, every, every, block, every, block, every)
    return jax.shard_map(staged, mesh=mesh, in_specs=ins, out_specs=outs, check_vma=False)
```
